32 devices in a mesh: groups: 2 (over x), expert: 16 (over z, y, core).
Axes of the slice: x: 2, y: 2, z: 4, core: 2. Of those that a mesh axis runs over, the one named last changes fastest.
Arguments:
- tokens: bfloat16 [4096, 4096], P(('groups', 'expert')), parts along dimension 0, may hold values from -6 to 6
- w_in: bfloat16 [16, 4096, 2048], P('expert'), may hold values from -0.09375 to 0.09375
- w_out: bfloat16 [16, 2048, 4096], P('expert'), may hold values from -0.09375 to 0.09375
- w_bcd: bfloat16 [4096, 160], replicated, may hold values from -0.09375 to 0.09375
- dt_bias: float32 [32], replicated, may hold values from -1 to 1
- decay_rate: float32 [32], replicated, may hold values from 0.00048828125 to 0.05
- skip_gain: float32 [32], replicated, may hold values from 0.5 to 1.5
- norm_gain: float32 [4096], replicated, may hold values from 0.5 to 1.5
- expert_ids: int32 [4096, 1], P(('groups', 'expert')), parts along dimension 0, may hold values from 0 to 7; in each aligned block of 128 rows (0 to 127, 128 to 255, ...) at most 24 rows name the same one
- decode_heads: int32 [16], P('expert'), may hold values from 0 to 15, as said below
Outputs:
- mixed: bfloat16 [4096, 4096], P(('groups', 'expert')), parts along dimension 0
- decode_state: float32 [32, 8192], P(('groups', 'expert')), parts along dimension 0
The draws below stay inside these ranges and needn't reach their ends.
There are 2 independent parts, one for each index of `groups`. The reference program is written for one: setup_inputs(seed, part) draws one part's arguments, and reference() takes and returns one part's arrays. A program takes and returns all parts, laid end to end along the dimension named above; an argument that names none is the same for every part. Nothing has to cross between parts.
Inputs may be any that keep to these rules, and one draw needn't show every extreme that they name: `expert_ids`: in each aligned block of 128 rows (the rows of one device) no expert is named more than 24 times. `decode_heads`: the entries are the device numbers modulo 32, shuffled.
All inputs are finite; a program needn't handle non-finite values.
Results may differ from the reference program's by a relative error of at most 0.0065.
Values may be sent and summed in bfloat16 or wider, within the bound.
No kernel may reach another device: no remote copies, remote signals or barrier semaphores. Data moves between devices by JAX's collectives and lax.ppermute only.
A program may use at most 192 MiB of HBM per device.

```python
import math
import jax
import jax.numpy as jnp
import numpy as np
from jax import lax

D = 4096
INNER = 4096
HEADDIM = 128
NS = 64
EXPERTS = 8
SPAN = 128
TOK_DEV = 128
HEADS = 32
CAP = 24
IN_DEV = 2048
SEQ = 2048
N_EXPERT = 16


def draw_decode_heads(key, part):
    key = jax.random.fold_in(key, 7)
    return jax.random.permutation(key, jnp.arange(N_EXPERT, dtype=jnp.int32) % HEADS).astype(jnp.int32)


def block_levels(key, extent, cuts, least, high):
    factor_of = 1.0
    for dim, blocks in cuts:
        draws = jax.random.uniform(jax.random.fold_in(jax.random.fold_in(key, 6), dim), (blocks,), jnp.float32, least / len(cuts), high / len(cuts))
        factor_of = factor_of * jnp.repeat(jnp.exp(draws), extent[dim] // blocks).reshape((-1,) + (1,) * (len(extent) - 1 - dim))
    return factor_of


def routed_block(key, own, number, rows, count, top, most, lean):
    order = jax.random.permutation(key, count)
    heavy_load, usual = load_shares(count, rows * top, most, lean, True), load_shares(count, rows * top, most, lean, False)
    places = jnp.arange(count)

    def named(tallies, offset_by):
        used = int((tallies > 0).sum())
        fixed = max(1, used // 4)
        moved = fixed + (places - fixed + offset_by * (used - fixed)) % max(1, count - fixed)
        return jnp.zeros((count,), jnp.int32).at[order[jnp.where(places < fixed, places, moved)]].set(jnp.asarray(tallies, jnp.int32))

    tallies = jnp.where(number % 4 == 0, named(heavy_load, number // 4), named(usual, number - number // 4 - 1))
    mixed = jax.random.permutation(jax.random.fold_in(own, 3), count)
    source_of, taker = mixed[0:count // 2 * 2:2], mixed[1:count // 2 * 2:2]
    slack = jnp.minimum(tallies[source_of] - 1, most - tallies[taker]) // 2
    slack = jnp.where((source_of == order[0]) | (taker == order[0]) | (tallies[taker] == 0), 0, jnp.maximum(slack, 0))
    moved = jax.random.randint(jax.random.fold_in(own, 4), (count // 2,), 0, 1 << 20) % (slack + 1)
    tallies = tallies.at[source_of].add(-moved).at[taker].add(moved)
    labels = jnp.searchsorted(jnp.cumsum(tallies), jnp.arange(rows * top), side="right").astype(jnp.int32)
    grid = labels.reshape(top, rows).T
    grid = grid[jax.random.permutation(jax.random.fold_in(own, 1), rows)]
    offset_by = jax.random.randint(jax.random.fold_in(own, 2), (rows, 1), 0, top)
    return jnp.take_along_axis(grid, (jnp.arange(top)[None, :] + offset_by) % top, axis=1)


def load_shares(count, total, reach, skew, full):
    weights = [(1 << 20) // math.isqrt(grade ** skew) + 1 for grade in range(1, count + 1)]
    largest = reach if full else min(reach, max(-(-total // count), total * weights[0] // sum(weights)))
    least = 1 if total - largest >= count - 1 else 0
    counts, surplus = [largest] + [least] * (count - 1), total - largest - least * (count - 1)
    while surplus > 0:
        free = [i for i in range(1, count) if counts[i] < largest] or [i for i in range(1, count) if counts[i] < reach]
        whole, remaining = sum([weights[i] for i in free]), surplus
        for i in free:
            extra = min(reach - counts[i], max(1, remaining * weights[i] // whole), surplus)
            counts[i] = counts[i] + extra
            surplus = surplus - extra
    return np.array(counts)


def scatter_about(stream_key, shape, scale, limit, cuts=(), kind=jnp.bfloat16):
    drawn = jax.random.normal(stream_key, shape, jnp.float32) * scale
    if len(cuts) > 0:
        drawn = block_levels(stream_key, shape, cuts, -0.22, 0.18) * drawn
    return jnp.clip(drawn, min=-limit, max=limit).astype(kind)


def setup_inputs(seed: int = 0, part: int = 0) -> dict:
    streams_of = jax.random.split(jax.random.key(seed), 11)
    part_keys = jax.random.split(jax.random.fold_in(streams_of[10], part), 11)
    tokens = scatter_about(part_keys[0], (SEQ, D), 1.0, 6.0, ((0, 16),))
    w_in = scatter_about(streams_of[1], (N_EXPERT, D, IN_DEV), D ** -0.5, 0.09375, ((0, 16),))
    w_out = scatter_about(streams_of[2], (N_EXPERT, IN_DEV, D), INNER ** -0.5, 0.09375, ((0, 16),))
    w_bcd = scatter_about(streams_of[3], (D, 2 * NS + HEADS), D ** -0.5, 0.09375)
    dt_bias = jnp.clip(jax.random.uniform(streams_of[4], (HEADS,), jnp.float32, -1.0, 1.0), -1.0, 1.0)
    decay_rate = jnp.clip(jnp.exp(jax.random.uniform(streams_of[5], (HEADS,), jnp.float32, math.log(0.00048828125), math.log(0.05))), 0.00048828125, 0.05)
    skip_gain = jnp.clip(jax.random.uniform(streams_of[6], (HEADS,), jnp.float32, 0.5, 1.5), 0.5, 1.5)
    norm_gain = jnp.clip(jax.random.uniform(streams_of[7], (INNER,), jnp.float32, 0.5, 1.5), 0.5, 1.5)
    expert_ids_keys = jax.random.split(jax.random.fold_in(part_keys[8], 1), SEQ // TOK_DEV)
    expert_ids_turns = jax.random.permutation(jax.random.fold_in(part_keys[8], 3), SEQ // TOK_DEV)
    expert_ids = jax.vmap(lambda own, number: routed_block(jax.random.fold_in(part_keys[8], 2), own, number, TOK_DEV, EXPERTS, 1, CAP, 2))(expert_ids_keys, expert_ids_turns).reshape((SEQ, 1))
    decode_heads = draw_decode_heads(jax.random.fold_in(streams_of[10], 71), part)
    return {"tokens": tokens, "w_in": w_in, "w_out": w_out, "w_bcd": w_bcd, "dt_bias": dt_bias, "decay_rate": decay_rate, "skip_gain": skip_gain, "norm_gain": norm_gain, "expert_ids": expert_ids, "decode_heads": decode_heads}


def slot_of(block_ids):
    onehot = (block_ids[:, None] == jnp.arange(EXPERTS, dtype=jnp.int32)[None, :]).astype(jnp.int32)
    return lax.optimization_barrier(jnp.sum((jnp.cumsum(onehot, axis=0) - onehot) * onehot, axis=1)).astype(jnp.int32)

def ssd_pass(x_heads, steps_dt, b_proj, c_proj, decay_rate):
    span_count = x_heads.shape[0] // SPAN
    head_count = x_heads.shape[1]
    best = lax.Precision.HIGHEST

    def span_step(carry_pair, pieces):
        carry_state, offset = carry_pair
        span_x, span_dt, span_b, span_c = pieces
        log_decay = -span_dt * decay_rate[None, :]
        running = jnp.cumsum(log_decay, axis=0)
        places = jnp.arange(SPAN)
        causal = (places[:, None] >= places[None, :])[:, :, None]
        log_gap = jnp.where(causal, running[:, None, :] - running[None, :, :], 0.0)
        scores = jnp.dot(span_c, span_b.T, precision=best)
        weights = jnp.where(causal, jnp.exp(log_gap), 0.0) * scores[:, :, None] * span_dt[None, :, :]
        within = jnp.einsum('tuh,uhp->thp', weights, span_x, precision=best)
        carried = jnp.exp(running)[:, :, None] * jnp.einsum('tn,hpn->thp', span_c, carry_state, precision=best)
        tail_weight = jnp.exp(running[-1][None, :] - running) * span_dt
        new_state = jnp.exp(running[-1])[:, None, None] * carry_state + jnp.einsum('uh,uhp,un->hpn', tail_weight, span_x, span_b, precision=best)
        return ((new_state, offset + running[-1]), (within + carried, offset[None, :] + running))
    init_state = jnp.zeros((head_count, HEADDIM, NS), jnp.float32)
    init_offset = jnp.zeros((head_count,), jnp.float32)
    pieces = (x_heads.reshape(span_count, SPAN, head_count, HEADDIM), steps_dt.reshape(span_count, SPAN, head_count), b_proj.reshape(span_count, SPAN, NS), c_proj.reshape(span_count, SPAN, NS))
    (final_state, log_total), (y_blocks, log_rows) = lax.scan(span_step, (init_state, init_offset), pieces)
    return (y_blocks.reshape(-1, head_count, HEADDIM), final_state, log_rows.reshape(-1, head_count), log_total)

def reference(tokens, w_in, w_out, w_bcd, dt_bias, decay_rate, skip_gain, norm_gain, expert_ids, decode_heads):
    slices = N_EXPERT // EXPERTS
    in_dev = INNER // slices
    blocks = SEQ // TOK_DEV
    head_count = INNER // HEADDIM
    full_in = w_in.astype(jnp.float32).reshape(EXPERTS, slices, D, in_dev).transpose(0, 2, 1, 3).reshape(EXPERTS, D, INNER)
    full_out = w_out.astype(jnp.float32).reshape(EXPERTS, slices, in_dev, D)
    routed = expert_ids[:, 0].reshape(blocks, TOK_DEV)

    def inner_block(pieces):
        row_block, block_ids = pieces
        slot_ids = slot_of(block_ids)
        sectioned = jnp.zeros((EXPERTS, CAP, D), jnp.float32).at[block_ids, slot_ids].set(row_block.astype(jnp.float32))
        inner_rows = jnp.einsum('ecd,edi->eci', sectioned, full_in)
        return inner_rows[block_ids, slot_ids].astype(jnp.bfloat16)
    x_inner = lax.map(inner_block, (tokens.reshape(blocks, TOK_DEV, D), routed)).reshape(SEQ, INNER)
    x_inner = lax.optimization_barrier(x_inner)
    mixing = jnp.dot(tokens, w_bcd, preferred_element_type=jnp.float32)
    b_proj = mixing[:, :NS]
    c_proj = mixing[:, NS:2 * NS]
    steps_dt = jax.nn.softplus(mixing[:, 2 * NS:] + dt_bias[None, :])
    x_heads = x_inner.astype(jnp.float32).reshape(SEQ, head_count, HEADDIM)
    y_rows, final_state, log_rows, log_total = ssd_pass(x_heads, steps_dt, b_proj, c_proj, decay_rate)
    y_flat = (y_rows + skip_gain[None, :, None] * x_heads).reshape(SEQ, INNER)
    normed = (y_flat * lax.rsqrt(lax.optimization_barrier(jnp.mean(y_flat * y_flat, axis=1, keepdims=True)) + 1e-05) * norm_gain[None, :]).astype(jnp.bfloat16)

    def outer_block(pieces):
        row_block, block_ids = pieces
        slot_ids = slot_of(block_ids)
        sectioned = jnp.zeros((EXPERTS, CAP, slices, in_dev), jnp.float32).at[block_ids, slot_ids].set(row_block.astype(jnp.float32).reshape(TOK_DEV, slices, in_dev))
        partial_value = jnp.einsum('ecgi,egid->ecgd', sectioned, full_out).astype(jnp.bfloat16)
        partial_value = lax.optimization_barrier(partial_value)
        summed = lax.optimization_barrier(jnp.sum(partial_value.astype(jnp.float32), axis=2))
        return summed[block_ids, slot_ids].astype(jnp.bfloat16)
    mixed_rows = lax.map(outer_block, (normed.reshape(blocks, TOK_DEV, INNER), routed)).reshape(SEQ, D)
    decode_state = final_state[decode_heads].reshape(N_EXPERT, HEADDIM * NS)
    return (mixed_rows, decode_state)
```

```python
import functools

import jax
import jax.numpy as jnp
from jax import lax
from jax.experimental import pallas as pl
from jax.experimental.pallas import tpu as pltpu
from jax.sharding import PartitionSpec as P

INNER = 4096
HEADDIM = 128
HEADS = 32
NS = 64
EXPERTS = 8
CAP = 24
PAIR = 256
PACK = 256
VMEM_BYTES = 48 * 1024 * 1024

f32 = jnp.float32
bf16 = jnp.bfloat16


def params(**extra):
    return pltpu.CompilerParams(vmem_limit_bytes=VMEM_BYTES, **extra)


def route_column(ids):
    rows = ids.shape[0]
    onehot = (ids == lax.broadcasted_iota(jnp.int32, (rows, 128), 1)).astype(f32)
    later = lax.broadcasted_iota(jnp.int32, (rows, rows), 0)
    earlier = lax.broadcasted_iota(jnp.int32, (rows, rows), 1)
    lower = (earlier < later).astype(f32).astype(bf16)
    before = jnp.dot(lower, onehot.astype(bf16), preferred_element_type=f32)
    return jnp.sum(before * onehot, axis=1, keepdims=True).astype(jnp.int32)


def dispatch_kernel(slices, ids_ref, tok_ref, out_ref, slot_ref):
    ids = ids_ref[...]
    rows, width = tok_ref.shape
    depth = width // slices
    step = min(512, depth)
    slot = route_column(ids)
    slot_ref[...] = slot
    pick = (
        (ids * CAP + slot == lax.broadcasted_iota(jnp.int32, (rows, EXPERTS * CAP), 1))
        .astype(f32)
        .astype(bf16)
    )
    for c in range(0, depth, step):
        got = [
            lax.dot_general(
                pick,
                tok_ref[:, s * depth + c : s * depth + c + step],
                (((0,), (0,)), ((), ())),
                preferred_element_type=f32,
            )
            for s in range(slices)
        ]
        for e in range(EXPERTS):
            piece = jnp.concatenate([g[e * CAP : (e + 1) * CAP] for g in got], axis=0)
            out_ref[e * slices * CAP : (e + 1) * slices * CAP, c : c + step] = piece.astype(bf16)


def dispatch(ids, tokens, slices):
    rows, width = tokens.shape
    return pl.pallas_call(
        functools.partial(dispatch_kernel, slices),
        out_shape=(
            jax.ShapeDtypeStruct((EXPERTS * slices * CAP, width // slices), bf16),
            jax.ShapeDtypeStruct((rows, 1), jnp.int32),
        ),
        compiler_params=params(),
        name="dispatch",
    )(ids, tokens)


def in_kernel(slices, units, place_ref, *refs):
    rows_refs, w_refs, out_ref = refs[:slices], refs[slices : 2 * slices], refs[-1]
    total = None
    for r in range(slices):
        part = jnp.dot(rows_refs[r][...], w_refs[r][...], preferred_element_type=f32)
        total = part if total is None else total + part
    for j in range(out_ref.shape[0]):
        out_ref[j] = total[:, j * units : (j + 1) * units].astype(bf16)


def in_projection(place, pieces, w_in, units):
    slices = len(pieces)
    rows, depth = pieces[0].shape
    in_dev = w_in.shape[1]
    tile = min(256, in_dev)

    def w_spec(r):
        return pl.BlockSpec(
            (depth, tile), lambda n, place_ref: ((place_ref[0] - r + slices) % slices, n)
        )

    return pl.pallas_call(
        functools.partial(in_kernel, slices, units),
        out_shape=jax.ShapeDtypeStruct((in_dev // units, rows, units), bf16),
        grid_spec=pltpu.PrefetchScalarGridSpec(
            num_scalar_prefetch=1,
            grid=(in_dev // tile,),
            in_specs=[pl.BlockSpec((rows, depth), lambda n, place_ref: (0, 0))] * slices
            + [w_spec(r) for r in range(slices)],
            out_specs=pl.BlockSpec(
                (tile // units, rows, units), lambda n, place_ref: (n, 0, 0)
            ),
        ),
        compiler_params=params(),
        cost_estimate=pl.CostEstimate(
            flops=2 * rows * slices * depth * in_dev,
            bytes_accessed=2 * slices * depth * (in_dev + rows) + 2 * rows * in_dev,
            transcendentals=0,
        ),
        name="in_projection",
    )(place, *pieces, *([w_in] * slices))


def prep_kernel(heads, head_ref, rate_ref, skip_ref, pack_ref, w_ref, c_ref, b_ref, a_ref):
    first = head_ref[0]
    pack = pack_ref[...]
    row = lax.broadcasted_iota(jnp.int32, (128, PACK), 0)
    lane = lax.broadcasted_iota(jnp.int32, (128, PACK), 1)
    at = lane - 2 * NS - first
    choose = ((row < heads) & ((at == row) | (at == row + HEADS))).astype(f32)
    route = jnp.where(lane == 2 * NS + 2 * HEADS, 2.0 * CAP, 0.0) + jnp.where(
        lane == 2 * NS + 2 * HEADS + 1, 1.0, 0.0
    )
    choose = choose + jnp.where(row == heads, route, 0.0)
    across = lax.dot_general(
        choose.astype(bf16), pack, (((1,), (1,)), ((), ())), preferred_element_type=f32
    )
    rate = jnp.zeros((128, PAIR), f32)
    row = lax.broadcasted_iota(jnp.int32, (128, PAIR), 0)
    for h in range(heads):
        rate = jnp.where(row == h, rate_ref[first + h], rate)
    upto = lax.broadcasted_iota(jnp.int32, (PAIR, PAIR), 0)
    now = lax.broadcasted_iota(jnp.int32, (PAIR, PAIR), 1)
    running = jnp.dot(
        -across * rate,
        (upto <= now).astype(f32),
        precision=lax.Precision.HIGHEST,
        preferred_element_type=f32,
    )
    second = lax.broadcasted_iota(jnp.int32, (1, PAIR), 1) >= PAIR // 2
    column = across[heads : heads + 1] + jnp.where(second, float(CAP), 0.0)
    slots = 2 * CAP * EXPERTS
    place_t = (
        (lax.broadcasted_iota(jnp.int32, (slots, PAIR), 0).astype(f32) == column)
        .astype(f32)
        .astype(bf16)
    )
    down = running.T
    b_rows = pack[:, :NS]
    c_rows = pack[:, NS : 2 * NS]
    scores = lax.dot_general(
        c_rows, b_rows, (((1,), (1,)), ((), ())), preferred_element_type=f32
    )
    causal = upto >= now
    diagonal = upto == now
    b_cols = b_rows.astype(f32).T
    c_wide = c_rows.astype(f32)
    for h in range(heads):
        run_row = running[h : h + 1]
        run_col = down[:, h : h + 1]
        dt_row = across[h : h + 1]
        last = run_row[:, PAIR - 1 : PAIR]
        gap = jnp.where(causal, run_col - run_row, 0.0)
        weights = jnp.where(causal, jnp.exp(gap) * scores * dt_row, 0.0)
        weights = weights + jnp.where(diagonal, skip_ref[first + h], 0.0)
        half = jnp.dot(place_t, weights.astype(bf16), preferred_element_type=f32).astype(bf16)
        w_ref[h, 0] = lax.dot_general(
            half, place_t, (((1,), (1,)), ((), ())), preferred_element_type=f32
        ).astype(bf16)
        c_now = (c_wide * jnp.exp(run_col)).astype(bf16)
        c_ref[h, 0] = jnp.dot(place_t, c_now, preferred_element_type=f32).astype(bf16)
        b_now = (b_cols * (jnp.exp(last - run_row) * dt_row)).astype(bf16)
        b_ref[h, 0] = lax.dot_general(
            b_now, place_t, (((1,), (1,)), ((), ())), preferred_element_type=f32
        ).astype(bf16)
        a_ref[h, 0] = jnp.broadcast_to(jnp.exp(last), (8, 128))


def prepare(first, rate, skip, pack, heads):
    pairs = pack.shape[0] // PAIR
    slots = 2 * CAP * EXPERTS
    smem = pl.BlockSpec(memory_space=pltpu.SMEM)
    return pl.pallas_call(
        functools.partial(prep_kernel, heads),
        out_shape=(
            jax.ShapeDtypeStruct((heads, pairs, slots, slots), bf16),
            jax.ShapeDtypeStruct((heads, pairs, slots, NS), bf16),
            jax.ShapeDtypeStruct((heads, pairs, NS, slots), bf16),
            jax.ShapeDtypeStruct((heads, pairs, 8, 128), f32),
        ),
        grid=(pairs,),
        in_specs=[smem, smem, smem, pl.BlockSpec((PAIR, PACK), lambda p: (p, 0))],
        out_specs=(
            pl.BlockSpec((heads, 1, slots, slots), lambda p: (0, p, 0, 0)),
            pl.BlockSpec((heads, 1, slots, NS), lambda p: (0, p, 0, 0)),
            pl.BlockSpec((heads, 1, NS, slots), lambda p: (0, p, 0, 0)),
            pl.BlockSpec((heads, 1, 8, 128), lambda p: (0, p, 0, 0)),
        ),
        compiler_params=params(),
        cost_estimate=pl.CostEstimate(
            flops=4 * heads * pairs * slots * slots * PAIR,
            bytes_accessed=2 * heads * pairs * slots * slots,
            transcendentals=heads * pairs * PAIR * PAIR,
        ),
        name="scan_weights",
    )(first, rate, skip, pack)


def scan_kernel(heads, x_ref, w_ref, c_ref, b_ref, a_ref, gain_ref, out_ref, last_ref, state):
    pair = pl.program_id(0)

    @pl.when(pair == 0)
    def _():
        state[...] = jnp.zeros_like(state)

    experts, rows, units = x_ref.shape
    width = units // heads
    x = x_ref[...].reshape(experts * rows, units)
    y = []
    for h in range(heads):
        x_head = x[:, h * width : (h + 1) * width]
        before = state[h]
        y.append(
            jnp.dot(w_ref[h, 0], x_head, preferred_element_type=f32)
            + jnp.dot(c_ref[h, 0], before.astype(bf16), preferred_element_type=f32)
        )
        after = before * a_ref[h, 0, 0:1, 0:1] + jnp.dot(
            b_ref[h, 0], x_head, preferred_element_type=f32
        )
        state[h] = after
        last_ref[h] = after
    z = y[0] if heads == 1 else jnp.concatenate(y, axis=1)
    out_ref[...] = (z * gain_ref[...]).astype(bf16).reshape(experts, rows, units)


def scan(x, weights, gain, heads):
    experts, rows, units = x.shape
    pairs = rows // (2 * CAP)
    slots = 2 * CAP * EXPERTS
    width = units // heads
    return pl.pallas_call(
        functools.partial(scan_kernel, heads),
        out_shape=(
            jax.ShapeDtypeStruct(x.shape, bf16),
            jax.ShapeDtypeStruct((heads, NS, width), f32),
        ),
        grid=(pairs,),
        in_specs=[
            pl.BlockSpec((experts, 2 * CAP, units), lambda p: (0, p, 0)),
            pl.BlockSpec((heads, 1, slots, slots), lambda p: (0, p, 0, 0)),
            pl.BlockSpec((heads, 1, slots, NS), lambda p: (0, p, 0, 0)),
            pl.BlockSpec((heads, 1, NS, slots), lambda p: (0, p, 0, 0)),
            pl.BlockSpec((heads, 1, 8, 128), lambda p: (0, p, 0, 0)),
            pl.BlockSpec((1, units), lambda p: (0, 0)),
        ],
        out_specs=(
            pl.BlockSpec((experts, 2 * CAP, units), lambda p: (0, p, 0)),
            pl.BlockSpec((heads, NS, width), lambda p: (0, 0, 0)),
        ),
        scratch_shapes=[pltpu.VMEM((heads, NS, width), f32)],
        compiler_params=params(),
        cost_estimate=pl.CostEstimate(
            flops=2 * heads * pairs * slots * (slots + 2 * NS) * width,
            bytes_accessed=2 * heads * pairs * slots * slots,
            transcendentals=0,
        ),
        name="scan",
    )(x, *weights, gain)


def out_kernel(z_ref, inverse_ref, w_ref, out_ref, square_ref):
    chunks, rows, units = z_ref.shape

    def squares():
        total = jnp.zeros((rows, 1), f32)
        for j in range(chunks):
            z = z_ref[j].astype(f32) * inverse_ref[:, j * units : (j + 1) * units]
            total = total + jnp.sum(z * z, axis=1, keepdims=True)
        square_ref[...] = total

    pl.when(pl.program_id(0) == 0)(squares)
    total = None
    for j in range(chunks):
        part = jnp.dot(
            z_ref[j], w_ref[j * units : (j + 1) * units, :], preferred_element_type=f32
        )
        total = part if total is None else total + part
    out_ref[0] = total.astype(bf16)


def out_projection(place, z, inverse, w_out, slices):
    chunks, rows, units = z.shape
    in_dev, width = w_out.shape
    depth = width // slices
    tile = min(512, depth)
    tiles = depth // tile

    def kernel(place_ref, *refs):
        out_kernel(*refs)

    return pl.pallas_call(
        kernel,
        out_shape=(
            jax.ShapeDtypeStruct((slices, rows, depth), bf16),
            jax.ShapeDtypeStruct((rows, 1), f32),
        ),
        grid_spec=pltpu.PrefetchScalarGridSpec(
            num_scalar_prefetch=1,
            grid=(slices * tiles,),
            in_specs=[
                pl.BlockSpec((chunks, rows, units), lambda n, place_ref: (0, 0, 0)),
                pl.BlockSpec((1, in_dev), lambda n, place_ref: (0, 0)),
                pl.BlockSpec(
                    (in_dev, tile),
                    lambda n, place_ref: (
                        0,
                        (place_ref[0] + 1 + n // tiles) % slices * tiles + n % tiles,
                    ),
                ),
            ],
            out_specs=(
                pl.BlockSpec(
                    (1, rows, tile), lambda n, place_ref: (n // tiles, 0, n % tiles)
                ),
                pl.BlockSpec((rows, 1), lambda n, place_ref: (0, 0)),
            ),
        ),
        compiler_params=params(),
        cost_estimate=pl.CostEstimate(
            flops=2 * rows * in_dev * width,
            bytes_accessed=2 * in_dev * width + 2 * rows * (in_dev + width),
            transcendentals=0,
        ),
        name="out_projection",
    )(place, z, inverse, w_out)


def collect_kernel(slices, ids_ref, slot_ref, rows_ref, out_ref):
    rows = ids_ref.shape[0]
    count, depth = rows_ref.shape
    step = min(512, depth)
    at = ids_ref[...] * (slices * CAP) + slot_ref[...]
    lane = lax.broadcasted_iota(jnp.int32, (rows, count), 1)
    for s in range(slices):
        pick = (at + s * CAP == lane).astype(f32).astype(bf16)
        for c in range(0, depth, step):
            out_ref[:, s * depth + c : s * depth + c + step] = jnp.dot(
                pick, rows_ref[:, c : c + step], preferred_element_type=f32
            ).astype(bf16)


def collect(ids, slot, rows, slices):
    return pl.pallas_call(
        functools.partial(collect_kernel, slices),
        out_shape=jax.ShapeDtypeStruct((ids.shape[0], rows.shape[1] * slices), bf16),
        compiler_params=params(),
        name="collect",
    )(ids, slot, rows)


def turn(a, n, slices, r):
    return lax.ppermute(
        a, "expert", [(d, d // slices * slices + (d + r) % slices) for d in range(n)]
    )


def shards(
    tokens, w_in, w_out, w_bcd, dt_bias, decay_rate, skip_gain, norm_gain, expert_ids, decode_heads
):
    n = lax.axis_size("expert")
    slices = n // EXPERTS
    in_dev = w_in.shape[2]
    units = in_dev // EXPERTS
    heads = max(1, units // HEADDIM)
    width = tokens.shape[1]
    me = lax.axis_index("expert")
    place = (me % slices).astype(jnp.int32)
    place_arr = place.reshape(1)
    own_units = place * in_dev + me // slices * units
    same_slice = [[j * slices + s for j in range(EXPERTS)] for s in range(slices)]

    outgoing, slot = dispatch(expert_ids, tokens, slices)
    landed = lax.all_to_all(outgoing, "expert", split_axis=0, concat_axis=0, tiled=True)

    mixing = jnp.dot(tokens, w_bcd, preferred_element_type=f32)
    steps_dt = jax.nn.softplus(mixing[:, 2 * NS :] + dt_bias[None, :])
    coarse = lax.reduce_precision(steps_dt, 8, 7)
    pack = jnp.concatenate(
        [
            mixing[:, : 2 * NS],
            coarse,
            steps_dt - coarse,
            expert_ids.astype(f32),
            slot.astype(f32),
            jnp.zeros((tokens.shape[0], PACK - 2 * NS - 2 * HEADS - 2), f32),
        ],
        axis=1,
    ).astype(bf16)
    pack = lax.all_gather(pack, "expert", axis=0, tiled=True)
    first_head = (own_units // HEADDIM).astype(jnp.int32).reshape(1)
    weights = prepare(first_head, decay_rate, skip_gain, pack, heads)

    pieces = [landed] + [turn(landed, n, slices, r) for r in range(1, slices)]
    inner = in_projection(place_arr, pieces, w_in[0], units)
    rows = inner.shape[1]
    x = lax.all_to_all(
        inner, "expert", split_axis=0, concat_axis=0, axis_index_groups=same_slice, tiled=True
    )
    gain = lax.dynamic_slice(norm_gain, (own_units,), (units,)).reshape(1, units)
    z, state = scan(x, weights, gain, heads)
    z = lax.all_to_all(
        z, "expert", split_axis=0, concat_axis=0, axis_index_groups=same_slice, tiled=True
    )
    inverse = (1.0 / lax.dynamic_slice(norm_gain, (place * in_dev,), (in_dev,))).reshape(1, in_dev)
    partial, squares = out_projection(place_arr, z, inverse, w_out[0], slices)
    summed = partial[slices - 1].astype(f32)
    whole_squares = squares
    for r in range(1, slices):
        summed = summed + turn(partial[r - 1], n, slices, r).astype(f32)
        whole_squares = whole_squares + turn(squares, n, slices, r)
    factor = lax.rsqrt(whole_squares / INNER + 1e-05)
    back = lax.all_to_all(
        (summed * factor).astype(bf16), "expert", split_axis=0, concat_axis=0, tiled=True
    )
    mixed = collect(expert_ids, slot, back, slices)

    states = lax.all_gather(state.astype(bf16), "expert", axis=0, tiled=False)
    per_head = HEADDIM * heads // units
    want = decode_heads[0]
    states = (
        states.reshape(EXPERTS, slices, heads, NS, units // heads)
        .transpose(1, 0, 2, 3, 4)
        .reshape(HEADS, per_head, NS, units // heads)
    )
    chosen = lax.dynamic_index_in_dim(states, want, 0, False).astype(f32)
    chosen = chosen.transpose(0, 2, 1).reshape(1, HEADDIM * NS)
    return (mixed, chosen)


def solution(mesh):
    in_specs = (
        P(("groups", "expert"), None),
        P("expert", None, None),
        P("expert", None, None),
        P(),
        P(),
        P(),
        P(),
        P(),
        P(("groups", "expert"), None),
        P("expert"),
    )
    out_specs = (P(("groups", "expert"), None), P(("groups", "expert"), None))
    return jax.shard_map(shards, mesh=mesh, in_specs=in_specs, out_specs=out_specs, check_vma=False)
```

```python
import functools

import jax
import jax.numpy as jnp
from jax import lax
from jax.experimental import pallas as pl
from jax.experimental.pallas import tpu as pltpu
from jax.sharding import PartitionSpec as P

INNER = 4096
HEADDIM = 128
HEADS = 32
NS = 64
EXPERTS = 8
CAP = 24
PAIR = 256
PACK = 256
CHUNKS = 2
VMEM_BYTES = 40 * 1024 * 1024

f32 = jnp.float32
bf16 = jnp.bfloat16


def params():
    return pltpu.CompilerParams(vmem_limit_bytes=VMEM_BYTES)


def mask(condition):
    return condition.astype(f32).astype(bf16)


def iota(shape, dim):
    return lax.broadcasted_iota(jnp.int32, shape, dim)


def route(ids_row):
    rows = ids_row.shape[1]
    ids = jnp.broadcast_to(ids_row.astype(f32), (rows, rows)).T
    onehot = (ids == iota((rows, rows), 1).astype(f32)).astype(f32)
    lower = mask(iota((rows, rows), 1) < iota((rows, rows), 0))
    before = jnp.dot(lower, onehot.astype(bf16), preferred_element_type=f32)
    return ids, jnp.sum(before * onehot, axis=1, keepdims=True)


def dispatch_kernel(slices, bias_ref, ids_ref, tok_ref, bcd_ref, *outs):
    pack_ref, out_refs = outs[0], outs[1:]
    rows, width = tok_ref.shape
    depth = width // slices
    ids, slot = route(ids_ref[...])
    pick = mask(ids[:, :1] * CAP + slot == iota((rows, EXPERTS * CAP), 1).astype(f32))
    part = depth // CHUNKS
    step = min(512, part)
    for k in range(CHUNKS):
        for c in range(0, part, step):
            got = [
                lax.dot_general(
                    pick,
                    tok_ref[:, s * depth + k * part + c : s * depth + k * part + c + step],
                    (((0,), (0,)), ((), ())),
                    preferred_element_type=f32,
                )
                for s in range(slices)
            ]
            for e in range(EXPERTS):
                piece = jnp.concatenate([g[e * CAP : (e + 1) * CAP] for g in got], axis=0)
                out_refs[k][e * slices * CAP : (e + 1) * slices * CAP, c : c + step] = (
                    piece.astype(bf16)
                )

    across = (((1,), (1,)), ((), ()))
    tok = tok_ref[...]
    pack_ref[:, : 2 * NS] = lax.dot_general(
        tok, bcd_ref[: 2 * NS, :], across, preferred_element_type=f32
    ).astype(bf16)
    steps = bcd_ref[2 * NS : 2 * NS + HEADS, :]
    raw = lax.dot_general(
        tok, jnp.concatenate([steps] * 4, axis=0), across, preferred_element_type=f32
    )
    lane = iota((rows, 128), 1)
    for h in range(HEADS):
        raw = raw + jnp.where(lane % HEADS == h, bias_ref[h], 0.0)
    steps_dt = jnp.maximum(raw, 0.0) + jnp.log1p(jnp.exp(-jnp.abs(raw)))
    coarse = steps_dt.astype(bf16).astype(f32)
    side = jnp.where(lane < HEADS, coarse, steps_dt - coarse)
    side = jnp.where(lane == 2 * HEADS, ids, jnp.where(lane == 2 * HEADS + 1, slot, side))
    pack_ref[:, 2 * NS :] = jnp.where(lane < 2 * HEADS + 2, side, 0.0).astype(bf16)


def dispatch(bias, ids_row, tokens, bcd, slices):
    rows, width = tokens.shape
    vmem = pl.BlockSpec(memory_space=pltpu.VMEM)
    out = jax.ShapeDtypeStruct((EXPERTS * slices * CAP, width // slices // CHUNKS), bf16)
    return pl.pallas_call(
        functools.partial(dispatch_kernel, slices),
        out_shape=(jax.ShapeDtypeStruct((rows, PACK), bf16),) + (out,) * CHUNKS,
        in_specs=[pl.BlockSpec(memory_space=pltpu.SMEM), vmem, vmem, vmem],
        compiler_params=params(),
        name="dispatch",
    )(bias, ids_row, tokens, bcd)


def in_kernel(count, width, last, place_ref, *refs):
    rows_refs, w_refs, out_ref = refs[:count], refs[count : 2 * count], refs[-1]
    total = refs[2 * count][...] if last else None
    for r in range(count):
        part = jnp.dot(rows_refs[r][...], w_refs[r][...], preferred_element_type=f32)
        total = part if total is None else total + part
    if not last:
        out_ref[...] = total
        return
    for j in range(out_ref.shape[0]):
        out_ref[j] = total[:, j * width : (j + 1) * width].astype(bf16)


def in_projection(place, pieces, w_in, chunk, width=None, total=None, at=None):
    slices = len(pieces)
    rows, depth = pieces[0].shape
    in_dev = w_in.shape[1]
    last = total is not None
    span = EXPERTS * width if last else in_dev
    tile = min(256, span)
    first = at * (span // tile) if last else 0

    def w_spec(r):
        return pl.BlockSpec(
            (depth, tile),
            lambda n, place_ref: (
                (place_ref[0] - r + slices) % slices * CHUNKS + chunk,
                first + n,
            ),
        )

    in_specs = [pl.BlockSpec((rows, depth), lambda n, place_ref: (0, 0))] * slices
    in_specs += [w_spec(r) for r in range(slices)]
    operands = [*pieces, *([w_in] * slices)]
    if last:
        in_specs.append(pl.BlockSpec((rows, tile), lambda n, place_ref: (0, first + n)))
        operands.append(total)
        out_shape = jax.ShapeDtypeStruct((EXPERTS, rows, width), bf16)
        out_spec = pl.BlockSpec((tile // width, rows, width), lambda n, place_ref: (n, 0, 0))
    else:
        out_shape = jax.ShapeDtypeStruct((rows, in_dev), f32)
        out_spec = pl.BlockSpec((rows, tile), lambda n, place_ref: (0, n))
    return pl.pallas_call(
        functools.partial(in_kernel, slices, width, last),
        out_shape=out_shape,
        grid_spec=pltpu.PrefetchScalarGridSpec(
            num_scalar_prefetch=1,
            grid=(span // tile,),
            in_specs=in_specs,
            out_specs=out_spec,
        ),
        compiler_params=params(),
        cost_estimate=pl.CostEstimate(
            flops=2 * rows * slices * depth * span,
            bytes_accessed=2 * slices * depth * (span + rows) + 4 * rows * span,
            transcendentals=0,
        ),
        name="in_finish" if last else "in_begin",
    )(place, *operands)


def prep_kernel(heads, head_ref, rate_ref, skip_ref, pack_ref, w_ref, c_ref, b_ref, a_ref):
    pack = pack_ref[...]
    row = iota((128, PACK), 0)
    lane = iota((128, PACK), 1)
    choose = jnp.where(lane == 2 * NS + 2 * HEADS, 2.0 * CAP, 0.0)
    choose = choose + jnp.where(lane == 2 * NS + 2 * HEADS + 1, 1.0, 0.0)
    choose = jnp.where(row == heads, choose, 0.0)
    rate = jnp.zeros((128, PAIR), f32)
    for h in range(heads):
        at = lane - 2 * NS - head_ref[h]
        choose = jnp.where((row == h) & ((at == 0) | (at == HEADS)), 1.0, choose)
        rate = jnp.where(iota((128, PAIR), 0) == h, rate_ref[head_ref[h]], rate)
    across = lax.dot_general(
        choose.astype(bf16), pack, (((1,), (1,)), ((), ())), preferred_element_type=f32
    )
    upto = iota((PAIR, PAIR), 0)
    now = iota((PAIR, PAIR), 1)
    running = jnp.dot(
        -across * rate,
        (upto <= now).astype(f32),
        precision=lax.Precision.HIGHEST,
        preferred_element_type=f32,
    )
    second = iota((1, PAIR), 1) >= PAIR // 2
    column = across[heads : heads + 1] + jnp.where(second, float(CAP), 0.0)
    slots = 2 * CAP * EXPERTS
    place_t = mask(iota((slots, PAIR), 0).astype(f32) == column)
    down = running.T
    b_rows = pack[:, :NS]
    c_rows = pack[:, NS : 2 * NS]
    scores = lax.dot_general(
        c_rows, b_rows, (((1,), (1,)), ((), ())), preferred_element_type=f32
    )
    causal = upto >= now
    diagonal = upto == now
    b_cols = b_rows.astype(f32).T
    c_wide = c_rows.astype(f32)
    for h in range(heads):
        run_row = running[h : h + 1]
        run_col = down[:, h : h + 1]
        dt_row = across[h : h + 1]
        last = run_row[:, PAIR - 1 : PAIR]
        gap = jnp.where(causal, run_col - run_row, 0.0)
        weights = jnp.where(causal, jnp.exp(gap) * scores * dt_row, 0.0)
        weights = weights + jnp.where(diagonal, skip_ref[head_ref[h]], 0.0)
        half = jnp.dot(place_t, weights.astype(bf16), preferred_element_type=f32).astype(bf16)
        w_ref[h, 0] = lax.dot_general(
            half, place_t, (((1,), (1,)), ((), ())), preferred_element_type=f32
        ).astype(bf16)
        c_now = (c_wide * jnp.exp(run_col)).astype(bf16)
        c_ref[h, 0] = jnp.dot(place_t, c_now, preferred_element_type=f32).astype(bf16)
        b_now = (b_cols * (jnp.exp(last - run_row) * dt_row)).astype(bf16)
        b_ref[h, 0] = lax.dot_general(
            b_now, place_t, (((1,), (1,)), ((), ())), preferred_element_type=f32
        ).astype(bf16)
        a_ref[h, 0] = jnp.broadcast_to(jnp.exp(last), (8, 128))


def prepare(own_heads, rate, skip, pack):
    heads = own_heads.shape[0]
    pairs = pack.shape[0] // PAIR
    slots = 2 * CAP * EXPERTS
    smem = pl.BlockSpec(memory_space=pltpu.SMEM)

    def block(*dims):
        return pl.BlockSpec((heads, 1, *dims), lambda p: (0, p, 0, 0))

    return pl.pallas_call(
        functools.partial(prep_kernel, heads),
        out_shape=(
            jax.ShapeDtypeStruct((heads, pairs, slots, slots), bf16),
            jax.ShapeDtypeStruct((heads, pairs, slots, NS), bf16),
            jax.ShapeDtypeStruct((heads, pairs, NS, slots), bf16),
            jax.ShapeDtypeStruct((heads, pairs, 8, 128), f32),
        ),
        grid=(pairs,),
        in_specs=[smem, smem, smem, pl.BlockSpec((PAIR, PACK), lambda p: (p, 0))],
        out_specs=(block(slots, slots), block(slots, NS), block(NS, slots), block(8, 128)),
        compiler_params=params(),
        cost_estimate=pl.CostEstimate(
            flops=4 * heads * pairs * slots * slots * PAIR,
            bytes_accessed=2 * heads * pairs * slots * slots,
            transcendentals=heads * pairs * PAIR * PAIR,
        ),
        name="scan_weights",
    )(own_heads, rate, skip, pack)


def scan_kernel(x_ref, w_ref, c_ref, b_ref, a_ref, gain_ref, out_ref, last_ref, state):
    @pl.when(pl.program_id(0) == 0)
    def _():
        state[...] = jnp.zeros_like(state)

    experts, rows, width = x_ref.shape
    x = x_ref[...].reshape(experts * rows, width)
    before = state[...]
    y = jnp.dot(w_ref[0, 0], x, preferred_element_type=f32) + jnp.dot(
        c_ref[0, 0], before.astype(bf16), preferred_element_type=f32
    )
    after = before * a_ref[0, 0, 0:1, 0:1] + jnp.dot(
        b_ref[0, 0], x, preferred_element_type=f32
    )
    state[...] = after
    last_ref[...] = after
    out_ref[...] = (y * gain_ref[...]).astype(bf16).reshape(experts, rows, width)


def scan(x, weights, gain, h):
    experts, rows, width = x.shape
    pairs = rows // (2 * CAP)
    slots = 2 * CAP * EXPERTS

    def block(*dims):
        return pl.BlockSpec((1, 1, *dims), lambda p: (h, p, 0, 0))

    return pl.pallas_call(
        scan_kernel,
        out_shape=(
            jax.ShapeDtypeStruct(x.shape, bf16),
            jax.ShapeDtypeStruct((NS, width), f32),
        ),
        grid=(pairs,),
        in_specs=[
            pl.BlockSpec((experts, 2 * CAP, width), lambda p: (0, p, 0)),
            block(slots, slots),
            block(slots, NS),
            block(NS, slots),
            block(8, 128),
            pl.BlockSpec((1, width), lambda p: (0, 0)),
        ],
        out_specs=(
            pl.BlockSpec((experts, 2 * CAP, width), lambda p: (0, p, 0)),
            pl.BlockSpec((NS, width), lambda p: (0, 0)),
        ),
        scratch_shapes=[pltpu.VMEM((NS, width), f32)],
        compiler_params=params(),
        cost_estimate=pl.CostEstimate(
            flops=2 * pairs * slots * (slots + 2 * NS) * width,
            bytes_accessed=2 * pairs * slots * slots,
            transcendentals=0,
        ),
        name="scan",
    )(x, *weights, gain)


def chunk_product(z_ref, w_ref):
    owners, rows, width = z_ref.shape
    group = max(1, min(owners, 256 // width)) if width % 128 == 0 else 1
    total = None
    for j in range(0, owners, group):
        z = z_ref[j]
        if group > 1:
            z = jnp.concatenate([z_ref[j + i] for i in range(group)], axis=1)
        part = jnp.dot(
            z, w_ref[j * width : (j + group) * width, :], preferred_element_type=f32
        )
        total = part if total is None else total + part
    return total


def chunk_squares(z_ref, inverse_ref):
    owners, rows, width = z_ref.shape
    total = jnp.zeros((rows, 1), f32)
    for j in range(owners):
        z = z_ref[j].astype(f32) * inverse_ref[:, j * width : (j + 1) * width]
        total = total + jnp.sum(z * z, axis=1, keepdims=True)
    return total


def out_begin_kernel(place_ref, z_ref, w_ref, inverse_ref, out_ref, square_ref):
    @pl.when(pl.program_id(0) == 0)
    def _():
        square_ref[...] = chunk_squares(z_ref, inverse_ref)

    out_ref[0] = chunk_product(z_ref, w_ref)


def out_send_kernel(
    chunked, first, place_ref, z_ref, w_ref, inverse_ref, *refs
):
    refs = list(refs)
    total_ref, before_ref = (refs.pop(0), refs.pop(0)) if chunked else (None, None)
    out_ref = refs.pop(0)
    if first:
        square_ref = refs.pop(0)

        @pl.when(pl.program_id(0) == 0)
        def _():
            squares = chunk_squares(z_ref, inverse_ref)
            square_ref[...] = squares + before_ref[...] if chunked else squares

    total = chunk_product(z_ref, w_ref)
    if chunked:
        total = total + total_ref[0]
    out_ref[0] = total.astype(bf16)


def out_finish_kernel(chunked, others, place_ref, z_ref, w_ref, square_ref, *refs):
    refs = list(refs)
    total_ref = refs.pop(0) if chunked else None
    part_refs, square_refs, out_ref = refs[:others], refs[others : 2 * others], refs[-1]
    total = chunk_product(z_ref, w_ref)
    if chunked:
        total = total + total_ref[0]
    squares = square_ref[...]
    for part, square in zip(part_refs, square_refs):
        total = total + part[...].astype(f32)
        squares = squares + square[...]
    out_ref[...] = (total * lax.rsqrt(squares / INNER + 1e-05)).astype(bf16)


def out_call(kernel, place, operands, extra, row_block, span, shape, z, w_out, name):
    owners, rows, width = z.shape
    depth = owners * width
    slices, first, count, chunk = span
    slice_width = w_out.shape[1] // slices
    part = slice_width if chunk is None else slice_width // CHUNKS
    tile = min(512, part)
    tiles = part // tile
    offset = 0 if chunk is None else chunk * tiles
    whole = slice_width // tile

    def column(n, place_ref):
        return (place_ref[0] + first + n // tiles) % slices * whole + offset + n % tiles

    fixed = lambda *dims: pl.BlockSpec(dims, lambda n, place_ref: (0,) * len(dims))
    specs = [
        fixed(owners, rows, width),
        pl.BlockSpec((depth, tile), lambda n, place_ref: (row_block, column(n, place_ref))),
    ]
    for kind, _ in operands:
        if kind == "fixed":
            specs.append(fixed(*_.shape))
        elif kind == "total":
            specs.append(
                pl.BlockSpec(
                    (1, rows, tile),
                    lambda n, place_ref: (first - 1 + n // tiles, 0, offset + n % tiles),
                )
            )
        else:
            specs.append(pl.BlockSpec((rows, tile), lambda n, place_ref: (0, n)))
    if shape == 3:
        out_shape = [jax.ShapeDtypeStruct((count, rows, part), f32 if extra == "begin" else bf16)]
        out_specs = [
            pl.BlockSpec((1, rows, tile), lambda n, place_ref: (n // tiles, 0, n % tiles))
        ]
    else:
        out_shape = [jax.ShapeDtypeStruct((rows, part), bf16)]
        out_specs = [pl.BlockSpec((rows, tile), lambda n, place_ref: (0, n))]
    if extra is not None:
        out_shape.append(jax.ShapeDtypeStruct((rows, 1), f32))
        out_specs.append(fixed(rows, 1))
    return pl.pallas_call(
        kernel,
        out_shape=out_shape,
        grid_spec=pltpu.PrefetchScalarGridSpec(
            num_scalar_prefetch=1, grid=(count * tiles,), in_specs=specs, out_specs=out_specs
        ),
        compiler_params=params(),
        cost_estimate=pl.CostEstimate(
            flops=2 * rows * depth * count * part,
            bytes_accessed=2 * depth * count * part + 4 * rows * count * part,
            transcendentals=0,
        ),
        name=name,
    )(place, z, w_out, *[a for _, a in operands])


def collect_kernel(slices, ids_ref, *refs):
    chunk_refs, out_ref = refs[:-1], refs[-1]
    count, part = chunk_refs[0].shape
    rows = ids_ref.shape[1]
    depth = part * len(chunk_refs)
    step = min(512, part)
    ids, slot = route(ids_ref[...])
    at = ids[:, :1] * (slices * CAP) + slot
    lane = iota((rows, count), 1).astype(f32)
    for s in range(slices):
        pick = mask(at + s * CAP == lane)
        for k, rows_ref in enumerate(chunk_refs):
            for c in range(0, part, step):
                start = s * depth + k * part + c
                out_ref[:, start : start + step] = jnp.dot(
                    pick, rows_ref[:, c : c + step], preferred_element_type=f32
                ).astype(bf16)


def collect(ids_row, chunks, slices):
    width = sum(c.shape[1] for c in chunks) * slices
    return pl.pallas_call(
        functools.partial(collect_kernel, slices),
        out_shape=jax.ShapeDtypeStruct((ids_row.shape[1], width), bf16),
        compiler_params=params(),
        name="collect",
    )(ids_row, *chunks)


def turn(a, n, slices, r):
    return lax.ppermute(
        a, "expert", [(d, d // slices * slices + (d + r) % slices) for d in range(n)]
    )


def swap(a, groups=None):
    return lax.all_to_all(
        a, "expert", split_axis=0, concat_axis=0, axis_index_groups=groups, tiled=True
    )


def shards(
    tokens, w_in, w_out, w_bcd, dt_bias, decay_rate, skip_gain, norm_gain, expert_ids, decode_heads
):
    n = lax.axis_size("expert")
    slices = n // EXPERTS
    in_dev = w_in.shape[2]
    width = min(HEADDIM, in_dev // EXPERTS)
    heads = in_dev // EXPERTS // width
    span = EXPERTS * width
    me = lax.axis_index("expert")
    place = (me % slices).astype(jnp.int32)
    owner = (me // slices).astype(jnp.int32)
    place_arr = place.reshape(1)
    starts = [place * in_dev + h * span + owner * width for h in range(heads)]
    same_slice = [[j * slices + s for j in range(EXPERTS)] for s in range(slices)]
    ids_row = expert_ids.reshape(1, -1)
    w_in, w_out = w_in[0], w_out[0]

    pack, *outgoing = dispatch(dt_bias, ids_row, tokens, w_bcd.T, slices)
    pack = lax.all_gather(pack, "expert", axis=0, tiled=True)
    landed = [swap(o) for o in outgoing]

    def with_turned(a):
        return [a] + [turn(a, n, slices, r) for r in range(1, slices)]

    begun = in_projection(place_arr, with_turned(landed[0]), w_in, 0)
    landed[1], pack = lax.optimization_barrier((landed[1], pack))
    own_heads = jnp.stack(starts) // HEADDIM
    weights = prepare(own_heads.astype(jnp.int32), decay_rate, skip_gain, pack)
    pieces = with_turned(landed[1])
    x = [
        swap(in_projection(place_arr, pieces, w_in, 1, width, begun, h), same_slice)
        for h in range(heads)
    ]

    z, states = [], []
    for h in range(heads):
        gain = lax.dynamic_slice(norm_gain, (starts[h],), (width,)).reshape(1, width)
        rows, state = scan(x[h], weights, gain, h)
        z.append(swap(rows, same_slice))
        states.append(state)
    states = lax.all_gather(jnp.stack(states), "expert", axis=0, tiled=False)

    inverse = 1.0 / lax.dynamic_slice(norm_gain, (place * in_dev,), (in_dev,))
    inverse = [inverse[h * span : (h + 1) * span].reshape(1, span) for h in range(heads)]
    chunked = heads > 1
    total = squares = None
    for h in range(heads - 1):
        total, squares = out_call(
            out_begin_kernel,
            place_arr,
            [("fixed", inverse[h])],
            "begin",
            h,
            (slices, 1, slices, None),
            3,
            z[h],
            w_out,
            "out_begin",
        )
    h = heads - 1
    sent = []
    for k in range(CHUNKS):
        operands = [("fixed", inverse[h])]
        if chunked:
            operands += [("total", total), ("fixed", squares)]
        got = out_call(
            functools.partial(out_send_kernel, chunked, k == 0),
            place_arr,
            operands,
            "send" if k == 0 else None,
            h,
            (slices, 1, slices - 1, k),
            3,
            z[h],
            w_out,
            "out_send",
        )
        if k == 0:
            all_squares = got[1]
            others = [turn(all_squares, n, slices, r) for r in range(1, slices)]
        sent.append([turn(got[0][r - 1], n, slices, r) for r in range(1, slices)])
    back = []
    for k in range(CHUNKS):
        operands = [("fixed", all_squares)]
        if chunked:
            operands.append(("total", total))
        operands += [("part", a) for a in sent[k]] + [("fixed", a) for a in others]
        [done] = out_call(
            functools.partial(out_finish_kernel, chunked, slices - 1),
            place_arr,
            operands,
            None,
            h,
            (slices, slices, 1, k),
            2,
            z[h],
            w_out,
            "out_finish",
        )
        if k == CHUNKS - 1:
            done, states = lax.optimization_barrier((done, states))
        back.append(swap(done))
    mixed = collect(ids_row, back, slices)

    start = decode_heads[0] * HEADDIM
    within = start % in_dev // width
    states = states.reshape(EXPERTS, slices, heads, NS, width)
    chosen = lax.dynamic_slice(
        states,
        (within % EXPERTS, start // in_dev, within // EXPERTS, 0, 0),
        (HEADDIM // width, 1, 1, NS, width),
    )
    chosen = chosen.reshape(HEADDIM // width, NS, width).transpose(0, 2, 1)
    return (mixed, chosen.reshape(1, HEADDIM * NS))


def solution(mesh):
    in_specs = (
        P(("groups", "expert"), None),
        P("expert", None, None),
        P("expert", None, None),
        P(),
        P(),
        P(),
        P(),
        P(),
        P(("groups", "expert"), None),
        P("expert"),
    )
    out_specs = (P(("groups", "expert"), None), P(("groups", "expert"), None))
    return jax.shard_map(shards, mesh=mesh, in_specs=in_specs, out_specs=out_specs, check_vma=False)
```

```python
import functools

import jax
import jax.numpy as jnp
from jax import lax
from jax.experimental import pallas as pl
from jax.experimental.pallas import tpu as pltpu
from jax.sharding import PartitionSpec as P

INNER = 4096
HEADDIM = 128
HEADS = 32
NS = 64
EXPERTS = 8
CAP = 24
PAIR = 256
PACK = 256
CHUNKS = 2
VMEM_BYTES = 32 * 1024 * 1024

f32 = jnp.float32
bf16 = jnp.bfloat16


def params():
    return pltpu.CompilerParams(vmem_limit_bytes=VMEM_BYTES)


def mask(condition):
    return condition.astype(f32).astype(bf16)


def iota(shape, dim):
    return lax.broadcasted_iota(jnp.int32, shape, dim)


def route(ids_row):
    rows = ids_row.shape[1]
    ids = jnp.broadcast_to(ids_row.astype(f32), (rows, rows)).T
    onehot = (ids == iota((rows, rows), 1).astype(f32)).astype(f32)
    lower = mask(iota((rows, rows), 1) < iota((rows, rows), 0))
    before = jnp.dot(lower, onehot.astype(bf16), preferred_element_type=f32)
    return ids, jnp.sum(before * onehot, axis=1, keepdims=True)


def dispatch_kernel(slices, bias_ref, ids_ref, tok_ref, bcd_ref, *outs):
    pack_ref, out_ref = outs
    rows, width = tok_ref.shape
    depth = width // slices
    ids, slot = route(ids_ref[...])
    pick = mask(ids[:, :1] * CAP + slot == iota((rows, EXPERTS * CAP), 1).astype(f32))
    step = min(512, depth)
    for c in range(0, depth, step):
        got = [
            lax.dot_general(
                pick,
                tok_ref[:, s * depth + c : s * depth + c + step],
                (((0,), (0,)), ((), ())),
                preferred_element_type=f32,
            )
            for s in range(slices)
        ]
        for e in range(EXPERTS):
            piece = jnp.concatenate([g[e * CAP : (e + 1) * CAP] for g in got], axis=0)
            out_ref[e * slices * CAP : (e + 1) * slices * CAP, c : c + step] = piece.astype(bf16)

    across = (((1,), (1,)), ((), ()))
    tok = tok_ref[...]
    pack_ref[:, : 2 * NS] = lax.dot_general(
        tok, bcd_ref[: 2 * NS, :], across, preferred_element_type=f32
    ).astype(bf16)
    steps = bcd_ref[2 * NS : 2 * NS + HEADS, :]
    raw = lax.dot_general(
        tok, jnp.concatenate([steps] * 4, axis=0), across, preferred_element_type=f32
    )
    lane = iota((rows, 128), 1)
    for h in range(HEADS):
        raw = raw + jnp.where(lane % HEADS == h, bias_ref[h], 0.0)
    steps_dt = jnp.maximum(raw, 0.0) + jnp.log1p(jnp.exp(-jnp.abs(raw)))
    coarse = steps_dt.astype(bf16).astype(f32)
    side = jnp.where(lane < HEADS, coarse, steps_dt - coarse)
    side = jnp.where(lane == 2 * HEADS, ids, jnp.where(lane == 2 * HEADS + 1, slot, side))
    pack_ref[:, 2 * NS :] = jnp.where(lane < 2 * HEADS + 2, side, 0.0).astype(bf16)


def dispatch(bias, ids_row, tokens, bcd, slices):
    rows, width = tokens.shape
    vmem = pl.BlockSpec(memory_space=pltpu.VMEM)
    out = jax.ShapeDtypeStruct((EXPERTS * slices * CAP, width // slices), bf16)
    return pl.pallas_call(
        functools.partial(dispatch_kernel, slices),
        out_shape=(jax.ShapeDtypeStruct((rows, PACK), bf16), out),
        in_specs=[pl.BlockSpec(memory_space=pltpu.SMEM), vmem, vmem, vmem],
        compiler_params=params(),
        name="dispatch",
    )(bias, ids_row, tokens, bcd)


def in_kernel(count, shares, turns, place_ref, *refs):
    rows_refs, w_refs, out_refs = refs[:count], refs[count : 2 * count], refs[2 * count :]
    total = None
    for r in range(count):
        part = jnp.dot(rows_refs[r][...], w_refs[r][...], preferred_element_type=f32)
        total = part if total is None else total + part
    for i, q in enumerate(turns):

        @pl.when(pl.program_id(0) == i)
        def _(i=i, q=q):
            units = out_refs[i].shape[1]
            own = total[:, :units]
            for k in range(1, shares):
                at = (place_ref[1] ^ q) % shares
                own = jnp.where(at == k, total[:, k * units : (k + 1) * units], own)
            out_refs[i][...] = own.astype(bf16)


def in_projection(place, pieces, w_in, units, turns):
    slices = len(pieces)
    rows, depth = pieces[0].shape
    tile = max(128, units)
    shares = tile // units

    def w_spec(r):
        def index(i, place_ref):
            q = sum(jnp.where(i == k, t, 0) for k, t in enumerate(turns))
            return (place_ref[0] - r + slices) % slices, (place_ref[1] ^ q) // shares

        return pl.BlockSpec((depth, tile), index)

    return pl.pallas_call(
        functools.partial(in_kernel, slices, shares, turns),
        out_shape=[jax.ShapeDtypeStruct((rows, units), bf16)] * len(turns),
        grid_spec=pltpu.PrefetchScalarGridSpec(
            num_scalar_prefetch=1,
            grid=(len(turns),),
            in_specs=[pl.BlockSpec((rows, depth), lambda i, place_ref: (0, 0))] * slices
            + [w_spec(r) for r in range(slices)],
            out_specs=[pl.BlockSpec((rows, units), lambda i, place_ref: (0, 0))] * len(turns),
        ),
        compiler_params=params(),
        cost_estimate=pl.CostEstimate(
            flops=2 * rows * slices * depth * tile * len(turns),
            bytes_accessed=2 * slices * depth * (tile * len(turns) + rows),
            transcendentals=0,
        ),
        name="in_projection",
    )(place, *pieces, *([w_in] * slices))


def prep_kernel(heads, place_ref, head_ref, rate_ref, skip_ref, pack_ref, w_ref, c_ref, b_ref, a_ref):
    pack = pack_ref[...]
    row = iota((128, PACK), 0)
    lane = iota((128, PACK), 1)
    side = lane - 2 * NS - 2 * HEADS
    choose = ((row == heads) & (side == 0)) | ((row == heads + 1) & (side == 1))
    choose = choose.astype(f32)
    rate = jnp.zeros((128, PAIR), f32)
    for h in range(heads):
        at = lane - 2 * NS - head_ref[h]
        choose = jnp.where((row == h) & ((at == 0) | (at == HEADS)), 1.0, choose)
        rate = jnp.where(iota((128, PAIR), 0) == h, rate_ref[head_ref[h]], rate)
    across = lax.dot_general(
        choose.astype(bf16), pack, (((1,), (1,)), ((), ())), preferred_element_type=f32
    )
    upto = iota((PAIR, PAIR), 0)
    now = iota((PAIR, PAIR), 1)
    running = jnp.dot(
        -across * rate,
        (upto <= now).astype(f32),
        precision=lax.Precision.HIGHEST,
        preferred_element_type=f32,
    )
    second = iota((1, PAIR), 1) >= PAIR // 2
    turn_of = across[heads : heads + 1].astype(jnp.int32) ^ place_ref[1]
    column = turn_of * (2 * CAP) + across[heads + 1 : heads + 2].astype(jnp.int32)
    column = column + jnp.where(second, CAP, 0)
    slots = 2 * CAP * EXPERTS
    place_t = mask(iota((slots, PAIR), 0) == column)
    down = running.T
    b_rows = pack[:, :NS]
    c_rows = pack[:, NS : 2 * NS]
    scores = lax.dot_general(
        c_rows, b_rows, (((1,), (1,)), ((), ())), preferred_element_type=f32
    )
    causal = upto >= now
    diagonal = upto == now
    b_cols = b_rows.astype(f32).T
    c_wide = c_rows.astype(f32)
    for h in range(heads):
        run_row = running[h : h + 1]
        run_col = down[:, h : h + 1]
        dt_row = across[h : h + 1]
        last = run_row[:, PAIR - 1 : PAIR]
        gap = jnp.where(causal, run_col - run_row, 0.0)
        weights = jnp.where(causal, jnp.exp(gap) * scores * dt_row, 0.0)
        weights = weights + jnp.where(diagonal, skip_ref[head_ref[h]], 0.0)
        half = jnp.dot(place_t, weights.astype(bf16), preferred_element_type=f32).astype(bf16)
        w_ref[h, 0] = lax.dot_general(
            half, place_t, (((1,), (1,)), ((), ())), preferred_element_type=f32
        ).astype(bf16)
        c_now = (c_wide * jnp.exp(run_col)).astype(bf16)
        c_ref[h, 0] = jnp.dot(place_t, c_now, preferred_element_type=f32).astype(bf16)
        b_now = (b_cols * (jnp.exp(last - run_row) * dt_row)).astype(bf16)
        b_ref[h, 0] = lax.dot_general(
            b_now, place_t, (((1,), (1,)), ((), ())), preferred_element_type=f32
        ).astype(bf16)
        a_ref[h, 0] = jnp.broadcast_to(jnp.exp(last), (8, 128))


def prepare(place, own_heads, rate, skip, pack):
    heads = own_heads.shape[0]
    pairs = pack.shape[0] // PAIR
    slots = 2 * CAP * EXPERTS
    smem = pl.BlockSpec(memory_space=pltpu.SMEM)

    def block(*dims):
        return pl.BlockSpec((heads, 1, *dims), lambda p: (0, p, 0, 0))

    return pl.pallas_call(
        functools.partial(prep_kernel, heads),
        out_shape=(
            jax.ShapeDtypeStruct((heads, pairs, slots, slots), bf16),
            jax.ShapeDtypeStruct((heads, pairs, slots, NS), bf16),
            jax.ShapeDtypeStruct((heads, pairs, NS, slots), bf16),
            jax.ShapeDtypeStruct((heads, pairs, 8, 128), f32),
        ),
        grid=(pairs,),
        in_specs=[smem, smem, smem, smem, pl.BlockSpec((PAIR, PACK), lambda p: (p, 0))],
        out_specs=(block(slots, slots), block(slots, NS), block(NS, slots), block(8, 128)),
        compiler_params=params(),
        cost_estimate=pl.CostEstimate(
            flops=4 * heads * pairs * slots * slots * PAIR,
            bytes_accessed=2 * heads * pairs * slots * slots,
            transcendentals=heads * pairs * PAIR * PAIR,
        ),
        name="scan_weights",
    )(place, own_heads, rate, skip, pack)


def scan_kernel(*refs):
    x_refs, refs = refs[:EXPERTS], refs[EXPERTS:]
    w_ref, c_ref, b_ref, a_ref, gain_ref = refs[:5]
    out_refs, last_ref, state = refs[5 : 5 + EXPERTS], refs[-2], refs[-1]

    @pl.when(pl.program_id(0) == 0)
    def _():
        state[...] = jnp.zeros_like(state)

    rows = x_refs[0].shape[0]
    x = jnp.concatenate([x_ref[...] for x_ref in x_refs], axis=0)
    before = state[...]
    y = jnp.dot(w_ref[0, 0], x, preferred_element_type=f32) + jnp.dot(
        c_ref[0, 0], before.astype(bf16), preferred_element_type=f32
    )
    after = before * a_ref[0, 0, 0:1, 0:1] + jnp.dot(
        b_ref[0, 0], x, preferred_element_type=f32
    )
    state[...] = after
    last_ref[...] = after
    z = (y * gain_ref[...]).astype(bf16)
    for q in range(EXPERTS):
        out_refs[q][...] = z[q * rows : (q + 1) * rows]


def scan(x, weights, gain, h):
    rows = x[0].shape[0]
    width = gain.shape[1]
    pairs = rows // (2 * CAP)
    slots = 2 * CAP * EXPERTS

    def block(*dims):
        return pl.BlockSpec((1, 1, *dims), lambda p: (h, p, 0, 0))

    *z, state = pl.pallas_call(
        scan_kernel,
        out_shape=[jax.ShapeDtypeStruct((rows, width), bf16)] * EXPERTS
        + [jax.ShapeDtypeStruct((NS, width), f32)],
        grid=(pairs,),
        in_specs=[pl.BlockSpec((2 * CAP, width), lambda p: (p, h))] * EXPERTS
        + [
            block(slots, slots),
            block(slots, NS),
            block(NS, slots),
            block(8, 128),
            pl.BlockSpec((1, width), lambda p: (0, 0)),
        ],
        out_specs=[pl.BlockSpec((2 * CAP, width), lambda p: (p, 0))] * EXPERTS
        + [pl.BlockSpec((NS, width), lambda p: (0, 0))],
        scratch_shapes=[pltpu.VMEM((NS, width), f32)],
        compiler_params=params(),
        cost_estimate=pl.CostEstimate(
            flops=2 * pairs * slots * (slots + 2 * NS) * width,
            bytes_accessed=2 * pairs * slots * slots,
            transcendentals=0,
        ),
        name="scan",
    )(*x, *weights, gain)
    return z, state


def chunk_product(z_refs, w_refs):
    width = z_refs[0].shape[1]
    group = max(1, 256 // width) if width % 128 == 0 else 1
    total = None
    for q in range(0, EXPERTS, group):
        z = [r[...] for r in z_refs[q : q + group]]
        w = [r[...] for r in w_refs[q : q + group]]
        z = jnp.concatenate(z, axis=1) if group > 1 else z[0]
        w = jnp.concatenate(w, axis=0) if group > 1 else w[0]
        part = jnp.dot(z, w, preferred_element_type=f32)
        total = part if total is None else total + part
    return total


def chunk_squares(place_ref, z_refs, inverse_ref, heads, h):
    total = jnp.zeros((z_refs[0].shape[0], 1), f32)
    for q in range(EXPERTS):
        z = z_refs[q][...].astype(f32) * inverse_ref[(place_ref[1] ^ q) * heads + h]
        total = total + jnp.sum(z * z, axis=1, keepdims=True)
    return total


def out_kernel(layout, place_ref, *refs):
    kind, heads, h, counted, others = layout
    refs = list(refs)

    def take(count):
        got = refs[:count]
        del refs[:count]
        return got

    z_refs, w_refs = take(EXPERTS), take(EXPERTS)
    inverse_ref = take(1)[0] if counted else None
    total_ref = take(1)[0] if kind != "begin" and h > 0 else None
    before_ref = take(1)[0] if counted and kind == "send" and h > 0 else None
    squares_refs = take(1 + others) if kind == "finish" else None
    part_refs = take(others) if kind == "finish" else None
    out_ref = take(1)[0]
    if inverse_ref is not None:

        @pl.when(pl.program_id(0) == 0)
        def _():
            squares = chunk_squares(place_ref, z_refs, inverse_ref, heads, h)
            refs[0][...] = squares if before_ref is None else squares + before_ref[...]

    total = chunk_product(z_refs, w_refs)
    if total_ref is not None:
        total = total + total_ref[0]
    if kind == "finish":
        squares = sum(r[...] for r in squares_refs)
        for part in part_refs:
            total = total + part[...].astype(f32)
        total = total * lax.rsqrt(squares / INNER + 1e-05)
        out_ref[...] = total.astype(bf16)
    else:
        out_ref[0] = total.astype(out_ref.dtype)


def out_projection(
    kind, *, place, z, w_out, heads, h, chunk, inverse=None, total=None, squares=(), parts=()
):
    rows, width = z[0].shape
    slices = INNER // w_out.shape[0]
    slice_width = w_out.shape[1] // slices
    part = slice_width if kind == "begin" else slice_width // CHUNKS
    count = {"begin": slices, "send": slices - 1, "finish": 1}[kind]
    first = slices if kind == "finish" else 1
    tile = min(512, part)
    tiles = part // tile
    whole = slice_width // tile
    offset = 0 if kind == "begin" else chunk * tiles

    def w_spec(q):
        return pl.BlockSpec(
            (width, tile),
            lambda n, place_ref: (
                (place_ref[1] ^ q) * heads + h,
                (place_ref[0] + first + n // tiles) % slices * whole + offset + n % tiles,
            ),
        )

    def fixed(*dims):
        return pl.BlockSpec(dims, lambda n, place_ref: (0,) * len(dims))

    operands = [*z, *([w_out] * EXPERTS)]
    specs = [fixed(rows, width)] * EXPERTS + [w_spec(q) for q in range(EXPERTS)]
    if inverse is not None:
        operands.append(inverse)
        specs.append(fixed(*inverse.shape))
    if total is not None:
        operands.append(total)
        specs.append(
            pl.BlockSpec(
                (1, rows, tile),
                lambda n, place_ref: (first - 1 + n // tiles, 0, offset + n % tiles),
            )
        )
    operands += [*squares, *parts]
    specs += [fixed(rows, 1)] * len(squares)
    specs += [pl.BlockSpec((rows, tile), lambda n, place_ref: (0, n))] * len(parts)
    if kind == "finish":
        out_shape = [jax.ShapeDtypeStruct((rows, part), bf16)]
        out_specs = [pl.BlockSpec((rows, tile), lambda n, place_ref: (0, n))]
    else:
        dtype = f32 if kind == "begin" else bf16
        out_shape = [jax.ShapeDtypeStruct((count, rows, part), dtype)]
        out_specs = [
            pl.BlockSpec((1, rows, tile), lambda n, place_ref: (n // tiles, 0, n % tiles))
        ]
    if inverse is not None:
        out_shape.append(jax.ShapeDtypeStruct((rows, 1), f32))
        out_specs.append(fixed(rows, 1))
    return pl.pallas_call(
        functools.partial(out_kernel, (kind, heads, h, inverse is not None, len(parts))),
        out_shape=out_shape,
        grid_spec=pltpu.PrefetchScalarGridSpec(
            num_scalar_prefetch=1, grid=(count * tiles,), in_specs=specs, out_specs=out_specs
        ),
        compiler_params=params(),
        cost_estimate=pl.CostEstimate(
            flops=2 * rows * EXPERTS * width * count * part,
            bytes_accessed=2 * EXPERTS * width * count * part + 4 * rows * count * part,
            transcendentals=0,
        ),
        name="out_" + kind,
    )(place, *operands)


def collect_kernel(slices, ids_ref, *refs):
    chunk_refs, out_ref = refs[:-1], refs[-1]
    count, part = chunk_refs[0].shape
    rows = ids_ref.shape[1]
    depth = part * len(chunk_refs)
    step = min(512, part)
    ids, slot = route(ids_ref[...])
    at = ids[:, :1] * (slices * CAP) + slot
    lane = iota((rows, count), 1).astype(f32)
    for s in range(slices):
        pick = mask(at + s * CAP == lane)
        for k, rows_ref in enumerate(chunk_refs):
            for c in range(0, part, step):
                start = s * depth + k * part + c
                out_ref[:, start : start + step] = jnp.dot(
                    pick, rows_ref[:, c : c + step], preferred_element_type=f32
                ).astype(bf16)


def collect(ids_row, chunks, slices):
    width = sum(c.shape[1] for c in chunks) * slices
    return pl.pallas_call(
        functools.partial(collect_kernel, slices),
        out_shape=jax.ShapeDtypeStruct((ids_row.shape[1], width), bf16),
        compiler_params=params(),
        name="collect",
    )(ids_row, *chunks)


def turn(a, n, slices, r):
    return lax.ppermute(
        a, "expert", [(d, d // slices * slices + (d + r) % slices) for d in range(n)]
    )


def swap(a, groups=None):
    return lax.all_to_all(
        a, "expert", split_axis=0, concat_axis=0, axis_index_groups=groups, tiled=True
    )


def exchange(arrays, n, slices):
    out = list(arrays)
    for q in reversed(range(1, EXPERTS)):
        pairs = [(d, (d // slices ^ q) * slices + d % slices) for d in range(n)]
        out[q] = lax.ppermute(arrays[q], "expert", pairs)
    return out


def shards(
    tokens, w_in, w_out, w_bcd, dt_bias, decay_rate, skip_gain, norm_gain, expert_ids, decode_heads
):
    n = lax.axis_size("expert")
    slices = n // EXPERTS
    in_dev = w_in.shape[2]
    units = in_dev // EXPERTS
    width = min(HEADDIM, units)
    heads = units // width
    me = lax.axis_index("expert")
    chip = (me // slices).astype(jnp.int32)
    place = jnp.stack([(me % slices).astype(jnp.int32), chip])
    start = place[0] * in_dev + chip * units
    ids_row = expert_ids.reshape(1, -1)
    w_in, w_out = w_in[0], w_out[0]

    pack, outgoing = dispatch(dt_bias, ids_row, tokens, w_bcd.T, slices)
    pack = lax.all_gather(pack, "expert", axis=0, tiled=True)
    landed = swap(outgoing)
    pieces = [landed] + [turn(landed, n, slices, r) for r in range(1, slices)]
    own_heads = start // HEADDIM + jnp.arange(heads, dtype=jnp.int32)
    inner = [None] * EXPERTS
    for order in ((7, 6), (5, 4), (3, 2), (1, 0)):
        got = in_projection(place, pieces, w_in, units, order)
        for q, a in zip(order, got):
            inner[q] = a
        if order == (7, 6):
            weights = prepare(place, own_heads, decay_rate, skip_gain, pack)
            pieces, weights = lax.optimization_barrier((pieces, weights))
    x = exchange(inner, n, slices)

    gain = lax.dynamic_slice(norm_gain, (start,), (units,))
    z, states = [], []
    for h in range(heads):
        rows, state = scan(x, weights, gain[h * width : (h + 1) * width].reshape(1, width), h)
        z.append(exchange(rows, n, slices))
        states.append(state)
    states = lax.all_gather(jnp.stack(states), "expert", axis=0, tiled=False)

    inverse = 1.0 / lax.dynamic_slice(norm_gain, (place[0] * in_dev,), (in_dev,))
    inverse = inverse.reshape(in_dev // width, 1, width)
    project = functools.partial(out_projection, place=place, w_out=w_out, heads=heads)
    total = None
    squares = ()
    for h in range(heads - 1):
        total, squares = project("begin", z=z[h], h=h, chunk=0, inverse=inverse)
        squares = (squares,)
    h = heads - 1
    sent = []
    for k in range(CHUNKS):
        first = inverse if k == 0 else None
        got = project(
            "send",
            z=z[h],
            h=h,
            chunk=k,
            inverse=first,
            total=total,
            squares=squares if k == 0 else (),
        )
        if k == 0:
            all_squares = [got[1]] + [turn(got[1], n, slices, r) for r in range(1, slices)]
        sent.append([turn(got[0][r - 1], n, slices, r) for r in range(1, slices)])
    back = []
    for k in range(CHUNKS):
        [done] = project(
            "finish", z=z[h], h=h, chunk=k, total=total, squares=all_squares, parts=sent[k]
        )
        back.append(swap(done))
    mixed = collect(ids_row, back, slices)

    want = decode_heads[0] * HEADDIM
    within = want % in_dev // width
    states = states.reshape(EXPERTS, slices, heads, NS, width)
    chosen = lax.dynamic_slice(
        states,
        (within // heads, want // in_dev, within % heads, 0, 0),
        (HEADDIM // width, 1, 1, NS, width),
    )
    chosen = chosen.reshape(HEADDIM // width, NS, width).transpose(0, 2, 1)
    return (mixed, chosen.reshape(1, HEADDIM * NS))


def solution(mesh):
    in_specs = (
        P(("groups", "expert"), None),
        P("expert", None, None),
        P("expert", None, None),
        P(),
        P(),
        P(),
        P(),
        P(),
        P(("groups", "expert"), None),
        P("expert"),
    )
    out_specs = (P(("groups", "expert"), None), P(("groups", "expert"), None))
    return jax.shard_map(shards, mesh=mesh, in_specs=in_specs, out_specs=out_specs, check_vma=False)
```

```python
import functools

import jax
import jax.numpy as jnp
from jax import lax
from jax.experimental import pallas as pl
from jax.experimental.pallas import tpu as pltpu
from jax.sharding import PartitionSpec as P

INNER = 4096
HEADDIM = 128
HEADS = 32
NS = 64
EXPERTS = 8
CAP = 24
PAIR = 256
PACK = 256
CHUNKS = 2
VMEM_BYTES = 32 * 1024 * 1024

f32 = jnp.float32
bf16 = jnp.bfloat16


def params():
    return pltpu.CompilerParams(vmem_limit_bytes=VMEM_BYTES)


def mask(condition):
    return condition.astype(f32).astype(bf16)


def iota(shape, dim):
    return lax.broadcasted_iota(jnp.int32, shape, dim)


def route(ids_row):
    rows = ids_row.shape[1]
    ids = jnp.broadcast_to(ids_row.astype(f32), (rows, rows)).T
    onehot = (ids == iota((rows, rows), 1).astype(f32)).astype(f32)
    lower = mask(iota((rows, rows), 1) < iota((rows, rows), 0))
    before = jnp.dot(lower, onehot.astype(bf16), preferred_element_type=f32)
    return ids, jnp.sum(before * onehot, axis=1, keepdims=True)


def fetched(refs, buffers, sems):
    copies = [
        pltpu.make_async_copy(ref, buffer, sems.at[i])
        for i, (ref, buffer) in enumerate(zip(refs, buffers))
    ]
    for copy in copies:
        copy.start()
    for copy in copies:
        copy.wait()


def fetching_call(kernel, operands, out_shape, name):
    buffers = [pltpu.VMEM(a.shape, a.dtype) for a in operands]
    return pl.pallas_call(
        kernel,
        out_shape=out_shape,
        in_specs=[pl.BlockSpec(memory_space=pl.ANY)] * len(operands),
        scratch_shapes=[*buffers, pltpu.SemaphoreType.DMA((len(operands),))],
        compiler_params=params(),
        name=name,
    )(*operands)


def dispatch_kernel(slices, ids_hbm, tok_hbm, out_ref, ids_ref, tok_ref, sems):
    fetched((ids_hbm, tok_hbm), (ids_ref, tok_ref), sems)
    rows, width = tok_ref.shape
    depth = width // slices
    ids, slot = route(ids_ref[...])
    pick = mask(ids[:, :1] * CAP + slot == iota((rows, EXPERTS * CAP), 1).astype(f32))
    step = min(512, depth)
    for c in range(0, depth, step):
        got = [
            lax.dot_general(
                pick,
                tok_ref[:, s * depth + c : s * depth + c + step],
                (((0,), (0,)), ((), ())),
                preferred_element_type=f32,
            )
            for s in range(slices)
        ]
        for e in range(EXPERTS):
            piece = jnp.concatenate([g[e * CAP : (e + 1) * CAP] for g in got], axis=0)
            out_ref[e * slices * CAP : (e + 1) * slices * CAP, c : c + step] = piece.astype(bf16)


def dispatch(ids_row, tokens, slices):
    width = tokens.shape[1]
    return fetching_call(
        functools.partial(dispatch_kernel, slices),
        (ids_row, tokens),
        jax.ShapeDtypeStruct((EXPERTS * slices * CAP, width // slices), bf16),
        "dispatch",
    )


def pack_kernel(*refs):
    pack_ref = refs[4]
    bias_ref, ids_ref, tok_ref, bcd_ref, sems = refs[5:]
    fetched(refs[:4], refs[5:9], sems)
    rows = tok_ref.shape[0]
    ids, slot = route(ids_ref[...])
    across = (((1,), (1,)), ((), ()))
    tok = tok_ref[...]
    pack_ref[:, : 2 * NS] = lax.dot_general(
        tok, bcd_ref[: 2 * NS, :], across, preferred_element_type=f32
    ).astype(bf16)
    steps = bcd_ref[2 * NS : 2 * NS + HEADS, :]
    raw = lax.dot_general(
        tok, jnp.concatenate([steps] * 4, axis=0), across, preferred_element_type=f32
    )
    spread = (iota((HEADS, 128), 1) % HEADS == iota((HEADS, 128), 0)).astype(f32)
    raw = raw + jnp.dot(
        bias_ref[...], spread, precision=lax.Precision.HIGHEST, preferred_element_type=f32
    )
    steps_dt = jnp.maximum(raw, 0.0) + jnp.log1p(jnp.exp(-jnp.abs(raw)))
    coarse = steps_dt.astype(bf16).astype(f32)
    lane = iota((rows, 128), 1)
    side = jnp.where(lane < HEADS, coarse, steps_dt - coarse)
    side = jnp.where(lane == 2 * HEADS, ids, jnp.where(lane == 2 * HEADS + 1, slot, side))
    pack_ref[:, 2 * NS :] = jnp.where(lane < 2 * HEADS + 2, side, 0.0).astype(bf16)


def scan_operands(bias, ids_row, tokens, bcd):
    return fetching_call(
        pack_kernel,
        (bias.reshape(1, -1), ids_row, tokens, bcd),
        jax.ShapeDtypeStruct((tokens.shape[0], PACK), bf16),
        "scan_operands",
    )


def in_kernel(count, shares, turns, place_ref, *refs):
    rows_refs, w_refs, out_refs = refs[:count], refs[count : 2 * count], refs[2 * count :]
    total = None
    for r in range(count):
        part = jnp.dot(rows_refs[r][...], w_refs[r][...], preferred_element_type=f32)
        total = part if total is None else total + part
    for i, q in enumerate(turns):

        @pl.when(pl.program_id(0) == i)
        def _(i=i, q=q):
            units = out_refs[i].shape[1]
            own = total[:, :units]
            for k in range(1, shares):
                at = (place_ref[1] ^ q) % shares
                own = jnp.where(at == k, total[:, k * units : (k + 1) * units], own)
            out_refs[i][...] = own.astype(bf16)


def in_projection(place, pieces, w_in, units, turns):
    slices = len(pieces)
    rows, depth = pieces[0].shape
    tile = max(128, units)
    shares = tile // units

    def w_spec(r):
        def index(i, place_ref):
            q = sum(jnp.where(i == k, t, 0) for k, t in enumerate(turns))
            return (place_ref[0] - r + slices) % slices, (place_ref[1] ^ q) // shares

        return pl.BlockSpec((depth, tile), index)

    return pl.pallas_call(
        functools.partial(in_kernel, slices, shares, turns),
        out_shape=[jax.ShapeDtypeStruct((rows, units), bf16)] * len(turns),
        grid_spec=pltpu.PrefetchScalarGridSpec(
            num_scalar_prefetch=1,
            grid=(len(turns),),
            in_specs=[pl.BlockSpec((rows, depth), lambda i, place_ref: (0, 0))] * slices
            + [w_spec(r) for r in range(slices)],
            out_specs=[pl.BlockSpec((rows, units), lambda i, place_ref: (0, 0))] * len(turns),
        ),
        compiler_params=params(),
        cost_estimate=pl.CostEstimate(
            flops=2 * rows * slices * depth * tile * len(turns),
            bytes_accessed=2 * slices * depth * (tile * len(turns) + rows),
            transcendentals=0,
        ),
        name="in_projection",
    )(place, *pieces, *([w_in] * slices))


def prep_kernel(heads, place_ref, head_ref, rate_ref, skip_ref, pack_ref, w_ref, c_ref, b_ref, a_ref):
    pack = pack_ref[...]
    row = iota((128, PACK), 0)
    lane = iota((128, PACK), 1)
    side = lane - 2 * NS - 2 * HEADS
    choose = ((row == heads) & (side == 0)) | ((row == heads + 1) & (side == 1))
    choose = choose.astype(f32)
    rate = jnp.zeros((128, PAIR), f32)
    for h in range(heads):
        at = lane - 2 * NS - head_ref[h]
        choose = jnp.where((row == h) & ((at == 0) | (at == HEADS)), 1.0, choose)
        rate = jnp.where(iota((128, PAIR), 0) == h, rate_ref[head_ref[h]], rate)
    across = lax.dot_general(
        choose.astype(bf16), pack, (((1,), (1,)), ((), ())), preferred_element_type=f32
    )
    upto = iota((PAIR, PAIR), 0)
    now = iota((PAIR, PAIR), 1)
    running = jnp.dot(
        -across * rate,
        (upto <= now).astype(f32),
        precision=lax.Precision.HIGHEST,
        preferred_element_type=f32,
    )
    second = iota((1, PAIR), 1) >= PAIR // 2
    turn_of = across[heads : heads + 1].astype(jnp.int32) ^ place_ref[1]
    column = turn_of * (2 * CAP) + across[heads + 1 : heads + 2].astype(jnp.int32)
    column = column + jnp.where(second, CAP, 0)
    slots = 2 * CAP * EXPERTS
    place_t = mask(iota((slots, PAIR), 0) == column)
    down = running.T
    b_rows = pack[:, :NS]
    c_rows = pack[:, NS : 2 * NS]
    scores = lax.dot_general(
        c_rows, b_rows, (((1,), (1,)), ((), ())), preferred_element_type=f32
    )
    causal = upto >= now
    diagonal = upto == now
    b_cols = b_rows.astype(f32).T
    c_wide = c_rows.astype(f32)
    for h in range(heads):
        run_row = running[h : h + 1]
        run_col = down[:, h : h + 1]
        dt_row = across[h : h + 1]
        last = run_row[:, PAIR - 1 : PAIR]
        gap = jnp.where(causal, run_col - run_row, 0.0)
        weights = jnp.where(causal, jnp.exp(gap) * scores * dt_row, 0.0)
        weights = weights + jnp.where(diagonal, skip_ref[head_ref[h]], 0.0)
        half = jnp.dot(place_t, weights.astype(bf16), preferred_element_type=f32).astype(bf16)
        w_ref[h, 0] = lax.dot_general(
            half, place_t, (((1,), (1,)), ((), ())), preferred_element_type=f32
        ).astype(bf16)
        c_now = (c_wide * jnp.exp(run_col)).astype(bf16)
        c_ref[h, 0] = jnp.dot(place_t, c_now, preferred_element_type=f32).astype(bf16)
        b_now = (b_cols * (jnp.exp(last - run_row) * dt_row)).astype(bf16)
        b_ref[h, 0] = lax.dot_general(
            b_now, place_t, (((1,), (1,)), ((), ())), preferred_element_type=f32
        ).astype(bf16)
        a_ref[h, 0] = jnp.broadcast_to(jnp.exp(last), (8, 128))


def prepare(place, own_heads, rate, skip, pack):
    heads = own_heads.shape[0]
    pairs = pack.shape[0] // PAIR
    slots = 2 * CAP * EXPERTS
    smem = pl.BlockSpec(memory_space=pltpu.SMEM)

    def block(*dims):
        return pl.BlockSpec((heads, 1, *dims), lambda p: (0, p, 0, 0))

    return pl.pallas_call(
        functools.partial(prep_kernel, heads),
        out_shape=(
            jax.ShapeDtypeStruct((heads, pairs, slots, slots), bf16),
            jax.ShapeDtypeStruct((heads, pairs, slots, NS), bf16),
            jax.ShapeDtypeStruct((heads, pairs, NS, slots), bf16),
            jax.ShapeDtypeStruct((heads, pairs, 8, 128), f32),
        ),
        grid=(pairs,),
        in_specs=[smem, smem, smem, smem, pl.BlockSpec((PAIR, PACK), lambda p: (p, 0))],
        out_specs=(block(slots, slots), block(slots, NS), block(NS, slots), block(8, 128)),
        compiler_params=params(),
        cost_estimate=pl.CostEstimate(
            flops=4 * heads * pairs * slots * slots * PAIR,
            bytes_accessed=2 * heads * pairs * slots * slots,
            transcendentals=heads * pairs * PAIR * PAIR,
        ),
        name="scan_weights",
    )(place, own_heads, rate, skip, pack)


def scan_kernel(*refs):
    x_refs, refs = refs[:EXPERTS], refs[EXPERTS:]
    w_ref, c_ref, b_ref, a_ref, gain_ref = refs[:5]
    out_refs, last_ref, state = refs[5 : 5 + EXPERTS], refs[-2], refs[-1]

    @pl.when(pl.program_id(0) == 0)
    def _():
        state[...] = jnp.zeros_like(state)

    rows = x_refs[0].shape[0]
    x = jnp.concatenate([x_ref[...] for x_ref in x_refs], axis=0)
    before = state[...]
    y = jnp.dot(w_ref[0, 0], x, preferred_element_type=f32) + jnp.dot(
        c_ref[0, 0], before.astype(bf16), preferred_element_type=f32
    )
    after = before * a_ref[0, 0, 0:1, 0:1] + jnp.dot(
        b_ref[0, 0], x, preferred_element_type=f32
    )
    state[...] = after
    last_ref[...] = after
    z = (y * gain_ref[...]).astype(bf16)
    for q in range(EXPERTS):
        out_refs[q][...] = z[q * rows : (q + 1) * rows]


def scan(x, weights, gain, h):
    rows = x[0].shape[0]
    width = gain.shape[1]
    pairs = rows // (2 * CAP)
    slots = 2 * CAP * EXPERTS

    def block(*dims):
        return pl.BlockSpec((1, 1, *dims), lambda p: (h, p, 0, 0))

    *z, state = pl.pallas_call(
        scan_kernel,
        out_shape=[jax.ShapeDtypeStruct((rows, width), bf16)] * EXPERTS
        + [jax.ShapeDtypeStruct((NS, width), f32)],
        grid=(pairs,),
        in_specs=[pl.BlockSpec((2 * CAP, width), lambda p: (p, h))] * EXPERTS
        + [
            block(slots, slots),
            block(slots, NS),
            block(NS, slots),
            block(8, 128),
            pl.BlockSpec((1, width), lambda p: (0, 0)),
        ],
        out_specs=[pl.BlockSpec((2 * CAP, width), lambda p: (p, 0))] * EXPERTS
        + [pl.BlockSpec((NS, width), lambda p: (0, 0))],
        scratch_shapes=[pltpu.VMEM((NS, width), f32)],
        compiler_params=params(),
        cost_estimate=pl.CostEstimate(
            flops=2 * pairs * slots * (slots + 2 * NS) * width,
            bytes_accessed=2 * pairs * slots * slots,
            transcendentals=0,
        ),
        name="scan",
    )(*x, *weights, gain)
    return z, state


def out_kernel(kind, heads, counted, others, place_ref, *refs):
    refs = list(refs)

    def take(count):
        got = refs[:count]
        del refs[:count]
        return got

    z_refs, w_refs = take(EXPERTS * heads), take(EXPERTS * heads)
    inverse_ref = take(1)[0] if counted else None
    squares_refs = take(1 + others) if kind == "finish" else None
    part_refs = take(others) if kind == "finish" else None
    out_ref = take(1)[0]
    rows, width = z_refs[0].shape
    if counted:

        @pl.when(pl.program_id(0) == 0)
        def _():
            squares = jnp.zeros((rows, 1), f32)
            for q in range(EXPERTS):
                for h in range(heads):
                    z = z_refs[q * heads + h][...].astype(f32)
                    z = z * inverse_ref[(place_ref[1] ^ q) * heads + h]
                    squares = squares + jnp.sum(z * z, axis=1, keepdims=True)
            refs[0][...] = squares

    group = max(1, 256 // width) if width % 128 == 0 else 1
    total = None
    for i in range(0, EXPERTS * heads, group):
        z = [r[...] for r in z_refs[i : i + group]]
        w = [r[...] for r in w_refs[i : i + group]]
        z = jnp.concatenate(z, axis=1) if group > 1 else z[0]
        w = jnp.concatenate(w, axis=0) if group > 1 else w[0]
        part = jnp.dot(z, w, preferred_element_type=f32)
        total = part if total is None else total + part
    if kind == "finish":
        squares = sum(r[...] for r in squares_refs)
        for part in part_refs:
            total = total + part[...].astype(f32)
        out_ref[...] = (total * lax.rsqrt(squares / INNER + 1e-05)).astype(bf16)
    else:
        out_ref[0] = total.astype(bf16)


def out_projection(kind, chunk, *, place, z, w_out, inverse=None, squares=(), parts=()):
    heads = len(z[0])
    rows, width = z[0][0].shape
    slices = INNER // w_out.shape[0]
    slice_width = w_out.shape[1] // slices
    part = slice_width // CHUNKS
    count, first = (slices - 1, 1) if kind == "send" else (1, 0)
    tile = min(512, part)
    tiles = part // tile
    whole = slice_width // tile
    offset = chunk * tiles

    def w_spec(q, h):
        return pl.BlockSpec(
            (width, tile),
            lambda n, place_ref: (
                (place_ref[1] ^ q) * heads + h,
                (place_ref[0] + first + n // tiles) % slices * whole + offset + n % tiles,
            ),
        )

    def fixed(*dims):
        return pl.BlockSpec(dims, lambda n, place_ref: (0,) * len(dims))

    pieces = [(q, h) for q in range(EXPERTS) for h in range(heads)]
    operands = [z[q][h] for q, h in pieces] + [w_out] * len(pieces)
    specs = [fixed(rows, width)] * len(pieces) + [w_spec(q, h) for q, h in pieces]
    if inverse is not None:
        operands.append(inverse)
        specs.append(fixed(*inverse.shape))
    operands += [*squares, *parts]
    specs += [fixed(rows, 1)] * len(squares)
    specs += [pl.BlockSpec((rows, tile), lambda n, place_ref: (0, n))] * len(parts)
    if kind == "finish":
        out_shape = [jax.ShapeDtypeStruct((rows, part), bf16)]
        out_specs = [pl.BlockSpec((rows, tile), lambda n, place_ref: (0, n))]
    else:
        out_shape = [jax.ShapeDtypeStruct((count, rows, part), bf16)]
        out_specs = [
            pl.BlockSpec((1, rows, tile), lambda n, place_ref: (n // tiles, 0, n % tiles))
        ]
    if inverse is not None:
        out_shape.append(jax.ShapeDtypeStruct((rows, 1), f32))
        out_specs.append(fixed(rows, 1))
    return pl.pallas_call(
        functools.partial(out_kernel, kind, heads, inverse is not None, len(parts)),
        out_shape=out_shape,
        grid_spec=pltpu.PrefetchScalarGridSpec(
            num_scalar_prefetch=1, grid=(count * tiles,), in_specs=specs, out_specs=out_specs
        ),
        compiler_params=params(),
        cost_estimate=pl.CostEstimate(
            flops=2 * rows * w_out.shape[0] * count * part,
            bytes_accessed=2 * w_out.shape[0] * count * part + 2 * rows * count * part,
            transcendentals=0,
        ),
        name="out_" + kind,
    )(place, *operands)


def collect_kernel(slices, ids_ref, *refs):
    chunk_refs, out_ref = refs[:-1], refs[-1]
    count, part = chunk_refs[0].shape
    rows = ids_ref.shape[1]
    depth = part * len(chunk_refs)
    step = min(512, part)
    ids, slot = route(ids_ref[...])
    at = ids[:, :1] * (slices * CAP) + slot
    lane = iota((rows, count), 1).astype(f32)
    for s in range(slices):
        pick = mask(at + s * CAP == lane)
        for k, rows_ref in enumerate(chunk_refs):
            for c in range(0, part, step):
                start = s * depth + k * part + c
                out_ref[:, start : start + step] = jnp.dot(
                    pick, rows_ref[:, c : c + step], preferred_element_type=f32
                ).astype(bf16)


def collect(ids_row, chunks, slices):
    width = sum(c.shape[1] for c in chunks) * slices
    return pl.pallas_call(
        functools.partial(collect_kernel, slices),
        out_shape=jax.ShapeDtypeStruct((ids_row.shape[1], width), bf16),
        compiler_params=params(),
        name="collect",
    )(ids_row, *chunks)


def turn(a, n, slices, r):
    return lax.ppermute(
        a, "expert", [(d, d // slices * slices + (d + r) % slices) for d in range(n)]
    )


def swap(a, groups=None):
    return lax.all_to_all(
        a, "expert", split_axis=0, concat_axis=0, axis_index_groups=groups, tiled=True
    )


def across(a, q, n, slices):
    pairs = [(d, (d // slices ^ q) * slices + d % slices) for d in range(n)]
    return lax.ppermute(a, "expert", pairs)


def exchange(arrays, n, slices):
    out = list(arrays)
    for q in reversed(range(1, EXPERTS)):
        out[q] = across(arrays[q], q, n, slices)
    return out


def decode_state(states, want, chip, place, n, slices):
    heads, _, width = states.shape
    held, seats = states[None], []
    for q in (4, 2, 1):
        held = jnp.concatenate([held, across(held, q, n, slices)], axis=0)
        seats.append(q)

    def picked(head):
        first = head * HEADDIM % (EXPERTS * heads * width) // width
        pieces = []
        for i in range(HEADDIM // width):
            distance = (first + i) // heads ^ chip
            seat = sum((distance // q % 2) << k for k, q in enumerate(seats))
            pieces.append(
                lax.dynamic_slice(held, (seat, (first + i) % heads, 0, 0), (1, 1, NS, width))
            )
        return jnp.concatenate(pieces, axis=0) if len(pieces) > 1 else pieces[0]

    chosen = picked(want)
    lies = want * HEADDIM // (EXPERTS * heads * width)
    for r in range(1, slices):
        asked = turn(want, n, slices, slices - r)
        got = turn(picked(asked), n, slices, r)
        chosen = jnp.where((place - lies + slices) % slices == r, got, chosen)
    chosen = chosen.reshape(HEADDIM // width, NS, width).transpose(0, 2, 1)
    return chosen.astype(f32).reshape(1, HEADDIM * NS)


def shards(
    tokens, w_in, w_out, w_bcd, dt_bias, decay_rate, skip_gain, norm_gain, expert_ids, decode_heads
):
    n = lax.axis_size("expert")
    slices = n // EXPERTS
    in_dev = w_in.shape[2]
    units = in_dev // EXPERTS
    width = min(HEADDIM, units)
    heads = units // width
    me = lax.axis_index("expert")
    chip = (me // slices).astype(jnp.int32)
    place = jnp.stack([(me % slices).astype(jnp.int32), chip])
    start = place[0] * in_dev + chip * units
    ids_row = expert_ids.reshape(1, -1)
    w_in, w_out = w_in[0], w_out[0]

    landed = swap(dispatch(ids_row, tokens, slices))
    pack = scan_operands(dt_bias, ids_row, tokens, w_bcd.T)
    pack = lax.all_gather(pack, "expert", axis=0, tiled=True)
    own_heads = start // HEADDIM + jnp.arange(heads, dtype=jnp.int32)
    weights = prepare(place, own_heads, decay_rate, skip_gain, pack)

    pieces = [landed] + [turn(landed, n, slices, r) for r in range(1, slices)]
    inner = [None] * EXPERTS
    for order in ((7, 6), (5, 4), (3, 2, 1), (0,)):
        if order == (0,):
            pieces, weights = lax.optimization_barrier((pieces, weights))
        for q, a in zip(order, in_projection(place, pieces, w_in, units, order)):
            inner[q] = a
    x = exchange(inner, n, slices)

    gain = lax.dynamic_slice(norm_gain, (start,), (units,))
    z, states = [], []
    for h in range(heads):
        rows, state = scan(x, weights, gain[h * width : (h + 1) * width].reshape(1, width), h)
        z.append(exchange(rows, n, slices))
        states.append(state.astype(bf16))
    z = [[z[h][q] for h in range(heads)] for q in range(EXPERTS)]
    decoded = decode_state(jnp.stack(states), decode_heads[0], chip, place[0], n, slices)

    inverse = 1.0 / lax.dynamic_slice(norm_gain, (place[0] * in_dev,), (in_dev,))
    inverse = inverse.reshape(in_dev // width, 1, width)
    project = functools.partial(out_projection, place=place, z=z, w_out=w_out)
    sent = []
    for k in range(CHUNKS):
        got = project("send", k, inverse=inverse if k == 0 else None)
        if k == 0:
            squares = [got[1]] + [turn(got[1], n, slices, r) for r in range(1, slices)]
        sent.append([turn(got[0][r - 1], n, slices, r) for r in range(1, slices)])
    back = []
    for k in range(CHUNKS):
        [done] = project("finish", k, squares=squares, parts=sent[k])
        back.append(swap(done))
    return (collect(ids_row, back, slices), decoded)


def solution(mesh):
    in_specs = (
        P(("groups", "expert"), None),
        P("expert", None, None),
        P("expert", None, None),
        P(),
        P(),
        P(),
        P(),
        P(),
        P(("groups", "expert"), None),
        P("expert"),
    )
    out_specs = (P(("groups", "expert"), None), P(("groups", "expert"), None))
    return jax.shard_map(shards, mesh=mesh, in_specs=in_specs, out_specs=out_specs, check_vma=False)
```

```python
import functools

import jax
import jax.numpy as jnp
from jax import lax
from jax.experimental import pallas as pl
from jax.experimental.pallas import tpu as pltpu
from jax.sharding import PartitionSpec as P

INNER = 4096
HEADDIM = 128
HEADS = 32
NS = 64
EXPERTS = 8
CAP = 24
PAIR = 256
PACK = 256
CHUNKS = 2
VMEM_BYTES = 48 * 1024 * 1024

f32 = jnp.float32
bf16 = jnp.bfloat16


def params():
    return pltpu.CompilerParams(vmem_limit_bytes=VMEM_BYTES)


def mask(condition):
    return condition.astype(f32).astype(bf16)


def iota(shape, dim):
    return lax.broadcasted_iota(jnp.int32, shape, dim)


def route(ids_row):
    rows = ids_row.shape[1]
    ids = jnp.broadcast_to(ids_row.astype(f32), (rows, rows)).T
    onehot = (ids == iota((rows, rows), 1).astype(f32)).astype(f32)
    lower = mask(iota((rows, rows), 1) < iota((rows, rows), 0))
    before = jnp.dot(lower, onehot.astype(bf16), preferred_element_type=f32)
    return ids, jnp.sum(before * onehot, axis=1, keepdims=True)


def fetched(refs, buffers, sems):
    copies = [
        pltpu.make_async_copy(ref, buffer, sems.at[i])
        for i, (ref, buffer) in enumerate(zip(refs, buffers))
    ]
    for copy in copies:
        copy.start()
    for copy in copies:
        copy.wait()


def fetching_call(kernel, operands, out_shape, name):
    buffers = [pltpu.VMEM(a.shape, a.dtype) for a in operands]
    return pl.pallas_call(
        kernel,
        out_shape=out_shape,
        in_specs=[pl.BlockSpec(memory_space=pltpu.HBM)] * len(operands),
        scratch_shapes=[*buffers, pltpu.SemaphoreType.DMA((len(operands),))],
        compiler_params=params(),
        name=name,
    )(*operands)


def dispatch_kernel(slices, *refs):
    pack_ref, out_ref = refs[4:6]
    bias_ref, ids_ref, tok_ref, bcd_ref, sems = refs[6:]
    fetched(refs[:4], refs[6:10], sems)
    rows, width = tok_ref.shape
    depth = width // slices
    ids, slot = route(ids_ref[...])
    pick = mask(ids[:, :1] * CAP + slot == iota((rows, EXPERTS * CAP), 1).astype(f32))
    step = min(512, depth)
    for c in range(0, depth, step):
        got = [
            lax.dot_general(
                pick,
                tok_ref[:, s * depth + c : s * depth + c + step],
                (((0,), (0,)), ((), ())),
                preferred_element_type=f32,
            )
            for s in range(slices)
        ]
        for e in range(EXPERTS):
            piece = jnp.concatenate([g[e * CAP : (e + 1) * CAP] for g in got], axis=0)
            out_ref[e * slices * CAP : (e + 1) * slices * CAP, c : c + step] = piece.astype(bf16)

    across = (((1,), (1,)), ((), ()))
    tok = tok_ref[...]
    pack_ref[:, : 2 * NS] = lax.dot_general(
        tok, bcd_ref[: 2 * NS, :], across, preferred_element_type=f32
    ).astype(bf16)
    steps = bcd_ref[2 * NS : 2 * NS + HEADS, :]
    raw = lax.dot_general(
        tok, jnp.concatenate([steps] * 4, axis=0), across, preferred_element_type=f32
    )
    spread = (iota((HEADS, 128), 1) % HEADS == iota((HEADS, 128), 0)).astype(f32)
    raw = raw + jnp.dot(
        bias_ref[...], spread, precision=lax.Precision.HIGHEST, preferred_element_type=f32
    )
    steps_dt = jnp.maximum(raw, 0.0) + jnp.log1p(jnp.exp(-jnp.abs(raw)))
    coarse = steps_dt.astype(bf16).astype(f32)
    lane = iota((rows, 128), 1)
    side = jnp.where(lane < HEADS, coarse, steps_dt - coarse)
    side = jnp.where(lane == 2 * HEADS, ids, jnp.where(lane == 2 * HEADS + 1, slot, side))
    pack_ref[:, 2 * NS :] = jnp.where(lane < 2 * HEADS + 2, side, 0.0).astype(bf16)


def dispatch(bias, ids_row, tokens, bcd, slices):
    rows, width = tokens.shape
    return fetching_call(
        functools.partial(dispatch_kernel, slices),
        (bias.reshape(1, -1), ids_row, tokens, bcd),
        (
            jax.ShapeDtypeStruct((rows, PACK), bf16),
            jax.ShapeDtypeStruct((EXPERTS * slices * CAP, width // slices), bf16),
        ),
        "dispatch",
    )


def in_kernel(count, shares, turns, place_ref, *refs):
    rows_refs, w_refs, out_refs = refs[:count], refs[count : 2 * count], refs[2 * count :]
    total = None
    for r in range(count):
        part = jnp.dot(rows_refs[r][...], w_refs[r][...], preferred_element_type=f32)
        total = part if total is None else total + part
    for i, q in enumerate(turns):

        @pl.when(pl.program_id(0) == i)
        def _(i=i, q=q):
            units = out_refs[i].shape[1]
            own = total[:, :units]
            for k in range(1, shares):
                at = (place_ref[1] ^ q) % shares
                own = jnp.where(at == k, total[:, k * units : (k + 1) * units], own)
            out_refs[i][...] = own.astype(bf16)


def in_projection(place, pieces, w_in, units, turns):
    slices = len(pieces)
    rows, depth = pieces[0].shape
    tile = max(128, units)
    shares = tile // units

    def w_spec(r):
        def index(i, place_ref):
            q = sum(jnp.where(i == k, t, 0) for k, t in enumerate(turns))
            return (place_ref[0] - r + slices) % slices, (place_ref[1] ^ q) // shares

        return pl.BlockSpec((depth, tile), index)

    return pl.pallas_call(
        functools.partial(in_kernel, slices, shares, turns),
        out_shape=[jax.ShapeDtypeStruct((rows, units), bf16)] * len(turns),
        grid_spec=pltpu.PrefetchScalarGridSpec(
            num_scalar_prefetch=1,
            grid=(len(turns),),
            in_specs=[pl.BlockSpec((rows, depth), lambda i, place_ref: (0, 0))] * slices
            + [w_spec(r) for r in range(slices)],
            out_specs=[pl.BlockSpec((rows, units), lambda i, place_ref: (0, 0))] * len(turns),
        ),
        compiler_params=params(),
        cost_estimate=pl.CostEstimate(
            flops=2 * rows * slices * depth * tile * len(turns),
            bytes_accessed=2 * slices * depth * (tile * len(turns) + rows),
            transcendentals=0,
        ),
        name="in_projection",
    )(place, *pieces, *([w_in] * slices))


def prep_kernel(heads, place_ref, head_ref, rate_ref, skip_ref, pack_ref, w_ref, c_ref, b_ref, a_ref):
    pack = pack_ref[...]
    row = iota((128, PACK), 0)
    lane = iota((128, PACK), 1)
    side = lane - 2 * NS - 2 * HEADS
    choose = ((row == heads) & (side == 0)) | ((row == heads + 1) & (side == 1))
    choose = choose.astype(f32)
    rate = jnp.zeros((128, PAIR), f32)
    for h in range(heads):
        at = lane - 2 * NS - head_ref[h]
        choose = jnp.where((row == h) & ((at == 0) | (at == HEADS)), 1.0, choose)
        rate = jnp.where(iota((128, PAIR), 0) == h, rate_ref[head_ref[h]], rate)
    across = lax.dot_general(
        choose.astype(bf16), pack, (((1,), (1,)), ((), ())), preferred_element_type=f32
    )
    upto = iota((PAIR, PAIR), 0)
    now = iota((PAIR, PAIR), 1)
    running = jnp.dot(
        -across * rate,
        (upto <= now).astype(f32),
        precision=lax.Precision.HIGHEST,
        preferred_element_type=f32,
    )
    second = iota((1, PAIR), 1) >= PAIR // 2
    turn_of = across[heads : heads + 1].astype(jnp.int32) ^ place_ref[1]
    column = turn_of * (2 * CAP) + across[heads + 1 : heads + 2].astype(jnp.int32)
    column = column + jnp.where(second, CAP, 0)
    slots = 2 * CAP * EXPERTS
    place_t = mask(iota((slots, PAIR), 0) == column)
    down = running.T
    b_rows = pack[:, :NS]
    c_rows = pack[:, NS : 2 * NS]
    scores = lax.dot_general(
        c_rows, b_rows, (((1,), (1,)), ((), ())), preferred_element_type=f32
    )
    causal = upto >= now
    diagonal = upto == now
    b_cols = b_rows.astype(f32).T
    c_wide = c_rows.astype(f32)
    for h in range(heads):
        run_row = running[h : h + 1]
        run_col = down[:, h : h + 1]
        dt_row = across[h : h + 1]
        last = run_row[:, PAIR - 1 : PAIR]
        gap = jnp.where(causal, run_col - run_row, 0.0)
        weights = jnp.where(causal, jnp.exp(gap) * scores * dt_row, 0.0)
        weights = weights + jnp.where(diagonal, skip_ref[head_ref[h]], 0.0)
        half = jnp.dot(place_t, weights.astype(bf16), preferred_element_type=f32).astype(bf16)
        w_ref[h, 0] = lax.dot_general(
            half, place_t, (((1,), (1,)), ((), ())), preferred_element_type=f32
        ).astype(bf16)
        c_now = (c_wide * jnp.exp(run_col)).astype(bf16)
        c_ref[h, 0] = jnp.dot(place_t, c_now, preferred_element_type=f32).astype(bf16)
        b_now = (b_cols * (jnp.exp(last - run_row) * dt_row)).astype(bf16)
        b_ref[h, 0] = lax.dot_general(
            b_now, place_t, (((1,), (1,)), ((), ())), preferred_element_type=f32
        ).astype(bf16)
        a_ref[h, 0] = jnp.broadcast_to(jnp.exp(last), (8, 128))


def prepare(place, own_heads, rate, skip, pack):
    heads = own_heads.shape[0]
    pairs = pack.shape[0] // PAIR
    slots = 2 * CAP * EXPERTS
    smem = pl.BlockSpec(memory_space=pltpu.SMEM)

    def block(*dims):
        return pl.BlockSpec((heads, 1, *dims), lambda p: (0, p, 0, 0))

    return pl.pallas_call(
        functools.partial(prep_kernel, heads),
        out_shape=(
            jax.ShapeDtypeStruct((heads, pairs, slots, slots), bf16),
            jax.ShapeDtypeStruct((heads, pairs, slots, NS), bf16),
            jax.ShapeDtypeStruct((heads, pairs, NS, slots), bf16),
            jax.ShapeDtypeStruct((heads, pairs, 8, 128), f32),
        ),
        grid=(pairs,),
        in_specs=[smem, smem, smem, smem, pl.BlockSpec((PAIR, PACK), lambda p: (p, 0))],
        out_specs=(block(slots, slots), block(slots, NS), block(NS, slots), block(8, 128)),
        compiler_params=params(),
        cost_estimate=pl.CostEstimate(
            flops=4 * heads * pairs * slots * slots * PAIR,
            bytes_accessed=2 * heads * pairs * slots * slots,
            transcendentals=heads * pairs * PAIR * PAIR,
        ),
        name="scan_weights",
    )(place, own_heads, rate, skip, pack)


def scan_kernel(*refs):
    x_refs, refs = refs[:EXPERTS], refs[EXPERTS:]
    w_ref, c_ref, b_ref, a_ref, gain_ref = refs[:5]
    out_refs, last_ref, state = refs[5 : 5 + EXPERTS], refs[-2], refs[-1]

    @pl.when(pl.program_id(0) == 0)
    def _():
        state[...] = jnp.zeros_like(state)

    rows = x_refs[0].shape[0]
    x = jnp.concatenate([x_ref[...] for x_ref in x_refs], axis=0)
    before = state[...]
    y = jnp.dot(w_ref[0, 0], x, preferred_element_type=f32) + jnp.dot(
        c_ref[0, 0], before.astype(bf16), preferred_element_type=f32
    )
    after = before * a_ref[0, 0, 0:1, 0:1] + jnp.dot(
        b_ref[0, 0], x, preferred_element_type=f32
    )
    state[...] = after
    last_ref[...] = after
    z = (y * gain_ref[...]).astype(bf16)
    for q in range(EXPERTS):
        out_refs[q][...] = z[q * rows : (q + 1) * rows]


def scan(x, weights, gain, h):
    rows = x[0].shape[0]
    width = gain.shape[1]
    pairs = rows // (2 * CAP)
    slots = 2 * CAP * EXPERTS

    def block(*dims):
        return pl.BlockSpec((1, 1, *dims), lambda p: (h, p, 0, 0))

    *z, state = pl.pallas_call(
        scan_kernel,
        out_shape=[jax.ShapeDtypeStruct((rows, width), bf16)] * EXPERTS
        + [jax.ShapeDtypeStruct((NS, width), f32)],
        grid=(pairs,),
        in_specs=[pl.BlockSpec((2 * CAP, width), lambda p: (p, h))] * EXPERTS
        + [
            block(slots, slots),
            block(slots, NS),
            block(NS, slots),
            block(8, 128),
            pl.BlockSpec((1, width), lambda p: (0, 0)),
        ],
        out_specs=[pl.BlockSpec((2 * CAP, width), lambda p: (p, 0))] * EXPERTS
        + [pl.BlockSpec((NS, width), lambda p: (0, 0))],
        scratch_shapes=[pltpu.VMEM((NS, width), f32)],
        compiler_params=params(),
        cost_estimate=pl.CostEstimate(
            flops=2 * pairs * slots * (slots + 2 * NS) * width,
            bytes_accessed=2 * pairs * slots * slots,
            transcendentals=0,
        ),
        name="scan",
    )(*x, *weights, gain)
    return z, state


def out_kernel(kind, heads, counted, others, place_ref, *refs):
    refs = list(refs)

    def take(count):
        got = refs[:count]
        del refs[:count]
        return got

    z_refs, w_refs = take(EXPERTS * heads), take(EXPERTS * heads)
    inverse_ref = take(1)[0] if counted else None
    squares_refs = take(1 + others) if kind == "finish" else None
    part_refs = take(others) if kind == "finish" else None
    out_ref = take(1)[0]
    rows, width = z_refs[0].shape
    if counted:

        @pl.when(pl.program_id(0) == 0)
        def _():
            squares = jnp.zeros((rows, 1), f32)
            for q in range(EXPERTS):
                for h in range(heads):
                    z = z_refs[q * heads + h][...].astype(f32)
                    z = z * inverse_ref[(place_ref[1] ^ q) * heads + h]
                    squares = squares + jnp.sum(z * z, axis=1, keepdims=True)
            refs[0][...] = squares

    group = max(1, 256 // width) if width % 128 == 0 else 1
    total = None
    for i in range(0, EXPERTS * heads, group):
        z = [r[...] for r in z_refs[i : i + group]]
        w = [r[...] for r in w_refs[i : i + group]]
        z = jnp.concatenate(z, axis=1) if group > 1 else z[0]
        w = jnp.concatenate(w, axis=0) if group > 1 else w[0]
        part = jnp.dot(z, w, preferred_element_type=f32)
        total = part if total is None else total + part
    if kind == "finish":
        squares = sum(r[...] for r in squares_refs)
        for part in part_refs:
            total = total + part[...].astype(f32)
        out_ref[...] = (total * lax.rsqrt(squares / INNER + 1e-05)).astype(bf16)
    else:
        out_ref[0] = total.astype(bf16)


def out_projection(kind, chunk, *, place, z, w_out, inverse=None, squares=(), parts=()):
    heads = len(z[0])
    rows, width = z[0][0].shape
    slices = INNER // w_out.shape[0]
    slice_width = w_out.shape[1] // slices
    part = slice_width // CHUNKS
    count, first = (slices - 1, 1) if kind == "send" else (1, 0)
    tile = min(512, part)
    tiles = part // tile
    whole = slice_width // tile
    offset = chunk * tiles

    def w_spec(q, h):
        return pl.BlockSpec(
            (width, tile),
            lambda n, place_ref: (
                (place_ref[1] ^ q) * heads + h,
                (place_ref[0] + first + n // tiles) % slices * whole + offset + n % tiles,
            ),
        )

    def fixed(*dims):
        return pl.BlockSpec(dims, lambda n, place_ref: (0,) * len(dims))

    pieces = [(q, h) for q in range(EXPERTS) for h in range(heads)]
    operands = [z[q][h] for q, h in pieces] + [w_out] * len(pieces)
    specs = [fixed(rows, width)] * len(pieces) + [w_spec(q, h) for q, h in pieces]
    if inverse is not None:
        operands.append(inverse)
        specs.append(fixed(*inverse.shape))
    operands += [*squares, *parts]
    specs += [fixed(rows, 1)] * len(squares)
    specs += [pl.BlockSpec((rows, tile), lambda n, place_ref: (0, n))] * len(parts)
    if kind == "finish":
        out_shape = [jax.ShapeDtypeStruct((rows, part), bf16)]
        out_specs = [pl.BlockSpec((rows, tile), lambda n, place_ref: (0, n))]
    else:
        out_shape = [jax.ShapeDtypeStruct((count, rows, part), bf16)]
        out_specs = [
            pl.BlockSpec((1, rows, tile), lambda n, place_ref: (n // tiles, 0, n % tiles))
        ]
    if inverse is not None:
        out_shape.append(jax.ShapeDtypeStruct((rows, 1), f32))
        out_specs.append(fixed(rows, 1))
    return pl.pallas_call(
        functools.partial(out_kernel, kind, heads, inverse is not None, len(parts)),
        out_shape=out_shape,
        grid_spec=pltpu.PrefetchScalarGridSpec(
            num_scalar_prefetch=1, grid=(count * tiles,), in_specs=specs, out_specs=out_specs
        ),
        compiler_params=params(),
        cost_estimate=pl.CostEstimate(
            flops=2 * rows * w_out.shape[0] * count * part,
            bytes_accessed=2 * w_out.shape[0] * count * part + 2 * rows * count * part,
            transcendentals=0,
        ),
        name="out_" + kind,
    )(place, *operands)


def collect_kernel(slices, ids_ref, *refs):
    chunk_refs, out_ref = refs[:-1], refs[-1]
    count, part = chunk_refs[0].shape
    rows = ids_ref.shape[1]
    depth = part * len(chunk_refs)
    step = min(512, part)
    ids, slot = route(ids_ref[...])
    at = ids[:, :1] * (slices * CAP) + slot
    lane = iota((rows, count), 1).astype(f32)
    for s in range(slices):
        pick = mask(at + s * CAP == lane)
        for k, rows_ref in enumerate(chunk_refs):
            for c in range(0, part, step):
                start = s * depth + k * part + c
                out_ref[:, start : start + step] = jnp.dot(
                    pick, rows_ref[:, c : c + step], preferred_element_type=f32
                ).astype(bf16)


def collect(ids_row, chunks, slices):
    width = sum(c.shape[1] for c in chunks) * slices
    return pl.pallas_call(
        functools.partial(collect_kernel, slices),
        out_shape=jax.ShapeDtypeStruct((ids_row.shape[1], width), bf16),
        compiler_params=params(),
        name="collect",
    )(ids_row, *chunks)


def turn(a, n, slices, r):
    return lax.ppermute(
        a, "expert", [(d, d // slices * slices + (d + r) % slices) for d in range(n)]
    )


def swap(a, groups=None):
    return lax.all_to_all(
        a, "expert", split_axis=0, concat_axis=0, axis_index_groups=groups, tiled=True
    )


def across(a, q, n, slices):
    pairs = [(d, (d // slices ^ q) * slices + d % slices) for d in range(n)]
    return lax.ppermute(a, "expert", pairs)


def exchange(arrays, n, slices):
    out = list(arrays)
    for q in reversed(range(1, EXPERTS)):
        out[q] = across(arrays[q], q, n, slices)
    return out


def shards(
    tokens, w_in, w_out, w_bcd, dt_bias, decay_rate, skip_gain, norm_gain, expert_ids, decode_heads
):
    n = lax.axis_size("expert")
    slices = n // EXPERTS
    in_dev = w_in.shape[2]
    units = in_dev // EXPERTS
    width = min(HEADDIM, units)
    heads = units // width
    me = lax.axis_index("expert")
    chip = (me // slices).astype(jnp.int32)
    place = jnp.stack([(me % slices).astype(jnp.int32), chip])
    start = place[0] * in_dev + chip * units
    ids_row = expert_ids.reshape(1, -1)
    w_in, w_out = w_in[0], w_out[0]

    pack, outgoing = dispatch(dt_bias, ids_row, tokens, w_bcd.T, slices)
    landed = swap(outgoing)
    pack = lax.all_gather(pack, "expert", axis=0, tiled=True)
    own_heads = start // HEADDIM + jnp.arange(heads, dtype=jnp.int32)
    weights = prepare(place, own_heads, decay_rate, skip_gain, pack)

    pieces = [landed] + [turn(landed, n, slices, r) for r in range(1, slices)]
    inner = [None] * EXPERTS
    for order in ((7,), (6, 5), (4, 3), (2, 1), (0,)):
        if order == (0,):
            pieces, weights = lax.optimization_barrier((pieces, weights))
        for q, a in zip(order, in_projection(place, pieces, w_in, units, order)):
            inner[q] = a
    x = exchange(inner, n, slices)

    gain = lax.dynamic_slice(norm_gain, (start,), (units,))
    z, states = [], []
    for h in range(heads):
        rows, state = scan(x, weights, gain[h * width : (h + 1) * width].reshape(1, width), h)
        z.append(exchange(rows, n, slices))
        states.append(state)
    z = [[z[h][q] for h in range(heads)] for q in range(EXPERTS)]
    states = lax.all_gather(jnp.stack(states), "expert", axis=0, tiled=False)

    inverse = 1.0 / lax.dynamic_slice(norm_gain, (place[0] * in_dev,), (in_dev,))
    inverse = inverse.reshape(in_dev // width, 1, width)
    project = functools.partial(out_projection, place=place, z=z, w_out=w_out)
    sent = []
    for k in range(CHUNKS):
        got = project("send", k, inverse=inverse if k == 0 else None)
        if k == 0:
            squares = [got[1]] + [turn(got[1], n, slices, r) for r in range(1, slices)]
        sent.append([turn(got[0][r - 1], n, slices, r) for r in range(1, slices)])
    back = []
    for k in range(CHUNKS):
        [done] = project("finish", k, squares=squares, parts=sent[k])
        back.append(swap(done))
    mixed = collect(ids_row, back, slices)

    want = decode_heads[0] * HEADDIM
    within = want % in_dev // width
    states = states.reshape(EXPERTS, slices, heads, NS, width)
    chosen = lax.dynamic_slice(
        states,
        (within // heads, want // in_dev, within % heads, 0, 0),
        (HEADDIM // width, 1, 1, NS, width),
    )
    chosen = chosen.reshape(HEADDIM // width, NS, width).transpose(0, 2, 1)
    return (mixed, chosen.reshape(1, HEADDIM * NS))


def solution(mesh):
    in_specs = (
        P(("groups", "expert"), None),
        P("expert", None, None),
        P("expert", None, None),
        P(),
        P(),
        P(),
        P(),
        P(),
        P(("groups", "expert"), None),
        P("expert"),
    )
    out_specs = (P(("groups", "expert"), None), P(("groups", "expert"), None))
    return jax.shard_map(shards, mesh=mesh, in_specs=in_specs, out_specs=out_specs, check_vma=False)
```

```python
import functools

import jax
import jax.numpy as jnp
from jax import lax
from jax.experimental import pallas as pl
from jax.experimental.pallas import tpu as pltpu
from jax.sharding import PartitionSpec as P

INNER = 4096
HEADDIM = 128
HEADS = 32
NS = 64
EXPERTS = 8
CAP = 24
PAIR = 256
PACK = 256
CHUNKS = 2
VMEM_BYTES = 48 * 1024 * 1024

f32 = jnp.float32
bf16 = jnp.bfloat16


def params():
    return pltpu.CompilerParams(vmem_limit_bytes=VMEM_BYTES)


def mask(condition):
    return condition.astype(f32).astype(bf16)


def iota(shape, dim):
    return lax.broadcasted_iota(jnp.int32, shape, dim)


def route(ids_row):
    rows = ids_row.shape[1]
    ids = jnp.broadcast_to(ids_row.astype(f32), (rows, rows)).T
    onehot = (ids == iota((rows, rows), 1).astype(f32)).astype(f32)
    lower = mask(iota((rows, rows), 1) < iota((rows, rows), 0))
    before = jnp.dot(lower, onehot.astype(bf16), preferred_element_type=f32)
    return ids, jnp.sum(before * onehot, axis=1, keepdims=True)


def fetched(refs, buffers, sems):
    copies = [
        pltpu.make_async_copy(ref, buffer, sems.at[i])
        for i, (ref, buffer) in enumerate(zip(refs, buffers))
    ]
    for copy in copies:
        copy.start()
    for copy in copies:
        copy.wait()


def fetching_call(kernel, operands, out_shape, name):
    buffers = [pltpu.VMEM(a.shape, a.dtype) for a in operands]
    return pl.pallas_call(
        kernel,
        out_shape=out_shape,
        in_specs=[pl.BlockSpec(memory_space=pltpu.HBM)] * len(operands),
        scratch_shapes=[*buffers, pltpu.SemaphoreType.DMA((len(operands),))],
        compiler_params=params(),
        name=name,
    )(*operands)


def dispatch_kernel(slices, *refs):
    pack_ref, out_ref = refs[4:6]
    bias_ref, ids_ref, tok_ref, bcd_ref, sems = refs[6:]
    fetched(refs[:4], refs[6:10], sems)
    rows, width = tok_ref.shape
    depth = width // slices
    ids, slot = route(ids_ref[...])
    pick = mask(ids[:, :1] * CAP + slot == iota((rows, EXPERTS * CAP), 1).astype(f32))
    step = min(512, depth)
    for c in range(0, depth, step):
        got = [
            lax.dot_general(
                pick,
                tok_ref[:, s * depth + c : s * depth + c + step],
                (((0,), (0,)), ((), ())),
                preferred_element_type=f32,
            )
            for s in range(slices)
        ]
        for e in range(EXPERTS):
            piece = jnp.concatenate([g[e * CAP : (e + 1) * CAP] for g in got], axis=0)
            out_ref[e * slices * CAP : (e + 1) * slices * CAP, c : c + step] = piece.astype(bf16)

    across = (((1,), (1,)), ((), ()))
    tok = tok_ref[...]
    pack_ref[:, : 2 * NS] = lax.dot_general(
        tok, bcd_ref[: 2 * NS, :], across, preferred_element_type=f32
    ).astype(bf16)
    steps = bcd_ref[2 * NS : 2 * NS + HEADS, :]
    raw = lax.dot_general(
        tok, jnp.concatenate([steps] * 4, axis=0), across, preferred_element_type=f32
    )
    spread = (iota((HEADS, 128), 1) % HEADS == iota((HEADS, 128), 0)).astype(f32)
    raw = raw + jnp.dot(
        bias_ref[...], spread, precision=lax.Precision.HIGHEST, preferred_element_type=f32
    )
    steps_dt = jnp.maximum(raw, 0.0) + jnp.log1p(jnp.exp(-jnp.abs(raw)))
    coarse = steps_dt.astype(bf16).astype(f32)
    lane = iota((rows, 128), 1)
    side = jnp.where(lane < HEADS, coarse, steps_dt - coarse)
    side = jnp.where(lane == 2 * HEADS, ids, jnp.where(lane == 2 * HEADS + 1, slot, side))
    pack_ref[:, 2 * NS :] = jnp.where(lane < 2 * HEADS + 2, side, 0.0).astype(bf16)


def dispatch(bias, ids_row, tokens, bcd, slices):
    rows, width = tokens.shape
    return fetching_call(
        functools.partial(dispatch_kernel, slices),
        (bias.reshape(1, -1), ids_row, tokens, bcd),
        (
            jax.ShapeDtypeStruct((rows, PACK), bf16),
            jax.ShapeDtypeStruct((EXPERTS * slices * CAP, width // slices), bf16),
        ),
        "dispatch",
    )


def in_kernel(count, shares, turns, place_ref, *refs):
    rows_refs, w_refs, out_refs = refs[:count], refs[count : 2 * count], refs[2 * count :]
    total = None
    for r in range(count):
        part = jnp.dot(rows_refs[r][...], w_refs[r][...], preferred_element_type=f32)
        total = part if total is None else total + part
    for i, q in enumerate(turns):

        @pl.when(pl.program_id(0) == i)
        def _(i=i, q=q):
            units = out_refs[i].shape[1]
            own = total[:, :units]
            for k in range(1, shares):
                at = (place_ref[1] ^ q) % shares
                own = jnp.where(at == k, total[:, k * units : (k + 1) * units], own)
            out_refs[i][...] = own.astype(bf16)


def in_projection(place, pieces, w_in, units, turns):
    slices = len(pieces)
    rows, depth = pieces[0].shape
    tile = max(128, units)
    shares = tile // units

    def w_spec(r):
        def index(i, place_ref):
            q = sum(jnp.where(i == k, t, 0) for k, t in enumerate(turns))
            return (place_ref[0] - r + slices) % slices, (place_ref[1] ^ q) // shares

        return pl.BlockSpec((depth, tile), index)

    return pl.pallas_call(
        functools.partial(in_kernel, slices, shares, turns),
        out_shape=[jax.ShapeDtypeStruct((rows, units), bf16)] * len(turns),
        grid_spec=pltpu.PrefetchScalarGridSpec(
            num_scalar_prefetch=1,
            grid=(len(turns),),
            in_specs=[pl.BlockSpec((rows, depth), lambda i, place_ref: (0, 0))] * slices
            + [w_spec(r) for r in range(slices)],
            out_specs=[pl.BlockSpec((rows, units), lambda i, place_ref: (0, 0))] * len(turns),
        ),
        compiler_params=params(),
        cost_estimate=pl.CostEstimate(
            flops=2 * rows * slices * depth * tile * len(turns),
            bytes_accessed=2 * slices * depth * (tile * len(turns) + rows),
            transcendentals=0,
        ),
        name="in_projection",
    )(place, *pieces, *([w_in] * slices))


def prep_kernel(heads, place_ref, head_ref, rate_ref, skip_ref, pack_ref, w_ref, c_ref, b_ref, a_ref):
    pack = pack_ref[...]
    row = iota((128, PACK), 0)
    lane = iota((128, PACK), 1)
    side = lane - 2 * NS - 2 * HEADS
    choose = ((row == heads) & (side == 0)) | ((row == heads + 1) & (side == 1))
    choose = choose.astype(f32)
    rate = jnp.zeros((128, PAIR), f32)
    for h in range(heads):
        at = lane - 2 * NS - head_ref[h]
        choose = jnp.where((row == h) & ((at == 0) | (at == HEADS)), 1.0, choose)
        rate = jnp.where(iota((128, PAIR), 0) == h, rate_ref[head_ref[h]], rate)
    across = lax.dot_general(
        choose.astype(bf16), pack, (((1,), (1,)), ((), ())), preferred_element_type=f32
    )
    upto = iota((PAIR, PAIR), 0)
    now = iota((PAIR, PAIR), 1)
    running = jnp.dot(
        -across * rate,
        (upto <= now).astype(f32),
        precision=lax.Precision.HIGHEST,
        preferred_element_type=f32,
    )
    second = iota((1, PAIR), 1) >= PAIR // 2
    turn_of = across[heads : heads + 1].astype(jnp.int32) ^ place_ref[1]
    column = turn_of * (2 * CAP) + across[heads + 1 : heads + 2].astype(jnp.int32)
    column = column + jnp.where(second, CAP, 0)
    slots = 2 * CAP * EXPERTS
    place_t = mask(iota((slots, PAIR), 0) == column)
    down = running.T
    b_rows = pack[:, :NS]
    c_rows = pack[:, NS : 2 * NS]
    scores = lax.dot_general(
        c_rows, b_rows, (((1,), (1,)), ((), ())), preferred_element_type=f32
    )
    causal = upto >= now
    diagonal = upto == now
    b_cols = b_rows.astype(f32).T
    c_wide = c_rows.astype(f32)
    for h in range(heads):
        run_row = running[h : h + 1]
        run_col = down[:, h : h + 1]
        dt_row = across[h : h + 1]
        last = run_row[:, PAIR - 1 : PAIR]
        gap = jnp.where(causal, run_col - run_row, 0.0)
        weights = jnp.where(causal, jnp.exp(gap) * scores * dt_row, 0.0)
        weights = weights + jnp.where(diagonal, skip_ref[head_ref[h]], 0.0)
        half = jnp.dot(place_t, weights.astype(bf16), preferred_element_type=f32).astype(bf16)
        w_ref[h, 0] = lax.dot_general(
            half, place_t, (((1,), (1,)), ((), ())), preferred_element_type=f32
        ).astype(bf16)
        c_now = (c_wide * jnp.exp(run_col)).astype(bf16)
        c_ref[h, 0] = jnp.dot(place_t, c_now, preferred_element_type=f32).astype(bf16)
        b_now = (b_cols * (jnp.exp(last - run_row) * dt_row)).astype(bf16)
        b_ref[h, 0] = lax.dot_general(
            b_now, place_t, (((1,), (1,)), ((), ())), preferred_element_type=f32
        ).astype(bf16)
        a_ref[h, 0] = jnp.broadcast_to(jnp.exp(last), (8, 128))


def prepare(place, own_heads, rate, skip, pack):
    heads = own_heads.shape[0]
    pairs = pack.shape[0] // PAIR
    slots = 2 * CAP * EXPERTS
    smem = pl.BlockSpec(memory_space=pltpu.SMEM)

    def block(*dims):
        return pl.BlockSpec((heads, 1, *dims), lambda p: (0, p, 0, 0))

    return pl.pallas_call(
        functools.partial(prep_kernel, heads),
        out_shape=(
            jax.ShapeDtypeStruct((heads, pairs, slots, slots), bf16),
            jax.ShapeDtypeStruct((heads, pairs, slots, NS), bf16),
            jax.ShapeDtypeStruct((heads, pairs, NS, slots), bf16),
            jax.ShapeDtypeStruct((heads, pairs, 8, 128), f32),
        ),
        grid=(pairs,),
        in_specs=[smem, smem, smem, smem, pl.BlockSpec((PAIR, PACK), lambda p: (p, 0))],
        out_specs=(block(slots, slots), block(slots, NS), block(NS, slots), block(8, 128)),
        compiler_params=params(),
        cost_estimate=pl.CostEstimate(
            flops=4 * heads * pairs * slots * slots * PAIR,
            bytes_accessed=2 * heads * pairs * slots * slots,
            transcendentals=heads * pairs * PAIR * PAIR,
        ),
        name="scan_weights",
    )(place, own_heads, rate, skip, pack)


def scan_kernel(*refs):
    x_refs, refs = refs[:EXPERTS], refs[EXPERTS:]
    w_ref, c_ref, b_ref, a_ref, gain_ref = refs[:5]
    out_refs, last_ref, state = refs[5 : 5 + EXPERTS], refs[-2], refs[-1]

    @pl.when(pl.program_id(0) == 0)
    def _():
        state[...] = jnp.zeros_like(state)

    rows = 2 * CAP
    now = state[...]
    for i in range(w_ref.shape[1]):
        at = slice(i * rows, (i + 1) * rows)
        x = jnp.concatenate([x_ref[at, :] for x_ref in x_refs], axis=0)
        y = jnp.dot(w_ref[0, i], x, preferred_element_type=f32) + jnp.dot(
            c_ref[0, i], now.astype(bf16), preferred_element_type=f32
        )
        now = now * a_ref[0, i, 0:1, 0:1] + jnp.dot(
            b_ref[0, i], x, preferred_element_type=f32
        )
        z = (y * gain_ref[...]).astype(bf16)
        for q in range(EXPERTS):
            out_refs[q][at, :] = z[q * rows : (q + 1) * rows]
    state[...] = now
    last_ref[...] = now


def scan(x, weights, gain, h):
    rows = x[0].shape[0]
    width = gain.shape[1]
    pairs = rows // (2 * CAP)
    step = 2
    slots = 2 * CAP * EXPERTS

    def block(*dims):
        return pl.BlockSpec((1, step, *dims), lambda p: (h, p, 0, 0))

    *z, state = pl.pallas_call(
        scan_kernel,
        out_shape=[jax.ShapeDtypeStruct((rows, width), bf16)] * EXPERTS
        + [jax.ShapeDtypeStruct((NS, width), f32)],
        grid=(pairs // step,),
        in_specs=[pl.BlockSpec((2 * CAP * step, width), lambda p: (p, h))] * EXPERTS
        + [
            block(slots, slots),
            block(slots, NS),
            block(NS, slots),
            block(8, 128),
            pl.BlockSpec((1, width), lambda p: (0, 0)),
        ],
        out_specs=[pl.BlockSpec((2 * CAP * step, width), lambda p: (p, 0))] * EXPERTS
        + [pl.BlockSpec((NS, width), lambda p: (0, 0))],
        scratch_shapes=[pltpu.VMEM((NS, width), f32)],
        compiler_params=pltpu.CompilerParams(vmem_limit_bytes=VMEM_BYTES // 2),
        cost_estimate=pl.CostEstimate(
            flops=2 * pairs * slots * (slots + 2 * NS) * width,
            bytes_accessed=2 * pairs * slots * slots,
            transcendentals=0,
        ),
        name="scan",
    )(*x, *weights, gain)
    return z, state


def out_kernel(kind, heads, counted, others, place_ref, *refs):
    refs = list(refs)

    def take(count):
        got = refs[:count]
        del refs[:count]
        return got

    z_refs, [w_ref] = take(EXPERTS * heads), take(1)
    inverse_ref = take(1)[0] if counted else None
    squares_refs = take(1 + others) if kind == "finish" else None
    part_refs = take(others) if kind == "finish" else None
    out_ref = take(1)[0]
    rows, width = z_refs[0].shape
    if counted:

        @pl.when(pl.program_id(0) == 0)
        def _():
            squares = jnp.zeros((rows, 1), f32)
            for q in range(EXPERTS):
                for h in range(heads):
                    z = z_refs[q * heads + h][...].astype(f32)
                    z = z * inverse_ref[(place_ref[1] ^ q) * heads + h]
                    squares = squares + jnp.sum(z * z, axis=1, keepdims=True)
            refs[0][...] = squares

    units = heads * width
    total = None
    for q in range(EXPERTS):
        z = [r[...] for r in z_refs[q * heads : (q + 1) * heads]]
        z = jnp.concatenate(z, axis=1) if heads > 1 else z[0]
        w = w_ref[pl.ds(pl.multiple_of((place_ref[1] ^ q) * units, units), units), :]
        part = jnp.dot(z, w, preferred_element_type=f32)
        total = part if total is None else total + part
    if kind == "finish":
        squares = sum(r[...] for r in squares_refs)
        for part in part_refs:
            total = total + part[...].astype(f32)
        out_ref[...] = (total * lax.rsqrt(squares / INNER + 1e-05)).astype(bf16)
    else:
        out_ref[0] = total.astype(bf16)


def out_projection(kind, chunk, *, place, z, w_out, inverse=None, squares=(), parts=()):
    heads = len(z[0])
    rows, width = z[0][0].shape
    slices = INNER // w_out.shape[0]
    slice_width = w_out.shape[1] // slices
    part = slice_width // CHUNKS
    count, first = (slices - 1, 1) if kind == "send" else (1, 0)
    tile = min(512, part)
    tiles = part // tile
    whole = slice_width // tile
    offset = chunk * tiles

    def column(n, place_ref):
        return (place_ref[0] + first + n // tiles) % slices * whole + offset + n % tiles

    def fixed(*dims):
        return pl.BlockSpec(dims, lambda n, place_ref: (0,) * len(dims))

    pieces = [(q, h) for q in range(EXPERTS) for h in range(heads)]
    operands = [z[q][h] for q, h in pieces] + [w_out]
    specs = [fixed(rows, width)] * len(pieces)
    specs.append(
        pl.BlockSpec((w_out.shape[0], tile), lambda n, place_ref: (0, column(n, place_ref)))
    )
    if inverse is not None:
        operands.append(inverse)
        specs.append(fixed(*inverse.shape))
    operands += [*squares, *parts]
    specs += [fixed(rows, 1)] * len(squares)
    specs += [pl.BlockSpec((rows, tile), lambda n, place_ref: (0, n))] * len(parts)
    if kind == "finish":
        out_shape = [jax.ShapeDtypeStruct((rows, part), bf16)]
        out_specs = [pl.BlockSpec((rows, tile), lambda n, place_ref: (0, n))]
    else:
        out_shape = [jax.ShapeDtypeStruct((count, rows, part), bf16)]
        out_specs = [
            pl.BlockSpec((1, rows, tile), lambda n, place_ref: (n // tiles, 0, n % tiles))
        ]
    if inverse is not None:
        out_shape.append(jax.ShapeDtypeStruct((rows, 1), f32))
        out_specs.append(fixed(rows, 1))
    return pl.pallas_call(
        functools.partial(out_kernel, kind, heads, inverse is not None, len(parts)),
        out_shape=out_shape,
        grid_spec=pltpu.PrefetchScalarGridSpec(
            num_scalar_prefetch=1, grid=(count * tiles,), in_specs=specs, out_specs=out_specs
        ),
        compiler_params=params(),
        cost_estimate=pl.CostEstimate(
            flops=2 * rows * w_out.shape[0] * count * part,
            bytes_accessed=2 * w_out.shape[0] * count * part + 2 * rows * count * part,
            transcendentals=0,
        ),
        name="out_" + kind,
    )(place, *operands)


def collect_kernel(slices, ids_ref, *refs):
    chunk_refs, out_ref = refs[:-1], refs[-1]
    count, part = chunk_refs[0].shape
    rows = ids_ref.shape[1]
    depth = part * len(chunk_refs)
    step = min(512, part)
    ids, slot = route(ids_ref[...])
    at = ids[:, :1] * (slices * CAP) + slot
    lane = iota((rows, count), 1).astype(f32)
    for s in range(slices):
        pick = mask(at + s * CAP == lane)
        for k, rows_ref in enumerate(chunk_refs):
            for c in range(0, part, step):
                start = s * depth + k * part + c
                out_ref[:, start : start + step] = jnp.dot(
                    pick, rows_ref[:, c : c + step], preferred_element_type=f32
                ).astype(bf16)


def collect(ids_row, chunks, slices):
    width = sum(c.shape[1] for c in chunks) * slices
    return pl.pallas_call(
        functools.partial(collect_kernel, slices),
        out_shape=jax.ShapeDtypeStruct((ids_row.shape[1], width), bf16),
        compiler_params=params(),
        name="collect",
    )(ids_row, *chunks)


def turn(a, n, slices, r):
    return lax.ppermute(
        a, "expert", [(d, d // slices * slices + (d + r) % slices) for d in range(n)]
    )


def swap(a, groups=None):
    return lax.all_to_all(
        a, "expert", split_axis=0, concat_axis=0, axis_index_groups=groups, tiled=True
    )


def across(a, q, n, slices):
    pairs = [(d, (d // slices ^ q) * slices + d % slices) for d in range(n)]
    return lax.ppermute(a, "expert", pairs)


def exchange(arrays, n, slices):
    out = list(arrays)
    for q in reversed(range(1, EXPERTS)):
        out[q] = across(arrays[q], q, n, slices)
    return out


def shards(
    tokens, w_in, w_out, w_bcd, dt_bias, decay_rate, skip_gain, norm_gain, expert_ids, decode_heads
):
    n = lax.axis_size("expert")
    slices = n // EXPERTS
    in_dev = w_in.shape[2]
    units = in_dev // EXPERTS
    width = min(HEADDIM, units)
    heads = units // width
    me = lax.axis_index("expert")
    chip = (me // slices).astype(jnp.int32)
    place = jnp.stack([(me % slices).astype(jnp.int32), chip])
    start = place[0] * in_dev + chip * units
    ids_row = expert_ids.reshape(1, -1)
    w_in, w_out = w_in[0], w_out[0]

    pack, outgoing = dispatch(dt_bias, ids_row, tokens, w_bcd.T, slices)
    landed = swap(outgoing)
    pack = lax.all_gather(pack, "expert", axis=0, tiled=True)
    own_heads = start // HEADDIM + jnp.arange(heads, dtype=jnp.int32)

    pieces = [landed] + [turn(landed, n, slices, r) for r in range(1, slices)]
    inner = [None] * EXPERTS
    for order in ((7,), (6, 5), (4, 3), (2, 1), (0,)):
        if order == (4, 3):
            pieces, pack = lax.optimization_barrier((pieces, pack))
            weights = prepare(place, own_heads, decay_rate, skip_gain, pack)
        if order == (0,):
            pieces, weights = lax.optimization_barrier((pieces, weights))
        for q, a in zip(order, in_projection(place, pieces, w_in, units, order)):
            inner[q] = a
    x = exchange(inner, n, slices)

    gain = lax.dynamic_slice(norm_gain, (start,), (units,))
    z, states = [], []
    for h in range(heads):
        rows, state = scan(x, weights, gain[h * width : (h + 1) * width].reshape(1, width), h)
        z.append(exchange(rows, n, slices))
        states.append(state)
    z = [[z[h][q] for h in range(heads)] for q in range(EXPERTS)]
    states = lax.all_gather(jnp.stack(states), "expert", axis=0, tiled=False)

    inverse = 1.0 / lax.dynamic_slice(norm_gain, (place[0] * in_dev,), (in_dev,))
    inverse = inverse.reshape(in_dev // width, 1, width)
    project = functools.partial(out_projection, place=place, z=z, w_out=w_out)
    sent = []
    for k in range(CHUNKS):
        got = project("send", k, inverse=inverse if k == 0 else None)
        if k == 0:
            squares = [got[1]] + [turn(got[1], n, slices, r) for r in range(1, slices)]
        sent.append([turn(got[0][r - 1], n, slices, r) for r in range(1, slices)])
    back = []
    for k in range(CHUNKS):
        [done] = project("finish", k, squares=squares, parts=sent[k])
        back.append(swap(done))
    mixed = collect(ids_row, back, slices)

    want = decode_heads[0] * HEADDIM
    within = want % in_dev // width
    states = states.reshape(EXPERTS, slices, heads, NS, width)
    chosen = lax.dynamic_slice(
        states,
        (within // heads, want // in_dev, within % heads, 0, 0),
        (HEADDIM // width, 1, 1, NS, width),
    )
    chosen = chosen.reshape(HEADDIM // width, NS, width).transpose(0, 2, 1)
    return (mixed, chosen.reshape(1, HEADDIM * NS))


def solution(mesh):
    in_specs = (
        P(("groups", "expert"), None),
        P("expert", None, None),
        P("expert", None, None),
        P(),
        P(),
        P(),
        P(),
        P(),
        P(("groups", "expert"), None),
        P("expert"),
    )
    out_specs = (P(("groups", "expert"), None), P(("groups", "expert"), None))
    return jax.shard_map(shards, mesh=mesh, in_specs=in_specs, out_specs=out_specs, check_vma=False)
```

```python
import functools

import jax
import jax.numpy as jnp
from jax import lax
from jax.experimental import pallas as pl
from jax.experimental.pallas import tpu as pltpu
from jax.sharding import PartitionSpec as P

INNER = 4096
HEADDIM = 128
HEADS = 32
NS = 64
EXPERTS = 8
CAP = 24
PAIR = 256
PACK = 256
CHUNKS = 1
VMEM_BYTES = 48 * 1024 * 1024

f32 = jnp.float32
bf16 = jnp.bfloat16


def params():
    return pltpu.CompilerParams(vmem_limit_bytes=VMEM_BYTES)


def mask(condition):
    return condition.astype(f32).astype(bf16)


def iota(shape, dim):
    return lax.broadcasted_iota(jnp.int32, shape, dim)


def route(ids_row):
    rows = ids_row.shape[1]
    ids = jnp.broadcast_to(ids_row.astype(f32), (rows, rows)).T
    onehot = (ids == iota((rows, rows), 1).astype(f32)).astype(f32)
    lower = mask(iota((rows, rows), 1) < iota((rows, rows), 0))
    before = jnp.dot(lower, onehot.astype(bf16), preferred_element_type=f32)
    return ids, jnp.sum(before * onehot, axis=1, keepdims=True)


def fetched(refs, buffers, sems):
    copies = [
        pltpu.make_async_copy(ref, buffer, sems.at[i])
        for i, (ref, buffer) in enumerate(zip(refs, buffers))
    ]
    for copy in copies:
        copy.start()
    for copy in copies:
        copy.wait()


def fetching_call(kernel, operands, out_shape, name):
    buffers = [pltpu.VMEM(a.shape, a.dtype) for a in operands]
    return pl.pallas_call(
        kernel,
        out_shape=out_shape,
        in_specs=[pl.BlockSpec(memory_space=pltpu.HBM)] * len(operands),
        scratch_shapes=[*buffers, pltpu.SemaphoreType.DMA((len(operands),))],
        compiler_params=params(),
        name=name,
    )(*operands)


def dispatch_kernel(slices, *refs):
    pack_ref, out_ref = refs[3:5]
    ids_ref, tok_ref, bcd_ref, sems = refs[5:]
    fetched(refs[:3], refs[5:8], sems)
    rows, width = tok_ref.shape
    depth = width // slices
    ids, slot = route(ids_ref[...])
    pick = mask(ids[:, :1] * CAP + slot == iota((rows, EXPERTS * CAP), 1).astype(f32))
    step = min(512, depth)
    for c in range(0, depth, step):
        got = [
            lax.dot_general(
                pick,
                tok_ref[:, s * depth + c : s * depth + c + step],
                (((0,), (0,)), ((), ())),
                preferred_element_type=f32,
            )
            for s in range(slices)
        ]
        for e in range(EXPERTS):
            piece = jnp.concatenate([g[e * CAP : (e + 1) * CAP] for g in got], axis=0)
            out_ref[e * slices * CAP : (e + 1) * slices * CAP, c : c + step] = piece.astype(bf16)

    across = (((1,), (1,)), ((), ()))
    tok = tok_ref[...]
    pack_ref[:, : 2 * NS] = lax.dot_general(
        tok, bcd_ref[: 2 * NS, :], across, preferred_element_type=f32
    ).astype(bf16)
    steps = bcd_ref[2 * NS : 2 * NS + HEADS, :]
    raw = lax.dot_general(
        tok, jnp.concatenate([steps] * 4, axis=0), across, preferred_element_type=f32
    )
    coarse = raw.astype(bf16).astype(f32)
    lane = iota((rows, 128), 1)
    side = jnp.where(lane < HEADS, coarse, raw - coarse)
    side = jnp.where(lane == 2 * HEADS, ids, jnp.where(lane == 2 * HEADS + 1, slot, side))
    pack_ref[:, 2 * NS :] = jnp.where(lane < 2 * HEADS + 2, side, 0.0).astype(bf16)


def dispatch(ids_row, tokens, bcd, slices):
    rows, width = tokens.shape
    return fetching_call(
        functools.partial(dispatch_kernel, slices),
        (ids_row, tokens, bcd),
        (
            jax.ShapeDtypeStruct((rows, PACK), bf16),
            jax.ShapeDtypeStruct((EXPERTS * slices * CAP, width // slices), bf16),
        ),
        "dispatch",
    )


def in_kernel(count, shares, turns, place_ref, *refs):
    rows_refs, w_refs, out_refs = refs[:count], refs[count : 2 * count], refs[2 * count :]
    total = None
    for r in range(count):
        part = jnp.dot(rows_refs[r][...], w_refs[r][...], preferred_element_type=f32)
        total = part if total is None else total + part
    for i, q in enumerate(turns):

        @pl.when(pl.program_id(0) == i)
        def _(i=i, q=q):
            units = out_refs[i].shape[1]
            own = total[:, :units]
            for k in range(1, shares):
                at = (place_ref[1] ^ q) % shares
                own = jnp.where(at == k, total[:, k * units : (k + 1) * units], own)
            out_refs[i][...] = own.astype(bf16)


def in_projection(place, pieces, w_in, units, turns):
    slices = len(pieces)
    rows, depth = pieces[0].shape
    tile = max(128, units)
    shares = tile // units

    def w_spec(r):
        def index(i, place_ref):
            q = sum(jnp.where(i == k, t, 0) for k, t in enumerate(turns))
            return (place_ref[0] - r + slices) % slices, (place_ref[1] ^ q) // shares

        return pl.BlockSpec((depth, tile), index)

    return pl.pallas_call(
        functools.partial(in_kernel, slices, shares, turns),
        out_shape=[jax.ShapeDtypeStruct((rows, units), bf16)] * len(turns),
        grid_spec=pltpu.PrefetchScalarGridSpec(
            num_scalar_prefetch=1,
            grid=(len(turns),),
            in_specs=[pl.BlockSpec((rows, depth), lambda i, place_ref: (0, 0))] * slices
            + [w_spec(r) for r in range(slices)],
            out_specs=[pl.BlockSpec((rows, units), lambda i, place_ref: (0, 0))] * len(turns),
        ),
        compiler_params=params(),
        cost_estimate=pl.CostEstimate(
            flops=2 * rows * slices * depth * tile * len(turns),
            bytes_accessed=2 * slices * depth * (tile * len(turns) + rows),
            transcendentals=0,
        ),
        name="in_projection",
    )(place, *pieces, *([w_in] * slices))


def prep_kernel(heads, place_ref, head_ref, bias_ref, rate_ref, skip_ref, pack_ref, w_ref, c_ref, b_ref, a_ref):
    pack = pack_ref[...]
    row = iota((128, PACK), 0)
    lane = iota((128, PACK), 1)
    side = lane - 2 * NS - 2 * HEADS
    choose = ((row == heads) & (side == 0)) | ((row == heads + 1) & (side == 1))
    choose = choose.astype(f32)
    rate = bias = jnp.zeros((128, PAIR), f32)
    for h in range(heads):
        at = lane - 2 * NS - head_ref[h]
        choose = jnp.where((row == h) & ((at == 0) | (at == HEADS)), 1.0, choose)
        rate = jnp.where(iota((128, PAIR), 0) == h, rate_ref[head_ref[h]], rate)
        bias = jnp.where(iota((128, PAIR), 0) == h, bias_ref[head_ref[h]], bias)
    across = lax.dot_general(
        choose.astype(bf16), pack, (((1,), (1,)), ((), ())), preferred_element_type=f32
    )
    raw = across + bias
    steps_dt = jnp.maximum(raw, 0.0) + jnp.log1p(jnp.exp(-jnp.abs(raw)))
    upto = iota((PAIR, PAIR), 0)
    now = iota((PAIR, PAIR), 1)
    running = jnp.dot(
        -steps_dt * rate,
        (upto <= now).astype(f32),
        precision=lax.Precision.HIGHEST,
        preferred_element_type=f32,
    )
    second = iota((1, PAIR), 1) >= PAIR // 2
    turn_of = across[heads : heads + 1].astype(jnp.int32) ^ place_ref[1]
    column = turn_of * (2 * CAP) + across[heads + 1 : heads + 2].astype(jnp.int32)
    column = column + jnp.where(second, CAP, 0)
    slots = 2 * CAP * EXPERTS
    place_t = mask(iota((slots, PAIR), 0) == column)
    down = running.T
    b_rows = pack[:, :NS]
    c_rows = pack[:, NS : 2 * NS]
    scores = lax.dot_general(
        c_rows, b_rows, (((1,), (1,)), ((), ())), preferred_element_type=f32
    )
    causal = upto >= now
    diagonal = upto == now
    b_cols = b_rows.astype(f32).T
    c_wide = c_rows.astype(f32)
    for h in range(heads):
        run_row = running[h : h + 1]
        run_col = down[:, h : h + 1]
        dt_row = steps_dt[h : h + 1]
        last = run_row[:, PAIR - 1 : PAIR]
        gap = jnp.where(causal, run_col - run_row, 0.0)
        weights = jnp.where(causal, jnp.exp(gap) * scores * dt_row, 0.0)
        weights = weights + jnp.where(diagonal, skip_ref[head_ref[h]], 0.0)
        half = jnp.dot(place_t, weights.astype(bf16), preferred_element_type=f32).astype(bf16)
        w_ref[h, 0] = lax.dot_general(
            half, place_t, (((1,), (1,)), ((), ())), preferred_element_type=f32
        ).astype(bf16)
        c_now = (c_wide * jnp.exp(run_col)).astype(bf16)
        c_ref[h, 0] = jnp.dot(place_t, c_now, preferred_element_type=f32).astype(bf16)
        b_now = (b_cols * (jnp.exp(last - run_row) * dt_row)).astype(bf16)
        b_ref[h, 0] = lax.dot_general(
            b_now, place_t, (((1,), (1,)), ((), ())), preferred_element_type=f32
        ).astype(bf16)
        a_ref[h, 0] = jnp.broadcast_to(jnp.exp(last), (8, 128))


def prepare(place, own_heads, bias, rate, skip, pack):
    heads = own_heads.shape[0]
    pairs = pack.shape[0] // PAIR
    slots = 2 * CAP * EXPERTS
    smem = pl.BlockSpec(memory_space=pltpu.SMEM)

    def block(*dims):
        return pl.BlockSpec((heads, 1, *dims), lambda p: (0, p, 0, 0))

    return pl.pallas_call(
        functools.partial(prep_kernel, heads),
        out_shape=(
            jax.ShapeDtypeStruct((heads, pairs, slots, slots), bf16),
            jax.ShapeDtypeStruct((heads, pairs, slots, NS), bf16),
            jax.ShapeDtypeStruct((heads, pairs, NS, slots), bf16),
            jax.ShapeDtypeStruct((heads, pairs, 8, 128), f32),
        ),
        grid=(pairs,),
        in_specs=[smem] * 5 + [pl.BlockSpec((PAIR, PACK), lambda p: (p, 0))],
        out_specs=(block(slots, slots), block(slots, NS), block(NS, slots), block(8, 128)),
        compiler_params=params(),
        cost_estimate=pl.CostEstimate(
            flops=4 * heads * pairs * slots * slots * PAIR,
            bytes_accessed=2 * heads * pairs * slots * slots,
            transcendentals=heads * pairs * PAIR * PAIR,
        ),
        name="scan_weights",
    )(place, own_heads, bias, rate, skip, pack)


def scan_kernel(place_ref, *refs):
    x_refs, refs = refs[:EXPERTS], refs[EXPERTS:]
    w_ref, c_ref, b_ref, a_ref, gain_ref, out_ref, last_ref, state = refs

    @pl.when(pl.program_id(0) == 0)
    def _():
        state[...] = jnp.zeros_like(state)

    rows = 2 * CAP
    now = state[...]
    for i in range(w_ref.shape[1]):
        at = slice(i * rows, (i + 1) * rows)
        x = jnp.concatenate([x_ref[at, :] for x_ref in x_refs], axis=0)
        y = jnp.dot(w_ref[0, i], x, preferred_element_type=f32) + jnp.dot(
            c_ref[0, i], now.astype(bf16), preferred_element_type=f32
        )
        now = now * a_ref[0, i, 0:1, 0:1] + jnp.dot(
            b_ref[0, i], x, preferred_element_type=f32
        )
        z = (y * gain_ref[...]).astype(bf16)
        for q in range(EXPERTS):
            out_ref[place_ref[1] ^ q, at, :] = z[q * rows : (q + 1) * rows]
    state[...] = now
    last_ref[...] = now


def scan(place, x, weights, gain, h):
    rows = x[0].shape[0]
    width = gain.shape[1]
    pairs = rows // (2 * CAP)
    step = 2
    slots = 2 * CAP * EXPERTS

    def block(*dims):
        return pl.BlockSpec((1, step, *dims), lambda p, place_ref: (h, p, 0, 0))

    return pl.pallas_call(
        scan_kernel,
        out_shape=(
            jax.ShapeDtypeStruct((EXPERTS, rows, width), bf16),
            jax.ShapeDtypeStruct((NS, width), f32),
        ),
        grid_spec=pltpu.PrefetchScalarGridSpec(
            num_scalar_prefetch=1,
            grid=(pairs // step,),
            in_specs=[pl.BlockSpec((2 * CAP * step, width), lambda p, place_ref: (p, h))] * EXPERTS
            + [
                block(slots, slots),
                block(slots, NS),
                block(NS, slots),
                block(8, 128),
                pl.BlockSpec((1, width), lambda p, place_ref: (0, 0)),
            ],
            out_specs=(
                pl.BlockSpec((EXPERTS, 2 * CAP * step, width), lambda p, place_ref: (0, p, 0)),
                pl.BlockSpec((NS, width), lambda p, place_ref: (0, 0)),
            ),
            scratch_shapes=[pltpu.VMEM((NS, width), f32)],
        ),
        compiler_params=pltpu.CompilerParams(vmem_limit_bytes=VMEM_BYTES // 2),
        cost_estimate=pl.CostEstimate(
            flops=2 * pairs * slots * (slots + 2 * NS) * width,
            bytes_accessed=2 * pairs * slots * slots,
            transcendentals=0,
        ),
        name="scan",
    )(place, *x, *weights, gain)


def out_kernel(kind, heads, counted, others, place_ref, *refs):
    refs = list(refs)

    def take(count):
        got = refs[:count]
        del refs[:count]
        return got

    z_refs, [w_ref] = take(heads), take(1)
    inverse_ref = take(1)[0] if counted else None
    squares_refs = take(1 + others) if kind == "finish" else None
    part_refs = take(others) if kind == "finish" else None
    out_ref = take(1)[0]
    _, rows, width = z_refs[0].shape
    if counted:

        @pl.when(pl.program_id(0) == 0)
        def _():
            squares = jnp.zeros((rows, 1), f32)
            for j in range(EXPERTS):
                for h in range(heads):
                    z = z_refs[h][j].astype(f32) * inverse_ref[j * heads + h]
                    squares = squares + jnp.sum(z * z, axis=1, keepdims=True)
            refs[0][...] = squares

    units = heads * width
    total = None
    for j in range(EXPERTS):
        z = [r[j] for r in z_refs]
        z = jnp.concatenate(z, axis=1) if heads > 1 else z[0]
        part = jnp.dot(z, w_ref[j * units : (j + 1) * units, :], preferred_element_type=f32)
        total = part if total is None else total + part
    if kind == "finish":
        squares = sum(r[...] for r in squares_refs)
        for part in part_refs:
            total = total + part[...].astype(f32)
        out_ref[...] = (total * lax.rsqrt(squares / INNER + 1e-05)).astype(bf16)
    else:
        out_ref[0] = total.astype(bf16)


def out_projection(kind, chunk, *, place, z, w_out, inverse=None, squares=(), parts=()):
    heads = len(z)
    _, rows, width = z[0].shape
    slices = INNER // w_out.shape[0]
    slice_width = w_out.shape[1] // slices
    part = slice_width // CHUNKS
    count, first = (slices - 1, 1) if kind == "send" else (1, 0)
    tile = min(512, part)
    tiles = part // tile
    whole = slice_width // tile
    offset = chunk * tiles

    def column(n, place_ref):
        return (place_ref[0] + first + n // tiles) % slices * whole + offset + n % tiles

    def fixed(*dims):
        return pl.BlockSpec(dims, lambda n, place_ref: (0,) * len(dims))

    operands = [*z, w_out]
    specs = [fixed(*z[0].shape)] * heads
    specs.append(
        pl.BlockSpec((w_out.shape[0], tile), lambda n, place_ref: (0, column(n, place_ref)))
    )
    if inverse is not None:
        operands.append(inverse)
        specs.append(fixed(*inverse.shape))
    operands += [*squares, *parts]
    specs += [fixed(rows, 1)] * len(squares)
    specs += [pl.BlockSpec((rows, tile), lambda n, place_ref: (0, n))] * len(parts)
    if kind == "finish":
        out_shape = [jax.ShapeDtypeStruct((rows, part), bf16)]
        out_specs = [pl.BlockSpec((rows, tile), lambda n, place_ref: (0, n))]
    else:
        out_shape = [jax.ShapeDtypeStruct((count, rows, part), bf16)]
        out_specs = [
            pl.BlockSpec((1, rows, tile), lambda n, place_ref: (n // tiles, 0, n % tiles))
        ]
    if inverse is not None:
        out_shape.append(jax.ShapeDtypeStruct((rows, 1), f32))
        out_specs.append(fixed(rows, 1))
    return pl.pallas_call(
        functools.partial(out_kernel, kind, heads, inverse is not None, len(parts)),
        out_shape=out_shape,
        grid_spec=pltpu.PrefetchScalarGridSpec(
            num_scalar_prefetch=1, grid=(count * tiles,), in_specs=specs, out_specs=out_specs
        ),
        compiler_params=params(),
        cost_estimate=pl.CostEstimate(
            flops=2 * rows * w_out.shape[0] * count * part,
            bytes_accessed=2 * w_out.shape[0] * count * part + 2 * rows * count * part,
            transcendentals=0,
        ),
        name="out_" + kind,
    )(place, *operands)


def collect_kernel(slices, ids_ref, *refs):
    chunk_refs, out_ref = refs[:-1], refs[-1]
    count, part = chunk_refs[0].shape
    rows = ids_ref.shape[1]
    depth = part * len(chunk_refs)
    step = min(512, part)
    ids, slot = route(ids_ref[...])
    at = ids[:, :1] * (slices * CAP) + slot
    lane = iota((rows, count), 1).astype(f32)
    for s in range(slices):
        pick = mask(at + s * CAP == lane)
        for k, rows_ref in enumerate(chunk_refs):
            for c in range(0, part, step):
                start = s * depth + k * part + c
                out_ref[:, start : start + step] = jnp.dot(
                    pick, rows_ref[:, c : c + step], preferred_element_type=f32
                ).astype(bf16)


def collect(ids_row, chunks, slices):
    width = sum(c.shape[1] for c in chunks) * slices
    return pl.pallas_call(
        functools.partial(collect_kernel, slices),
        out_shape=jax.ShapeDtypeStruct((ids_row.shape[1], width), bf16),
        compiler_params=params(),
        name="collect",
    )(ids_row, *chunks)


def turn(a, n, slices, r):
    return lax.ppermute(
        a, "expert", [(d, d // slices * slices + (d + r) % slices) for d in range(n)]
    )


def swap(a, groups=None):
    return lax.all_to_all(
        a, "expert", split_axis=0, concat_axis=0, axis_index_groups=groups, tiled=True
    )


def across(a, q, n, slices):
    pairs = [(d, (d // slices ^ q) * slices + d % slices) for d in range(n)]
    return lax.ppermute(a, "expert", pairs)


def gathered(a, me, n):
    other = lax.ppermute(a, "expert", [(d, d ^ 1) for d in range(n)])
    first = me % 2 == 0
    pair = jnp.concatenate([jnp.where(first, a, other), jnp.where(first, other, a)], axis=0)
    groups = [list(range(k, n, 2)) for k in range(2)]
    return lax.all_gather(pair, "expert", axis=0, axis_index_groups=groups, tiled=True)


def exchange(arrays, n, slices):
    out = list(arrays)
    for q in reversed(range(1, EXPERTS)):
        out[q] = across(arrays[q], q, n, slices)
    return out


def shards(
    tokens, w_in, w_out, w_bcd, dt_bias, decay_rate, skip_gain, norm_gain, expert_ids, decode_heads
):
    n = lax.axis_size("expert")
    slices = n // EXPERTS
    in_dev = w_in.shape[2]
    units = in_dev // EXPERTS
    width = min(HEADDIM, units)
    heads = units // width
    me = lax.axis_index("expert")
    chip = (me // slices).astype(jnp.int32)
    place = jnp.stack([(me % slices).astype(jnp.int32), chip])
    start = place[0] * in_dev + chip * units
    same_slice = [[j * slices + k for j in range(EXPERTS)] for k in range(slices)]
    ids_row = expert_ids.reshape(1, -1)
    w_in, w_out = w_in[0], w_out[0]

    pack, outgoing = dispatch(ids_row, tokens, w_bcd.T, slices)
    landed = swap(outgoing)
    pack = gathered(pack, me, n)
    own_heads = start // HEADDIM + jnp.arange(heads, dtype=jnp.int32)

    pieces = [landed] + [turn(landed, n, slices, r) for r in range(1, slices)]
    inner = [None] * EXPERTS
    for order in ((7,), (6, 5), (4, 3), (2, 1), (0,)):
        if order == (4, 3):
            pieces, pack = lax.optimization_barrier((pieces, pack))
            weights = prepare(place, own_heads, dt_bias, decay_rate, skip_gain, pack)
        if order == (0,):
            pieces, weights = lax.optimization_barrier((pieces, weights))
        for q, a in zip(order, in_projection(place, pieces, w_in, units, order)):
            inner[q] = a
    x = exchange(inner, n, slices)

    gain = lax.dynamic_slice(norm_gain, (start,), (units,))
    z, states = [], []
    for h in range(heads):
        own_gain = gain[h * width : (h + 1) * width].reshape(1, width)
        rows, state = scan(place, x, weights, own_gain, h)
        z.append(swap(rows, same_slice))
        states.append(state)
    states = gathered(jnp.stack(states), me, n)

    inverse = 1.0 / lax.dynamic_slice(norm_gain, (place[0] * in_dev,), (in_dev,))
    inverse = inverse.reshape(in_dev // width, 1, width)
    project = functools.partial(out_projection, place=place, z=z, w_out=w_out)
    sent = []
    for k in range(CHUNKS):
        got = project("send", k, inverse=inverse if k == 0 else None)
        if k == 0:
            squares = [got[1]] + [turn(got[1], n, slices, r) for r in range(1, slices)]
        sent.append([turn(got[0][r - 1], n, slices, r) for r in range(1, slices)])
    back = []
    for k in range(CHUNKS):
        [done] = project("finish", k, squares=squares, parts=sent[k])
        back.append(swap(done))
    mixed = collect(ids_row, back, slices)

    want = decode_heads[0] * HEADDIM
    within = want % in_dev // width
    states = states.reshape(EXPERTS, slices, heads, NS, width)
    chosen = lax.dynamic_slice(
        states,
        (within // heads, want // in_dev, within % heads, 0, 0),
        (HEADDIM // width, 1, 1, NS, width),
    )
    chosen = chosen.reshape(HEADDIM // width, NS, width).transpose(0, 2, 1)
    return (mixed, chosen.reshape(1, HEADDIM * NS))


def solution(mesh):
    in_specs = (
        P(("groups", "expert"), None),
        P("expert", None, None),
        P("expert", None, None),
        P(),
        P(),
        P(),
        P(),
        P(),
        P(("groups", "expert"), None),
        P("expert"),
    )
    out_specs = (P(("groups", "expert"), None), P(("groups", "expert"), None))
    return jax.shard_map(shards, mesh=mesh, in_specs=in_specs, out_specs=out_specs, check_vma=False)
```

```python
import functools

import jax
import jax.numpy as jnp
from jax import lax
from jax.experimental import pallas as pl
from jax.experimental.pallas import tpu as pltpu
from jax.sharding import PartitionSpec as P

INNER = 4096
HEADDIM = 128
HEADS = 32
NS = 64
EXPERTS = 8
CAP = 24
PAIR = 256
PACK = 256
CHUNKS = 1
VMEM_BYTES = 48 * 1024 * 1024

f32 = jnp.float32
bf16 = jnp.bfloat16


def params():
    return pltpu.CompilerParams(vmem_limit_bytes=VMEM_BYTES)


def mask(condition):
    return condition.astype(f32).astype(bf16)


def iota(shape, dim):
    return lax.broadcasted_iota(jnp.int32, shape, dim)


def route(ids_row):
    rows = ids_row.shape[1]
    ids = jnp.broadcast_to(ids_row.astype(f32), (rows, rows)).T
    onehot = (ids == iota((rows, rows), 1).astype(f32)).astype(f32)
    lower = mask(iota((rows, rows), 1) < iota((rows, rows), 0))
    before = jnp.dot(lower, onehot.astype(bf16), preferred_element_type=f32)
    return ids, jnp.sum(before * onehot, axis=1, keepdims=True)


def fetched(refs, buffers, sems):
    copies = [
        pltpu.make_async_copy(ref, buffer, sems.at[i])
        for i, (ref, buffer) in enumerate(zip(refs, buffers))
    ]
    for copy in copies:
        copy.start()
    for copy in copies:
        copy.wait()


def fetching_call(kernel, operands, out_shape, name):
    buffers = [pltpu.VMEM(a.shape, a.dtype) for a in operands]
    return pl.pallas_call(
        kernel,
        out_shape=out_shape,
        in_specs=[pl.BlockSpec(memory_space=pltpu.HBM)] * len(operands),
        scratch_shapes=[*buffers, pltpu.SemaphoreType.DMA((len(operands),))],
        compiler_params=params(),
        name=name,
    )(*operands)


def dispatch_kernel(slices, *refs):
    pack_ref, out_ref = refs[3:5]
    ids_ref, tok_ref, bcd_ref, sems = refs[5:]
    fetched(refs[:3], refs[5:8], sems)
    rows, width = tok_ref.shape
    depth = width // slices
    ids, slot = route(ids_ref[...])
    pick = mask(ids[:, :1] * CAP + slot == iota((rows, EXPERTS * CAP), 1).astype(f32))
    step = min(512, depth)
    for c in range(0, depth, step):
        got = [
            lax.dot_general(
                pick,
                tok_ref[:, s * depth + c : s * depth + c + step],
                (((0,), (0,)), ((), ())),
                preferred_element_type=f32,
            )
            for s in range(slices)
        ]
        for e in range(EXPERTS):
            piece = jnp.concatenate([g[e * CAP : (e + 1) * CAP] for g in got], axis=0)
            out_ref[e * slices * CAP : (e + 1) * slices * CAP, c : c + step] = piece.astype(bf16)

    across = (((1,), (1,)), ((), ()))
    tok = tok_ref[...]
    pack_ref[:, : 2 * NS] = lax.dot_general(
        tok, bcd_ref[: 2 * NS, :], across, preferred_element_type=f32
    ).astype(bf16)
    steps = bcd_ref[2 * NS : 2 * NS + HEADS, :]
    raw = lax.dot_general(
        tok, jnp.concatenate([steps] * 4, axis=0), across, preferred_element_type=f32
    )
    coarse = raw.astype(bf16).astype(f32)
    lane = iota((rows, 128), 1)
    side = jnp.where(lane < HEADS, coarse, raw - coarse)
    side = jnp.where(lane == 2 * HEADS, ids, jnp.where(lane == 2 * HEADS + 1, slot, side))
    pack_ref[:, 2 * NS :] = jnp.where(lane < 2 * HEADS + 2, side, 0.0).astype(bf16)


def dispatch(ids_row, tokens, bcd, slices):
    rows, width = tokens.shape
    return fetching_call(
        functools.partial(dispatch_kernel, slices),
        (ids_row, tokens, bcd),
        (
            jax.ShapeDtypeStruct((rows, PACK), bf16),
            jax.ShapeDtypeStruct((EXPERTS * slices * CAP, width // slices), bf16),
        ),
        "dispatch",
    )


def in_kernel(count, shares, turns, place_ref, *refs):
    rows_refs, w_refs, out_refs = refs[:count], refs[count : 2 * count], refs[2 * count :]
    total = None
    for r in range(count):
        part = jnp.dot(rows_refs[r][...], w_refs[r][...], preferred_element_type=f32)
        total = part if total is None else total + part
    for i, q in enumerate(turns):

        @pl.when(pl.program_id(0) == i)
        def _(i=i, q=q):
            units = out_refs[i].shape[1]
            own = total[:, :units]
            for k in range(1, shares):
                at = (place_ref[1] ^ q) % shares
                own = jnp.where(at == k, total[:, k * units : (k + 1) * units], own)
            out_refs[i][...] = own.astype(bf16)


def in_projection(place, pieces, w_in, units, turns):
    slices = len(pieces)
    rows, depth = pieces[0].shape
    tile = max(128, units)
    shares = tile // units

    def w_spec(r):
        def index(i, place_ref):
            q = sum(jnp.where(i == k, t, 0) for k, t in enumerate(turns))
            return (place_ref[0] - r + slices) % slices, (place_ref[1] ^ q) // shares

        return pl.BlockSpec((depth, tile), index)

    return pl.pallas_call(
        functools.partial(in_kernel, slices, shares, turns),
        out_shape=[jax.ShapeDtypeStruct((rows, units), bf16)] * len(turns),
        grid_spec=pltpu.PrefetchScalarGridSpec(
            num_scalar_prefetch=1,
            grid=(len(turns),),
            in_specs=[pl.BlockSpec((rows, depth), lambda i, place_ref: (0, 0))] * slices
            + [w_spec(r) for r in range(slices)],
            out_specs=[pl.BlockSpec((rows, units), lambda i, place_ref: (0, 0))] * len(turns),
        ),
        compiler_params=params(),
        cost_estimate=pl.CostEstimate(flops=rows, bytes_accessed=rows, transcendentals=0),
        name="in_projection",
    )(place, *pieces, *([w_in] * slices))


def prep_kernel(heads, place_ref, head_ref, bias_ref, rate_ref, skip_ref, pack_ref, w_ref, c_ref, b_ref, a_ref):
    pack = pack_ref[...]
    row = iota((128, PACK), 0)
    lane = iota((128, PACK), 1)
    side = lane - 2 * NS - 2 * HEADS
    choose = ((row == heads) & (side == 0)) | ((row == heads + 1) & (side == 1))
    choose = choose.astype(f32)
    rate = bias = jnp.zeros((128, PAIR), f32)
    for h in range(heads):
        at = lane - 2 * NS - head_ref[h]
        choose = jnp.where((row == h) & ((at == 0) | (at == HEADS)), 1.0, choose)
        rate = jnp.where(iota((128, PAIR), 0) == h, rate_ref[head_ref[h]], rate)
        bias = jnp.where(iota((128, PAIR), 0) == h, bias_ref[head_ref[h]], bias)
    across = lax.dot_general(
        choose.astype(bf16), pack, (((1,), (1,)), ((), ())), preferred_element_type=f32
    )
    raw = across + bias
    steps_dt = jnp.maximum(raw, 0.0) + jnp.log1p(jnp.exp(-jnp.abs(raw)))
    upto = iota((PAIR, PAIR), 0)
    now = iota((PAIR, PAIR), 1)
    running = jnp.dot(
        -steps_dt * rate,
        (upto <= now).astype(f32),
        precision=lax.Precision.HIGHEST,
        preferred_element_type=f32,
    )
    second = iota((1, PAIR), 1) >= PAIR // 2
    turn_of = across[heads : heads + 1].astype(jnp.int32) ^ place_ref[1]
    column = turn_of * (2 * CAP) + across[heads + 1 : heads + 2].astype(jnp.int32)
    column = column + jnp.where(second, CAP, 0)
    slots = 2 * CAP * EXPERTS
    place_t = mask(iota((slots, PAIR), 0) == column)
    down = running.T
    b_rows = pack[:, :NS]
    c_rows = pack[:, NS : 2 * NS]
    scores = lax.dot_general(
        c_rows, b_rows, (((1,), (1,)), ((), ())), preferred_element_type=f32
    )
    causal = upto >= now
    diagonal = upto == now
    b_cols = b_rows.astype(f32).T
    c_wide = c_rows.astype(f32)
    for h in range(heads):
        run_row = running[h : h + 1]
        run_col = down[:, h : h + 1]
        dt_row = steps_dt[h : h + 1]
        last = run_row[:, PAIR - 1 : PAIR]
        gap = jnp.where(causal, run_col - run_row, 0.0)
        weights = jnp.where(causal, jnp.exp(gap) * scores * dt_row, 0.0)
        weights = weights + jnp.where(diagonal, skip_ref[head_ref[h]], 0.0)
        half = jnp.dot(place_t, weights.astype(bf16), preferred_element_type=f32).astype(bf16)
        w_ref[h, 0] = lax.dot_general(
            half, place_t, (((1,), (1,)), ((), ())), preferred_element_type=f32
        ).astype(bf16)
        c_now = (c_wide * jnp.exp(run_col)).astype(bf16)
        c_ref[h, 0] = jnp.dot(place_t, c_now, preferred_element_type=f32).astype(bf16)
        b_now = (b_cols * (jnp.exp(last - run_row) * dt_row)).astype(bf16)
        b_ref[h, 0] = lax.dot_general(
            b_now, place_t, (((1,), (1,)), ((), ())), preferred_element_type=f32
        ).astype(bf16)
        a_ref[h, 0] = jnp.broadcast_to(jnp.exp(last), (8, 128))


def prepare(place, own_heads, bias, rate, skip, pack):
    heads = own_heads.shape[0]
    pairs = pack.shape[0] // PAIR
    slots = 2 * CAP * EXPERTS
    smem = pl.BlockSpec(memory_space=pltpu.SMEM)

    def block(*dims):
        return pl.BlockSpec((heads, 1, *dims), lambda p: (0, p, 0, 0))

    return pl.pallas_call(
        functools.partial(prep_kernel, heads),
        out_shape=(
            jax.ShapeDtypeStruct((heads, pairs, slots, slots), bf16),
            jax.ShapeDtypeStruct((heads, pairs, slots, NS), bf16),
            jax.ShapeDtypeStruct((heads, pairs, NS, slots), bf16),
            jax.ShapeDtypeStruct((heads, pairs, 8, 128), f32),
        ),
        grid=(pairs,),
        in_specs=[smem] * 5 + [pl.BlockSpec((PAIR, PACK), lambda p: (p, 0))],
        out_specs=(block(slots, slots), block(slots, NS), block(NS, slots), block(8, 128)),
        compiler_params=params(),
        cost_estimate=pl.CostEstimate(
            flops=4 * heads * pairs * slots * slots * PAIR,
            bytes_accessed=2 * heads * pairs * slots * slots,
            transcendentals=heads * pairs * PAIR * PAIR,
        ),
        name="scan_weights",
    )(place, own_heads, bias, rate, skip, pack)


def scan_kernel(heads, place_ref, *refs):
    x_refs, refs = refs[:EXPERTS], refs[EXPERTS:]
    w_ref, c_ref, b_ref, a_ref, gain_ref, out_ref, state = refs

    @pl.when(pl.program_id(0) == 0)
    def _():
        state[...] = jnp.zeros_like(state)

    rows = 2 * CAP
    width = state.shape[2]
    steps = w_ref.shape[1]
    for i in range(steps):
        at = slice(i * rows, (i + 1) * rows)
        to = pl.ds(pl.multiple_of((pl.program_id(0) * steps + i) * rows, rows), rows)
        x = jnp.concatenate([x_ref[at, :] for x_ref in x_refs], axis=0)
        y = []
        for h in range(heads):
            x_head = x[:, h * width : (h + 1) * width]
            now = state[h]
            y.append(
                jnp.dot(w_ref[h, i], x_head, preferred_element_type=f32)
                + jnp.dot(c_ref[h, i], now.astype(bf16), preferred_element_type=f32)
            )
            state[h] = now * a_ref[h, i, 0:1, 0:1] + jnp.dot(
                b_ref[h, i], x_head, preferred_element_type=f32
            )
        y = jnp.concatenate(y, axis=1) if heads > 1 else y[0]
        z = (y * gain_ref[...]).astype(bf16)
        for q in range(EXPERTS):
            out_ref[place_ref[1] ^ q, to, :] = z[q * rows : (q + 1) * rows]

    @pl.when(pl.program_id(0) == pl.num_programs(0) - 1)
    def _():
        last = [state[h].astype(bf16) for h in range(heads)]
        last = jnp.concatenate(last, axis=1) if heads > 1 else last[0]
        for j in range(EXPERTS):
            out_ref[j, out_ref.shape[1] - NS :, :] = last


def scan(place, x, weights, gain, heads):
    rows, units = x[0].shape
    width = units // heads
    pairs = rows // (2 * CAP)
    step = 2
    slots = 2 * CAP * EXPERTS

    def block(*dims):
        return pl.BlockSpec((heads, step, *dims), lambda p, place_ref: (0, p, 0, 0))

    return pl.pallas_call(
        functools.partial(scan_kernel, heads),
        out_shape=jax.ShapeDtypeStruct((EXPERTS, rows + NS, units), bf16),
        grid_spec=pltpu.PrefetchScalarGridSpec(
            num_scalar_prefetch=1,
            grid=(pairs // step,),
            in_specs=[pl.BlockSpec((2 * CAP * step, units), lambda p, place_ref: (p, 0))] * EXPERTS
            + [
                block(slots, slots),
                block(slots, NS),
                block(NS, slots),
                block(8, 128),
                pl.BlockSpec((1, units), lambda p, place_ref: (0, 0)),
            ],
            out_specs=pl.BlockSpec(
                (EXPERTS, rows + NS, units), lambda p, place_ref: (0, 0, 0)
            ),
            scratch_shapes=[pltpu.VMEM((heads, NS, width), f32)],
        ),
        compiler_params=pltpu.CompilerParams(vmem_limit_bytes=VMEM_BYTES // 2),
        cost_estimate=pl.CostEstimate(
            flops=2 * heads * pairs * slots * (slots + 2 * NS) * width,
            bytes_accessed=2 * heads * pairs * slots * slots,
            transcendentals=0,
        ),
        name="scan",
    )(place, *x, *weights, gain)


def out_kernel(kind, counted, others, place_ref, *refs):
    refs = list(refs)

    def take(count):
        got = refs[:count]
        del refs[:count]
        return got

    z_ref, w_ref = take(2)
    inverse_ref = take(1)[0] if counted else None
    squares_refs = take(1 + others) if kind == "finish" else None
    part_refs = take(others) if kind == "finish" else None
    out_ref = take(1)[0]
    _, rows, units = z_ref.shape
    if counted:

        @pl.when(pl.program_id(0) == 0)
        def _():
            squares = jnp.zeros((rows, units), f32)
            for j in range(EXPERTS):
                z = z_ref[j].astype(f32) * inverse_ref[:, j * units : (j + 1) * units]
                squares = squares + z * z
            refs[0][...] = jnp.sum(squares, axis=1, keepdims=True)

    total = None
    for j in range(EXPERTS):
        part = jnp.dot(
            z_ref[j], w_ref[j * units : (j + 1) * units, :], preferred_element_type=f32
        )
        total = part if total is None else total + part
    if kind == "finish":
        squares = sum(r[...] for r in squares_refs)
        for part in part_refs:
            total = total + part[...].astype(f32)
        out_ref[...] = (total * lax.rsqrt(squares / INNER + 1e-05)).astype(bf16)
    else:
        out_ref[0] = total.astype(bf16)


def out_projection(kind, chunk, *, place, z, w_out, inverse=None, squares=(), parts=()):
    _, rows, units = z.shape
    rows = rows - NS
    slices = INNER // w_out.shape[0]
    slice_width = w_out.shape[1] // slices
    part = slice_width // CHUNKS
    count, first = (slices - 1, 1) if kind == "send" else (1, 0)
    tile = min(512, part)
    tiles = part // tile
    whole = slice_width // tile
    offset = chunk * tiles

    def column(n, place_ref):
        return (place_ref[0] + first + n // tiles) % slices * whole + offset + n % tiles

    def fixed(*dims):
        return pl.BlockSpec(dims, lambda n, place_ref: (0,) * len(dims))

    operands = [z, w_out]
    specs = [fixed(EXPERTS, rows, units)]
    specs.append(
        pl.BlockSpec((w_out.shape[0], tile), lambda n, place_ref: (0, column(n, place_ref)))
    )
    if inverse is not None:
        operands.append(inverse)
        specs.append(fixed(*inverse.shape))
    operands += [*squares, *parts]
    specs += [fixed(rows, 1)] * len(squares)
    specs += [pl.BlockSpec((rows, tile), lambda n, place_ref: (0, n))] * len(parts)
    if kind == "finish":
        out_shape = [jax.ShapeDtypeStruct((rows, part), bf16)]
        out_specs = [pl.BlockSpec((rows, tile), lambda n, place_ref: (0, n))]
    else:
        out_shape = [jax.ShapeDtypeStruct((count, rows, part), bf16)]
        out_specs = [
            pl.BlockSpec((1, rows, tile), lambda n, place_ref: (n // tiles, 0, n % tiles))
        ]
    if inverse is not None:
        out_shape.append(jax.ShapeDtypeStruct((rows, 1), f32))
        out_specs.append(fixed(rows, 1))
    return pl.pallas_call(
        functools.partial(out_kernel, kind, inverse is not None, len(parts)),
        out_shape=out_shape,
        grid_spec=pltpu.PrefetchScalarGridSpec(
            num_scalar_prefetch=1, grid=(count * tiles,), in_specs=specs, out_specs=out_specs
        ),
        compiler_params=params(),
        cost_estimate=pl.CostEstimate(
            flops=2 * rows * w_out.shape[0] * count * part,
            bytes_accessed=2 * w_out.shape[0] * count * part + 2 * rows * count * part,
            transcendentals=0,
        ),
        name="out_" + kind,
    )(place, *operands)


def collect_kernel(slices, ids_ref, *refs):
    chunk_refs, out_ref = refs[:-1], refs[-1]
    count, part = chunk_refs[0].shape
    rows = ids_ref.shape[1]
    depth = part * len(chunk_refs)
    step = min(512, part)
    ids, slot = route(ids_ref[...])
    at = ids[:, :1] * (slices * CAP) + slot
    lane = iota((rows, count), 1).astype(f32)
    for s in range(slices):
        pick = mask(at + s * CAP == lane)
        for k, rows_ref in enumerate(chunk_refs):
            for c in range(0, part, step):
                start = s * depth + k * part + c
                out_ref[:, start : start + step] = jnp.dot(
                    pick, rows_ref[:, c : c + step], preferred_element_type=f32
                ).astype(bf16)


def collect(ids_row, chunks, slices):
    width = sum(c.shape[1] for c in chunks) * slices
    return pl.pallas_call(
        functools.partial(collect_kernel, slices),
        out_shape=jax.ShapeDtypeStruct((ids_row.shape[1], width), bf16),
        compiler_params=params(),
        name="collect",
    )(ids_row, *chunks)


def turn(a, n, slices, r):
    return lax.ppermute(
        a, "expert", [(d, d // slices * slices + (d + r) % slices) for d in range(n)]
    )


def swap(a, groups=None):
    return lax.all_to_all(
        a, "expert", split_axis=0, concat_axis=0, axis_index_groups=groups, tiled=True
    )


def across(a, q, n, slices):
    pairs = [(d, (d // slices ^ q) * slices + d % slices) for d in range(n)]
    return lax.ppermute(a, "expert", pairs)


def exchange(arrays, n, slices):
    out = list(arrays)
    for q in reversed(range(1, EXPERTS)):
        out[q] = across(arrays[q], q, n, slices)
    return out


def shards(
    tokens, w_in, w_out, w_bcd, dt_bias, decay_rate, skip_gain, norm_gain, expert_ids, decode_heads
):
    n = lax.axis_size("expert")
    slices = n // EXPERTS
    in_dev = w_in.shape[2]
    units = in_dev // EXPERTS
    width = min(HEADDIM, units)
    heads = units // width
    me = lax.axis_index("expert")
    chip = (me // slices).astype(jnp.int32)
    place = jnp.stack([(me % slices).astype(jnp.int32), chip])
    start = place[0] * in_dev + chip * units
    same_slice = [[j * slices + k for j in range(EXPERTS)] for k in range(slices)]
    ids_row = expert_ids.reshape(1, -1)
    w_in, w_out = w_in[0], w_out[0]

    pack, outgoing = dispatch(ids_row, tokens, w_bcd.T, slices)
    landed = swap(outgoing)
    pack = lax.all_gather(pack, "expert", axis=0, tiled=True)
    own_heads = start // HEADDIM + jnp.arange(heads, dtype=jnp.int32)

    pieces = [landed] + [turn(landed, n, slices, r) for r in range(1, slices)]
    inner = [None] * EXPERTS
    for order in ((7,), (6, 5), (4, 3), (2, 1), (0,)):
        if order == (0,):
            weights = prepare(place, own_heads, dt_bias, decay_rate, skip_gain, pack)
            pieces, weights = lax.optimization_barrier((pieces, weights))
        for q, a in zip(order, in_projection(place, pieces, w_in, units, order)):
            inner[q] = a
    x = exchange(inner, n, slices)

    gain = lax.dynamic_slice(norm_gain, (start,), (units,)).reshape(1, units)
    z = swap(scan(place, x, weights, gain, heads), same_slice)

    inverse = 1.0 / lax.dynamic_slice(norm_gain, (place[0] * in_dev,), (in_dev,))
    inverse = inverse.reshape(1, in_dev)
    project = functools.partial(out_projection, place=place, z=z, w_out=w_out)
    sent = []
    for k in range(CHUNKS):
        got = project("send", k, inverse=inverse if k == 0 else None)
        if k == 0:
            squares = [got[1]] + [turn(got[1], n, slices, r) for r in range(1, slices)]
        sent.append([turn(got[0][r - 1], n, slices, r) for r in range(1, slices)])
    back = []
    for k in range(CHUNKS):
        [done] = project("finish", k, squares=squares, parts=sent[k])
        back.append(swap(done))
    mixed = collect(ids_row, back, slices)

    def picked(head):
        first = head * HEADDIM % in_dev
        parts = [
            lax.dynamic_slice(
                z, ((first + i) // units, z.shape[1] - NS, (first + i) % units), (1, NS, width)
            )
            for i in range(0, HEADDIM, width)
        ]
        return jnp.concatenate(parts, axis=0) if len(parts) > 1 else parts[0]

    want = decode_heads[0]
    chosen = picked(want)
    for r in range(1, slices):
        asked = turn(want, n, slices, slices - r)
        got = turn(picked(asked), n, slices, r)
        lies = want * HEADDIM // in_dev
        chosen = jnp.where((place[0] - lies + slices) % slices == r, got, chosen)
    chosen = chosen.transpose(0, 2, 1).astype(f32)
    return (mixed, chosen.reshape(1, HEADDIM * NS))


def solution(mesh):
    in_specs = (
        P(("groups", "expert"), None),
        P("expert", None, None),
        P("expert", None, None),
        P(),
        P(),
        P(),
        P(),
        P(),
        P(("groups", "expert"), None),
        P("expert"),
    )
    out_specs = (P(("groups", "expert"), None), P(("groups", "expert"), None))
    return jax.shard_map(shards, mesh=mesh, in_specs=in_specs, out_specs=out_specs, check_vma=False)
```

```python
import functools

import jax
import jax.numpy as jnp
from jax import lax
from jax.experimental import pallas as pl
from jax.experimental.pallas import tpu as pltpu
from jax.sharding import PartitionSpec as P

INNER = 4096
HEADDIM = 128
HEADS = 32
NS = 64
EXPERTS = 8
CAP = 24
PAIR = 256
PACK = 256
CHUNKS = 2
VMEM_BYTES = 48 * 1024 * 1024

f32 = jnp.float32
bf16 = jnp.bfloat16


def params(limit=VMEM_BYTES):
    return pltpu.CompilerParams(vmem_limit_bytes=limit)


def mask(condition):
    return condition.astype(f32).astype(bf16)


def iota(shape, dim):
    return lax.broadcasted_iota(jnp.int32, shape, dim)


def route(ids_row):
    rows = ids_row.shape[1]
    ids = jnp.broadcast_to(ids_row.astype(f32), (rows, rows)).T
    onehot = (ids == iota((rows, rows), 1).astype(f32)).astype(f32)
    lower = mask(iota((rows, rows), 1) < iota((rows, rows), 0))
    before = jnp.dot(lower, onehot.astype(bf16), preferred_element_type=f32)
    return ids, jnp.sum(before * onehot, axis=1, keepdims=True)


def fetched(refs, buffers, sems):
    copies = [
        pltpu.make_async_copy(ref, buffer, sems.at[i])
        for i, (ref, buffer) in enumerate(zip(refs, buffers))
    ]
    for copy in copies:
        copy.start()
    for copy in copies:
        copy.wait()


def dispatch_kernel(slices, *refs):
    pack_ref, out_ref = refs[4:6]
    want_ref = refs[0]
    ids_ref, tok_ref, bcd_ref, sems = refs[6:]
    fetched(refs[1:4], refs[6:9], sems)
    rows, width = tok_ref.shape
    depth = width // slices
    ids, slot = route(ids_ref[...])
    pick = mask(ids[:, :1] * CAP + slot == iota((rows, EXPERTS * CAP), 1).astype(f32))
    step = min(512, depth)
    for c in range(0, depth, step):
        got = [
            lax.dot_general(
                pick,
                tok_ref[:, s * depth + c : s * depth + c + step],
                (((0,), (0,)), ((), ())),
                preferred_element_type=f32,
            )
            for s in range(slices)
        ]
        for e in range(EXPERTS):
            piece = jnp.concatenate([g[e * CAP : (e + 1) * CAP] for g in got], axis=0)
            out_ref[e * slices * CAP : (e + 1) * slices * CAP, c : c + step] = piece.astype(bf16)

    across = (((1,), (1,)), ((), ()))
    tok = tok_ref[...]
    pack_ref[:, : 2 * NS] = lax.dot_general(
        tok, bcd_ref[: 2 * NS, :], across, preferred_element_type=f32
    ).astype(bf16)
    steps = bcd_ref[2 * NS : 2 * NS + HEADS, :]
    raw = lax.dot_general(
        tok, jnp.concatenate([steps] * 4, axis=0), across, preferred_element_type=f32
    )
    coarse = raw.astype(bf16).astype(f32)
    lane = iota((rows, 128), 1)
    side = jnp.where(lane < HEADS, coarse, raw - coarse)
    side = jnp.where(lane == 2 * HEADS, ids, jnp.where(lane == 2 * HEADS + 1, slot, side))
    side = jnp.where(lane == 2 * HEADS + 2, want_ref[0].astype(f32), side)
    pack_ref[:, 2 * NS :] = jnp.where(lane < 2 * HEADS + 3, side, 0.0).astype(bf16)


def dispatch(want, ids_row, tokens, bcd, slices):
    rows, width = tokens.shape
    operands = (ids_row, tokens, bcd)
    return pl.pallas_call(
        functools.partial(dispatch_kernel, slices),
        out_shape=(
            jax.ShapeDtypeStruct((rows, PACK), bf16),
            jax.ShapeDtypeStruct((EXPERTS * slices * CAP, width // slices), bf16),
        ),
        in_specs=[pl.BlockSpec(memory_space=pltpu.SMEM)]
        + [pl.BlockSpec(memory_space=pltpu.HBM)] * len(operands),
        scratch_shapes=[pltpu.VMEM(a.shape, a.dtype) for a in operands]
        + [pltpu.SemaphoreType.DMA((len(operands),))],
        compiler_params=params(60 * 1024 * 1024),
        name="dispatch",
    )(want, *operands)


def in_kernel(count, shares, turns, place_ref, *refs):
    rows_refs, w_refs, out_refs = refs[:count], refs[count : 2 * count], refs[2 * count :]
    total = None
    for r in range(count):
        part = jnp.dot(rows_refs[r][...], w_refs[r][...], preferred_element_type=f32)
        total = part if total is None else total + part
    for i, q in enumerate(turns):

        @pl.when(pl.program_id(0) == i)
        def _(i=i, q=q):
            units = out_refs[i].shape[1]
            own = total[:, :units]
            for k in range(1, shares):
                at = (place_ref[1] ^ q) % shares
                own = jnp.where(at == k, total[:, k * units : (k + 1) * units], own)
            out_refs[i][...] = own.astype(bf16)


def in_projection(place, pieces, w_in, units, turns):
    slices = len(pieces)
    rows, depth = pieces[0].shape
    tile = max(128, units)
    shares = tile // units

    def w_spec(r):
        def index(i, place_ref):
            q = sum(jnp.where(i == k, t, 0) for k, t in enumerate(turns))
            return (place_ref[0] - r + slices) % slices, (place_ref[1] ^ q) // shares

        return pl.BlockSpec((depth, tile), index)

    return pl.pallas_call(
        functools.partial(in_kernel, slices, shares, turns),
        out_shape=[jax.ShapeDtypeStruct((rows, units), bf16)] * len(turns),
        grid_spec=pltpu.PrefetchScalarGridSpec(
            num_scalar_prefetch=1,
            grid=(len(turns),),
            in_specs=[pl.BlockSpec((rows, depth), lambda i, place_ref: (0, 0))] * slices
            + [w_spec(r) for r in range(slices)],
            out_specs=[pl.BlockSpec((rows, units), lambda i, place_ref: (0, 0))] * len(turns),
        ),
        compiler_params=params(),
        cost_estimate=pl.CostEstimate(flops=rows, bytes_accessed=rows, transcendentals=0),
        name="in_projection",
    )(place, *pieces, *([w_in] * slices))


def prep_kernel(heads, place_ref, head_ref, bias_ref, rate_ref, skip_ref, pack_ref, w_ref, c_ref, b_ref, a_ref):
    pack = pack_ref[...]
    few = 8
    row = iota((few, PACK), 0)
    lane = iota((few, PACK), 1)
    side = lane - 2 * NS - 2 * HEADS
    choose = ((row == heads) & (side == 0)) | ((row == heads + 1) & (side == 1))
    choose = choose.astype(f32)
    row = iota((few, PAIR), 0)
    rate = bias = jnp.zeros((few, PAIR), f32)
    for h in range(heads):
        at = lane - 2 * NS - head_ref[h]
        choose = jnp.where((iota((few, PACK), 0) == h) & ((at == 0) | (at == HEADS)), 1.0, choose)
        rate = jnp.where(row == h, rate_ref[head_ref[h]], rate)
        bias = jnp.where(row == h, bias_ref[head_ref[h]], bias)
    across = lax.dot_general(
        choose.astype(bf16), pack, (((1,), (1,)), ((), ())), preferred_element_type=f32
    )
    raw = across + bias
    steps_dt = jnp.maximum(raw, 0.0) + jnp.log1p(jnp.exp(-jnp.abs(raw)))
    upto = iota((PAIR, PAIR), 0)
    now = iota((PAIR, PAIR), 1)
    rest = -steps_dt * rate
    split = []
    for _ in range(3):
        split.append(rest.astype(bf16).astype(f32))
        rest = rest - split[-1]
    sums = jnp.dot(
        jnp.concatenate(split + [jnp.zeros_like(rest)], axis=0).astype(bf16),
        mask(upto <= now),
        preferred_element_type=f32,
    )
    running = sums[:few] + sums[few : 2 * few] + sums[2 * few : 3 * few]
    second = iota((1, PAIR), 1) >= PAIR // 2
    turn_of = across[heads : heads + 1].astype(jnp.int32) ^ place_ref[1]
    column = turn_of * (2 * CAP) + across[heads + 1 : heads + 2].astype(jnp.int32)
    column = column + jnp.where(second, CAP, 0)
    slots = 2 * CAP * EXPERTS
    place_t = mask(iota((slots, PAIR), 0) == column)
    down = jnp.concatenate([running] * (128 // few), axis=0).T
    b_rows = pack[:, :NS]
    c_rows = pack[:, NS : 2 * NS]
    scores = lax.dot_general(
        c_rows, b_rows, (((1,), (1,)), ((), ())), preferred_element_type=f32
    )
    causal = upto >= now
    diagonal = upto == now
    b_cols = b_rows.astype(f32).T
    c_wide = c_rows.astype(f32)
    for h in range(heads):
        run_row = running[h : h + 1]
        run_col = down[:, h : h + 1]
        dt_row = steps_dt[h : h + 1]
        last = run_row[:, PAIR - 1 : PAIR]
        gap = jnp.where(causal, run_col - run_row, 0.0)
        weights = jnp.where(causal, jnp.exp(gap) * scores * dt_row, 0.0)
        weights = weights + jnp.where(diagonal, skip_ref[head_ref[h]], 0.0)
        half = jnp.dot(place_t, weights.astype(bf16), preferred_element_type=f32).astype(bf16)
        w_ref[h, 0] = lax.dot_general(
            half, place_t, (((1,), (1,)), ((), ())), preferred_element_type=f32
        ).astype(bf16)
        c_now = (c_wide * jnp.exp(run_col)).astype(bf16)
        c_ref[h, 0] = jnp.dot(place_t, c_now, preferred_element_type=f32).astype(bf16)
        b_now = (b_cols * (jnp.exp(last - run_row) * dt_row)).astype(bf16)
        b_ref[h, 0] = lax.dot_general(
            b_now, place_t, (((1,), (1,)), ((), ())), preferred_element_type=f32
        ).astype(bf16)
        a_ref[h, 0] = jnp.broadcast_to(jnp.exp(last), (8, 128))


def prepare(place, own_heads, bias, rate, skip, pack):
    heads = own_heads.shape[0]
    pairs = pack.shape[0] // PAIR
    slots = 2 * CAP * EXPERTS
    smem = pl.BlockSpec(memory_space=pltpu.SMEM)

    def block(*dims):
        return pl.BlockSpec((heads, 1, *dims), lambda p: (0, p, 0, 0))

    return pl.pallas_call(
        functools.partial(prep_kernel, heads),
        out_shape=(
            jax.ShapeDtypeStruct((heads, pairs, slots, slots), bf16),
            jax.ShapeDtypeStruct((heads, pairs, slots, NS), bf16),
            jax.ShapeDtypeStruct((heads, pairs, NS, slots), bf16),
            jax.ShapeDtypeStruct((heads, pairs, 8, 128), f32),
        ),
        grid=(pairs,),
        in_specs=[smem] * 5 + [pl.BlockSpec((PAIR, PACK), lambda p: (p, 0))],
        out_specs=(block(slots, slots), block(slots, NS), block(NS, slots), block(8, 128)),
        compiler_params=params(),
        cost_estimate=pl.CostEstimate(
            flops=4 * heads * pairs * slots * slots * PAIR,
            bytes_accessed=2 * heads * pairs * slots * slots,
            transcendentals=heads * pairs * PAIR * PAIR,
        ),
        name="scan_weights",
    )(place, own_heads, bias, rate, skip, pack)


def scan_kernel(heads, place_ref, *refs):
    x_refs, refs = refs[:EXPERTS], refs[EXPERTS:]
    w_ref, c_ref, b_ref, a_ref, gain_ref, out_ref, state = refs

    @pl.when(pl.program_id(0) == 0)
    def _():
        state[...] = jnp.zeros_like(state)

    rows = 2 * CAP
    width = state.shape[2]
    steps = w_ref.shape[1]
    for i in range(steps):
        at = slice(i * rows, (i + 1) * rows)
        to = pl.ds(pl.multiple_of((pl.program_id(0) * steps + i) * rows, rows), rows)
        x = jnp.concatenate([x_ref[at, :] for x_ref in x_refs], axis=0)
        y = []
        for h in range(heads):
            x_head = x[:, h * width : (h + 1) * width]
            now = state[h]
            y.append(
                jnp.dot(w_ref[h, i], x_head, preferred_element_type=f32)
                + jnp.dot(c_ref[h, i], now.astype(bf16), preferred_element_type=f32)
            )
            state[h] = now * a_ref[h, i, 0:1, 0:1] + jnp.dot(
                b_ref[h, i], x_head, preferred_element_type=f32
            )
        y = jnp.concatenate(y, axis=1) if heads > 1 else y[0]
        z = (y * gain_ref[...]).astype(bf16)
        for q in range(EXPERTS):
            out_ref[place_ref[1] ^ q, to, :] = z[q * rows : (q + 1) * rows]

    @pl.when(pl.program_id(0) == pl.num_programs(0) - 1)
    def _():
        last = [state[h].astype(bf16) for h in range(heads)]
        last = jnp.concatenate(last, axis=1) if heads > 1 else last[0]
        for j in range(EXPERTS):
            out_ref[j, out_ref.shape[1] - NS :, :] = last


def scan(place, x, weights, gain, heads):
    rows, units = x[0].shape
    width = units // heads
    pairs = rows // (2 * CAP)
    step = 2
    slots = 2 * CAP * EXPERTS

    def block(*dims):
        return pl.BlockSpec((heads, step, *dims), lambda p, place_ref: (0, p, 0, 0))

    return pl.pallas_call(
        functools.partial(scan_kernel, heads),
        out_shape=pltpu.HBM((EXPERTS, rows + NS, units), bf16),
        grid_spec=pltpu.PrefetchScalarGridSpec(
            num_scalar_prefetch=1,
            grid=(pairs // step,),
            in_specs=[pl.BlockSpec((2 * CAP * step, units), lambda p, place_ref: (p, 0))] * EXPERTS
            + [
                block(slots, slots),
                block(slots, NS),
                block(NS, slots),
                block(8, 128),
                pl.BlockSpec((1, units), lambda p, place_ref: (0, 0)),
            ],
            out_specs=pl.BlockSpec(
                (EXPERTS, rows + NS, units), lambda p, place_ref: (0, 0, 0)
            ),
            scratch_shapes=[pltpu.VMEM((heads, NS, width), f32)],
        ),
        compiler_params=pltpu.CompilerParams(vmem_limit_bytes=VMEM_BYTES // 2),
        cost_estimate=pl.CostEstimate(
            flops=2 * heads * pairs * slots * (slots + 2 * NS) * width,
            bytes_accessed=2 * heads * pairs * slots * slots,
            transcendentals=0,
        ),
        name="scan",
    )(place, *x, *weights, gain)


def out_kernel(kind, counted, others, resumed, place_ref, *refs):
    refs = list(refs)

    def take(count):
        got = refs[:count]
        del refs[:count]
        return got

    z_ref, w_ref = take(2)
    inverse_ref = take(1)[0] if counted else None
    squares_refs = take(1 + others) if kind == "finish" else None
    part_refs = take(others) if kind == "finish" else None
    if resumed:
        take(1)
    out_ref = take(1)[0]
    _, rows, units = z_ref.shape
    if counted:

        @pl.when(pl.program_id(0) == 0)
        def _():
            squares = jnp.zeros((rows, units), f32)
            for j in range(EXPERTS):
                z = z_ref[j].astype(f32) * inverse_ref[:, j * units : (j + 1) * units]
                squares = squares + z * z
            refs[0][...] = jnp.sum(squares, axis=1, keepdims=True)

    total = None
    for j in range(EXPERTS):
        part = jnp.dot(
            z_ref[j], w_ref[j * units : (j + 1) * units, :], preferred_element_type=f32
        )
        total = part if total is None else total + part
    if kind == "finish":
        squares = sum(r[...] for r in squares_refs)
        for part in part_refs:
            total = total + part[...].astype(f32)
        out_ref[...] = (total * lax.rsqrt(squares / INNER + 1e-05)).astype(bf16)
    else:
        out_ref[0] = total.astype(bf16)


def out_projection(
    kind, chunk, *, place, z, w_out, inverse=None, squares=(), parts=(), before=None
):
    _, rows, units = z.shape
    rows = rows - NS
    slices = INNER // w_out.shape[0]
    slice_width = w_out.shape[1] // slices
    part = slice_width // CHUNKS
    count, first = (slices - 1, 1) if kind == "send" else (1, 0)
    tile = min(256, part)
    tiles = part // tile
    whole = slice_width // tile
    offset = chunk * tiles

    def column(n, place_ref):
        return (place_ref[0] + first + n // tiles) % slices * whole + offset + n % tiles

    def fixed(*dims):
        return pl.BlockSpec(dims, lambda n, place_ref: (0,) * len(dims))

    operands = [z, w_out]
    specs = [fixed(EXPERTS, rows, units)]
    specs.append(
        pl.BlockSpec((w_out.shape[0], tile), lambda n, place_ref: (0, column(n, place_ref)))
    )
    if inverse is not None:
        operands.append(inverse)
        specs.append(fixed(*inverse.shape))
    operands += [*squares, *parts]
    specs += [fixed(rows, 1)] * len(squares)
    specs += [pl.BlockSpec((rows, tile), lambda n, place_ref: (0, n))] * len(parts)
    aliases = {}
    if before is not None:
        aliases = {1 + len(operands): 0}
        operands.append(before)
        specs.append(pl.BlockSpec(memory_space=pl.ANY))
    if kind == "finish":
        out_shape = [pltpu.HBM((rows, slice_width), bf16)]
        out_specs = [pl.BlockSpec((rows, tile), lambda n, place_ref: (0, offset + n))]
    else:
        out_shape = [jax.ShapeDtypeStruct((count, rows, part), bf16)]
        out_specs = [
            pl.BlockSpec((1, rows, tile), lambda n, place_ref: (n // tiles, 0, n % tiles))
        ]
    if inverse is not None:
        out_shape.append(jax.ShapeDtypeStruct((rows, 1), f32))
        out_specs.append(fixed(rows, 1))
    return pl.pallas_call(
        functools.partial(out_kernel, kind, inverse is not None, len(parts), before is not None),
        out_shape=out_shape,
        grid_spec=pltpu.PrefetchScalarGridSpec(
            num_scalar_prefetch=1, grid=(count * tiles,), in_specs=specs, out_specs=out_specs
        ),
        input_output_aliases=aliases,
        compiler_params=params(),
        cost_estimate=pl.CostEstimate(
            flops=2 * rows * w_out.shape[0] * count * part,
            bytes_accessed=2 * w_out.shape[0] * count * part + 2 * rows * count * part,
            transcendentals=0,
        ),
        name="out_" + kind,
    )(place, *operands)


def collect_kernel(slices, ids_ref, *refs):
    chunk_refs, out_ref = refs[:-1], refs[-1]
    count, part = chunk_refs[0].shape
    rows = ids_ref.shape[1]
    depth = part * len(chunk_refs)
    step = min(512, part)
    ids, slot = route(ids_ref[...])
    at = ids[:, :1] * (slices * CAP) + slot
    lane = iota((rows, count), 1).astype(f32)
    for s in range(slices):
        pick = mask(at + s * CAP == lane)
        for k, rows_ref in enumerate(chunk_refs):
            for c in range(0, part, step):
                start = s * depth + k * part + c
                out_ref[:, start : start + step] = jnp.dot(
                    pick, rows_ref[:, c : c + step], preferred_element_type=f32
                ).astype(bf16)


def collect(ids_row, chunks, slices):
    width = sum(c.shape[1] for c in chunks) * slices
    return pl.pallas_call(
        functools.partial(collect_kernel, slices),
        out_shape=jax.ShapeDtypeStruct((ids_row.shape[1], width), bf16),
        compiler_params=params(),
        name="collect",
    )(ids_row, *chunks)


def turn(a, n, slices, r):
    return lax.ppermute(
        a, "expert", [(d, d // slices * slices + (d + r) % slices) for d in range(n)]
    )


def swap(a, groups=None):
    return lax.all_to_all(
        a, "expert", split_axis=0, concat_axis=0, axis_index_groups=groups, tiled=True
    )


def across(a, q, n, slices):
    pairs = [(d, (d // slices ^ q) * slices + d % slices) for d in range(n)]
    return lax.ppermute(a, "expert", pairs)


def exchange(arrays, n, slices):
    out = list(arrays)
    for q in reversed(range(1, EXPERTS)):
        out[q] = across(arrays[q], q, n, slices)
    return out


def shards(
    tokens, w_in, w_out, w_bcd, dt_bias, decay_rate, skip_gain, norm_gain, expert_ids, decode_heads
):
    n = lax.axis_size("expert")
    slices = n // EXPERTS
    in_dev = w_in.shape[2]
    units = in_dev // EXPERTS
    width = min(HEADDIM, units)
    heads = units // width
    me = lax.axis_index("expert")
    chip = (me // slices).astype(jnp.int32)
    place = jnp.stack([(me % slices).astype(jnp.int32), chip])
    start = place[0] * in_dev + chip * units
    same_slice = [[j * slices + k for j in range(EXPERTS)] for k in range(slices)]
    ids_row = expert_ids.reshape(1, -1)
    w_in, w_out = w_in[0], w_out[0]

    pack, outgoing = dispatch(decode_heads, ids_row, tokens, w_bcd.T, slices)
    landed = swap(outgoing)
    pack = lax.all_gather(pack, "expert", axis=0, tiled=True)
    own_heads = start // HEADDIM + jnp.arange(heads, dtype=jnp.int32)

    pieces = [landed] + [turn(landed, n, slices, r) for r in range(1, slices)]
    inner = [None] * EXPERTS
    for order in ((7, 6), (5, 4, 3), (2, 1), (0,)):
        if order == (0,):
            weights = prepare(place, own_heads, dt_bias, decay_rate, skip_gain, pack)
            pieces, weights = lax.optimization_barrier((pieces, weights))
        for q, a in zip(order, in_projection(place, pieces, w_in, units, order)):
            inner[q] = a
    x = exchange(inner, n, slices)

    gain = lax.dynamic_slice(norm_gain, (start,), (units,)).reshape(1, units)
    z = swap(scan(place, x, weights, gain, heads), same_slice)

    inverse = 1.0 / lax.dynamic_slice(norm_gain, (place[0] * in_dev,), (in_dev,))
    inverse = inverse.reshape(1, in_dev)
    project = functools.partial(out_projection, place=place, z=z, w_out=w_out)
    sent = []
    for k in range(CHUNKS):
        got = project("send", k, inverse=inverse if k == 0 else None)
        if k == 0:
            squares = [got[1]] + [turn(got[1], n, slices, r) for r in range(1, slices)]
        sent.append([turn(got[0][r - 1], n, slices, r) for r in range(1, slices)])
    done = None
    for k in range(CHUNKS):
        [done] = project("finish", k, squares=squares, parts=sent[k], before=done)
    mixed = collect(ids_row, [swap(done)], slices)

    def picked(head):
        first = head * HEADDIM % in_dev
        parts = [
            lax.dynamic_slice(
                z, ((first + i) // units, z.shape[1] - NS, (first + i) % units), (1, NS, width)
            )
            for i in range(0, HEADDIM, width)
        ]
        return jnp.concatenate(parts, axis=0) if len(parts) > 1 else parts[0]

    want = decode_heads[0]
    chosen = picked(want)
    for r in range(1, slices):
        other = chip * slices + (place[0] + r) % slices
        asked = lax.dynamic_slice(
            pack, (other * tokens.shape[0], 2 * NS + 2 * HEADS + 2), (1, 1)
        )[0, 0].astype(jnp.int32)
        got = turn(picked(asked), n, slices, r)
        lies = want * HEADDIM // in_dev
        chosen = jnp.where((place[0] - lies + slices) % slices == r, got, chosen)
    chosen = chosen.transpose(0, 2, 1).astype(f32)
    return (mixed, chosen.reshape(1, HEADDIM * NS))


def solution(mesh):
    in_specs = (
        P(("groups", "expert"), None),
        P("expert", None, None),
        P("expert", None, None),
        P(),
        P(),
        P(),
        P(),
        P(),
        P(("groups", "expert"), None),
        P("expert"),
    )
    out_specs = (P(("groups", "expert"), None), P(("groups", "expert"), None))
    return jax.shard_map(shards, mesh=mesh, in_specs=in_specs, out_specs=out_specs, check_vma=False)
```

```python
import functools

import jax
import jax.numpy as jnp
from jax import lax
from jax.experimental import pallas as pl
from jax.experimental.pallas import tpu as pltpu
from jax.sharding import PartitionSpec as P

INNER = 4096
HEADDIM = 128
HEADS = 32
NS = 64
EXPERTS = 8
CAP = 24
PAIR = 256
PACK = 256
CHUNKS = 1
VMEM_BYTES = 48 * 1024 * 1024

f32 = jnp.float32
bf16 = jnp.bfloat16


def params(limit=VMEM_BYTES):
    return pltpu.CompilerParams(vmem_limit_bytes=limit)


def mask(condition):
    return condition.astype(f32).astype(bf16)


def iota(shape, dim):
    return lax.broadcasted_iota(jnp.int32, shape, dim)


def route(ids_row):
    rows = ids_row.shape[1]
    ids = jnp.broadcast_to(ids_row.astype(f32), (rows, rows)).T
    onehot = (ids == iota((rows, rows), 1).astype(f32)).astype(f32)
    lower = mask(iota((rows, rows), 1) < iota((rows, rows), 0))
    before = jnp.dot(lower, onehot.astype(bf16), preferred_element_type=f32)
    return ids, jnp.sum(before * onehot, axis=1, keepdims=True)


def fetched(refs, buffers, sems):
    copies = [
        pltpu.make_async_copy(ref, buffer, sems.at[i])
        for i, (ref, buffer) in enumerate(zip(refs, buffers))
    ]
    for copy in copies:
        copy.start()
    for copy in copies:
        copy.wait()


def dispatch_kernel(slices, *refs):
    pack_ref, out_ref = refs[4:6]
    want_ref = refs[0]
    ids_ref, tok_ref, bcd_ref, sems = refs[6:]
    fetched(refs[1:4], refs[6:9], sems)
    rows, width = tok_ref.shape
    depth = width // slices
    ids, slot = route(ids_ref[...])
    pick = mask(ids[:, :1] * CAP + slot == iota((rows, EXPERTS * CAP), 1).astype(f32))
    step = min(512, depth)
    for c in range(0, depth, step):
        got = [
            lax.dot_general(
                pick,
                tok_ref[:, s * depth + c : s * depth + c + step],
                (((0,), (0,)), ((), ())),
                preferred_element_type=f32,
            )
            for s in range(slices)
        ]
        for e in range(EXPERTS):
            piece = jnp.concatenate([g[e * CAP : (e + 1) * CAP] for g in got], axis=0)
            out_ref[e * slices * CAP : (e + 1) * slices * CAP, c : c + step] = piece.astype(bf16)

    across = (((1,), (1,)), ((), ()))
    tok = tok_ref[...]
    pack_ref[:, : 2 * NS] = lax.dot_general(
        tok, bcd_ref[: 2 * NS, :], across, preferred_element_type=f32
    ).astype(bf16)
    steps = bcd_ref[2 * NS : 2 * NS + HEADS, :]
    raw = lax.dot_general(
        tok, jnp.concatenate([steps] * 4, axis=0), across, preferred_element_type=f32
    )
    coarse = raw.astype(bf16).astype(f32)
    lane = iota((rows, 128), 1)
    side = jnp.where(lane < HEADS, coarse, raw - coarse)
    side = jnp.where(lane == 2 * HEADS, ids, jnp.where(lane == 2 * HEADS + 1, slot, side))
    side = jnp.where(lane == 2 * HEADS + 2, want_ref[0].astype(f32), side)
    pack_ref[:, 2 * NS :] = jnp.where(lane < 2 * HEADS + 3, side, 0.0).astype(bf16)


def dispatch(want, ids_row, tokens, bcd, slices):
    rows, width = tokens.shape
    operands = (ids_row, tokens, bcd)
    return pl.pallas_call(
        functools.partial(dispatch_kernel, slices),
        out_shape=(
            jax.ShapeDtypeStruct((rows, PACK), bf16),
            jax.ShapeDtypeStruct((EXPERTS * slices * CAP, width // slices), bf16),
        ),
        in_specs=[pl.BlockSpec(memory_space=pltpu.SMEM)]
        + [pl.BlockSpec(memory_space=pltpu.HBM)] * len(operands),
        scratch_shapes=[pltpu.VMEM(a.shape, a.dtype) for a in operands]
        + [pltpu.SemaphoreType.DMA((len(operands),))],
        compiler_params=params(60 * 1024 * 1024),
        name="dispatch",
    )(want, *operands)


def in_kernel(count, shares, turns, place_ref, *refs):
    rows_refs, w_refs, out_refs = refs[:count], refs[count : 2 * count], refs[2 * count :]
    total = None
    for r in range(count):
        part = jnp.dot(rows_refs[r][...], w_refs[r][...], preferred_element_type=f32)
        total = part if total is None else total + part
    for i, q in enumerate(turns):

        @pl.when(pl.program_id(0) == i)
        def _(i=i, q=q):
            units = out_refs[i].shape[1]
            own = total[:, :units]
            for k in range(1, shares):
                at = (place_ref[1] ^ q) % shares
                own = jnp.where(at == k, total[:, k * units : (k + 1) * units], own)
            out_refs[i][...] = own.astype(bf16)


def in_projection(place, pieces, w_in, units, turns):
    slices = len(pieces)
    rows, depth = pieces[0].shape
    tile = max(128, units)
    shares = tile // units

    def w_spec(r):
        def index(i, place_ref):
            q = sum(jnp.where(i == k, t, 0) for k, t in enumerate(turns))
            return (place_ref[0] - r + slices) % slices, (place_ref[1] ^ q) // shares

        return pl.BlockSpec((depth, tile), index)

    return pl.pallas_call(
        functools.partial(in_kernel, slices, shares, turns),
        out_shape=[jax.ShapeDtypeStruct((rows, units), bf16)] * len(turns),
        grid_spec=pltpu.PrefetchScalarGridSpec(
            num_scalar_prefetch=1,
            grid=(len(turns),),
            in_specs=[pl.BlockSpec((rows, depth), lambda i, place_ref: (0, 0))] * slices
            + [w_spec(r) for r in range(slices)],
            out_specs=[pl.BlockSpec((rows, units), lambda i, place_ref: (0, 0))] * len(turns),
        ),
        compiler_params=params(),
        cost_estimate=pl.CostEstimate(flops=rows, bytes_accessed=rows, transcendentals=0),
        name="in_projection",
    )(place, *pieces, *([w_in] * slices))


def prep_kernel(heads, place_ref, head_ref, bias_ref, rate_ref, skip_ref, pack_ref, w_ref, c_ref, b_ref, a_ref):
    pack = pack_ref[...]
    few = 8
    row = iota((few, PACK), 0)
    lane = iota((few, PACK), 1)
    side = lane - 2 * NS - 2 * HEADS
    choose = ((row == heads) & (side == 0)) | ((row == heads + 1) & (side == 1))
    choose = choose.astype(f32)
    row = iota((few, PAIR), 0)
    rate = bias = jnp.zeros((few, PAIR), f32)
    for h in range(heads):
        at = lane - 2 * NS - head_ref[h]
        choose = jnp.where((iota((few, PACK), 0) == h) & ((at == 0) | (at == HEADS)), 1.0, choose)
        rate = jnp.where(row == h, rate_ref[head_ref[h]], rate)
        bias = jnp.where(row == h, bias_ref[head_ref[h]], bias)
    across = lax.dot_general(
        choose.astype(bf16), pack, (((1,), (1,)), ((), ())), preferred_element_type=f32
    )
    raw = across + bias
    steps_dt = jnp.maximum(raw, 0.0) + jnp.log1p(jnp.exp(-jnp.abs(raw)))
    upto = iota((PAIR, PAIR), 0)
    now = iota((PAIR, PAIR), 1)
    rest = -steps_dt * rate
    split = []
    for _ in range(3):
        split.append(rest.astype(bf16).astype(f32))
        rest = rest - split[-1]
    sums = jnp.dot(
        jnp.concatenate(split + [jnp.zeros_like(rest)], axis=0).astype(bf16),
        mask(upto <= now),
        preferred_element_type=f32,
    )
    running = sums[:few] + sums[few : 2 * few] + sums[2 * few : 3 * few]
    second = iota((1, PAIR), 1) >= PAIR // 2
    turn_of = across[heads : heads + 1].astype(jnp.int32) ^ place_ref[1]
    column = turn_of * (2 * CAP) + across[heads + 1 : heads + 2].astype(jnp.int32)
    column = column + jnp.where(second, CAP, 0)
    slots = 2 * CAP * EXPERTS
    place_t = mask(iota((slots, PAIR), 0) == column)
    down = jnp.concatenate([running] * (128 // few), axis=0).T
    b_rows = pack[:, :NS]
    c_rows = pack[:, NS : 2 * NS]
    scores = lax.dot_general(
        c_rows, b_rows, (((1,), (1,)), ((), ())), preferred_element_type=f32
    )
    causal = upto >= now
    diagonal = upto == now
    b_cols = b_rows.astype(f32).T
    c_wide = c_rows.astype(f32)
    to_place, b_now = [], []
    for h in range(heads):
        run_row = running[h : h + 1]
        run_col = down[:, h : h + 1]
        dt_row = steps_dt[h : h + 1]
        last = run_row[:, PAIR - 1 : PAIR]
        gap = jnp.where(causal, run_col - run_row, 0.0)
        weights = jnp.where(causal, jnp.exp(gap) * scores * dt_row, 0.0)
        weights = weights + jnp.where(diagonal, skip_ref[head_ref[h]], 0.0)
        to_place.append(weights.astype(bf16))
        b_now.append((b_cols * (jnp.exp(last - run_row) * dt_row)).astype(bf16))
        c_now = (c_wide * jnp.exp(run_col)).astype(bf16)
        c_ref[h, 0] = jnp.dot(place_t, c_now, preferred_element_type=f32).astype(bf16)
        a_ref[h, 0] = jnp.broadcast_to(jnp.exp(last), (8, 128))
    together = jnp.concatenate(to_place, axis=1) if heads > 1 else to_place[0]
    half = jnp.dot(place_t, together, preferred_element_type=f32).astype(bf16)
    rows = [half[:, h * PAIR : (h + 1) * PAIR] for h in range(heads)] + b_now
    placed = lax.dot_general(
        jnp.concatenate(rows, axis=0),
        place_t,
        (((1,), (1,)), ((), ())),
        preferred_element_type=f32,
    ).astype(bf16)
    for h in range(heads):
        w_ref[h, 0] = placed[h * slots : (h + 1) * slots]
        below = heads * slots + h * NS
        b_ref[h, 0] = placed[below : below + NS]


def prepare(place, own_heads, bias, rate, skip, pack):
    heads = own_heads.shape[0]
    pairs = pack.shape[0] // PAIR
    slots = 2 * CAP * EXPERTS
    smem = pl.BlockSpec(memory_space=pltpu.SMEM)

    def block(*dims):
        return pl.BlockSpec((heads, 1, *dims), lambda p: (0, p, 0, 0))

    return pl.pallas_call(
        functools.partial(prep_kernel, heads),
        out_shape=(
            jax.ShapeDtypeStruct((heads, pairs, slots, slots), bf16),
            jax.ShapeDtypeStruct((heads, pairs, slots, NS), bf16),
            jax.ShapeDtypeStruct((heads, pairs, NS, slots), bf16),
            jax.ShapeDtypeStruct((heads, pairs, 8, 128), f32),
        ),
        grid=(pairs,),
        in_specs=[smem] * 5 + [pl.BlockSpec((PAIR, PACK), lambda p: (p, 0))],
        out_specs=(block(slots, slots), block(slots, NS), block(NS, slots), block(8, 128)),
        compiler_params=params(),
        cost_estimate=pl.CostEstimate(
            flops=4 * heads * pairs * slots * slots * PAIR,
            bytes_accessed=2 * heads * pairs * slots * slots,
            transcendentals=heads * pairs * PAIR * PAIR,
        ),
        name="scan_weights",
    )(place, own_heads, bias, rate, skip, pack)


def scan_kernel(heads, place_ref, *refs):
    x_refs, refs = refs[:EXPERTS], refs[EXPERTS:]
    w_ref, c_ref, b_ref, a_ref, gain_ref, out_ref, state = refs

    @pl.when(pl.program_id(0) == 0)
    def _():
        state[...] = jnp.zeros_like(state)

    rows = 2 * CAP
    width = state.shape[2]
    steps = w_ref.shape[1]
    for i in range(steps):
        at = slice(i * rows, (i + 1) * rows)
        to = pl.ds(pl.multiple_of((pl.program_id(0) * steps + i) * rows, rows), rows)
        x = jnp.concatenate([x_ref[at, :] for x_ref in x_refs], axis=0)
        y = []
        for h in range(heads):
            x_head = x[:, h * width : (h + 1) * width]
            now = state[h]
            y.append(
                jnp.dot(w_ref[h, i], x_head, preferred_element_type=f32)
                + jnp.dot(c_ref[h, i], now.astype(bf16), preferred_element_type=f32)
            )
            state[h] = now * a_ref[h, i, 0:1, 0:1] + jnp.dot(
                b_ref[h, i], x_head, preferred_element_type=f32
            )
        y = jnp.concatenate(y, axis=1) if heads > 1 else y[0]
        z = (y * gain_ref[...]).astype(bf16)
        for q in range(EXPERTS):
            out_ref[place_ref[1] ^ q, to, :] = z[q * rows : (q + 1) * rows]

    @pl.when(pl.program_id(0) == pl.num_programs(0) - 1)
    def _():
        last = [state[h].astype(bf16) for h in range(heads)]
        last = jnp.concatenate(last, axis=1) if heads > 1 else last[0]
        for j in range(EXPERTS):
            out_ref[j, out_ref.shape[1] - NS :, :] = last


def scan(place, x, weights, gain, heads):
    rows, units = x[0].shape
    width = units // heads
    pairs = rows // (2 * CAP)
    step = 2
    slots = 2 * CAP * EXPERTS

    def block(*dims):
        return pl.BlockSpec((heads, step, *dims), lambda p, place_ref: (0, p, 0, 0))

    return pl.pallas_call(
        functools.partial(scan_kernel, heads),
        out_shape=pltpu.HBM((EXPERTS, rows + NS, units), bf16),
        grid_spec=pltpu.PrefetchScalarGridSpec(
            num_scalar_prefetch=1,
            grid=(pairs // step,),
            in_specs=[pl.BlockSpec((2 * CAP * step, units), lambda p, place_ref: (p, 0))] * EXPERTS
            + [
                block(slots, slots),
                block(slots, NS),
                block(NS, slots),
                block(8, 128),
                pl.BlockSpec((1, units), lambda p, place_ref: (0, 0)),
            ],
            out_specs=pl.BlockSpec(
                (EXPERTS, rows + NS, units), lambda p, place_ref: (0, 0, 0)
            ),
            scratch_shapes=[pltpu.VMEM((heads, NS, width), f32)],
        ),
        compiler_params=pltpu.CompilerParams(vmem_limit_bytes=VMEM_BYTES // 2),
        cost_estimate=pl.CostEstimate(
            flops=2 * heads * pairs * slots * (slots + 2 * NS) * width,
            bytes_accessed=2 * heads * pairs * slots * slots,
            transcendentals=0,
        ),
        name="scan",
    )(place, *x, *weights, gain)


def out_kernel(kind, counted, others, resumed, place_ref, *refs):
    refs = list(refs)

    def take(count):
        got = refs[:count]
        del refs[:count]
        return got

    z_ref, w_ref = take(2)
    inverse_ref = take(1)[0] if counted else None
    squares_refs = take(1 + others) if kind == "finish" else None
    part_refs = take(others) if kind == "finish" else None
    if resumed:
        take(1)
    out_ref = take(1)[0]
    _, rows, units = z_ref.shape
    if counted:

        @pl.when(pl.program_id(0) == 0)
        def _():
            squares = jnp.zeros((rows, units), f32)
            for j in range(EXPERTS):
                z = z_ref[j].astype(f32) * inverse_ref[:, j * units : (j + 1) * units]
                squares = squares + z * z
            refs[0][...] = jnp.sum(squares, axis=1, keepdims=True)

    total = None
    for j in range(EXPERTS):
        part = jnp.dot(
            z_ref[j], w_ref[j * units : (j + 1) * units, :], preferred_element_type=f32
        )
        total = part if total is None else total + part
    if kind == "finish":
        squares = sum(r[...] for r in squares_refs)
        for part in part_refs:
            total = total + part[...].astype(f32)
        out_ref[...] = (total * lax.rsqrt(squares / INNER + 1e-05)).astype(bf16)
    else:
        out_ref[0] = total.astype(bf16)


def out_projection(
    kind, chunk, *, place, z, w_out, inverse=None, squares=(), parts=(), before=None
):
    _, rows, units = z.shape
    rows = rows - NS
    slices = INNER // w_out.shape[0]
    slice_width = w_out.shape[1] // slices
    part = slice_width // CHUNKS
    count, first = (slices - 1, 1) if kind == "send" else (1, 0)
    tile = min(512, part)
    tiles = part // tile
    whole = slice_width // tile
    offset = chunk * tiles

    def column(n, place_ref):
        return (place_ref[0] + first + n // tiles) % slices * whole + offset + n % tiles

    def fixed(*dims):
        return pl.BlockSpec(dims, lambda n, place_ref: (0,) * len(dims))

    operands = [z, w_out]
    specs = [fixed(EXPERTS, rows, units)]
    specs.append(
        pl.BlockSpec((w_out.shape[0], tile), lambda n, place_ref: (0, column(n, place_ref)))
    )
    if inverse is not None:
        operands.append(inverse)
        specs.append(fixed(*inverse.shape))
    operands += [*squares, *parts]
    specs += [fixed(rows, 1)] * len(squares)
    specs += [pl.BlockSpec((rows, tile), lambda n, place_ref: (0, n))] * len(parts)
    aliases = {}
    if before is not None:
        aliases = {1 + len(operands): 0}
        operands.append(before)
        specs.append(pl.BlockSpec(memory_space=pl.ANY))
    if kind == "finish":
        out_shape = [pltpu.HBM((rows, slice_width), bf16)]
        out_specs = [pl.BlockSpec((rows, tile), lambda n, place_ref: (0, offset + n))]
    else:
        out_shape = [jax.ShapeDtypeStruct((count, rows, part), bf16)]
        out_specs = [
            pl.BlockSpec((1, rows, tile), lambda n, place_ref: (n // tiles, 0, n % tiles))
        ]
    if inverse is not None:
        out_shape.append(jax.ShapeDtypeStruct((rows, 1), f32))
        out_specs.append(fixed(rows, 1))
    return pl.pallas_call(
        functools.partial(out_kernel, kind, inverse is not None, len(parts), before is not None),
        out_shape=out_shape,
        grid_spec=pltpu.PrefetchScalarGridSpec(
            num_scalar_prefetch=1, grid=(count * tiles,), in_specs=specs, out_specs=out_specs
        ),
        input_output_aliases=aliases,
        compiler_params=params(),
        cost_estimate=pl.CostEstimate(
            flops=2 * rows * w_out.shape[0] * count * part,
            bytes_accessed=2 * w_out.shape[0] * count * part + 2 * rows * count * part,
            transcendentals=0,
        ),
        name="out_" + kind,
    )(place, *operands)


def collect_kernel(slices, ids_ref, *refs):
    chunk_refs, out_ref = refs[:-1], refs[-1]
    count, part = chunk_refs[0].shape
    rows = ids_ref.shape[1]
    depth = part * len(chunk_refs)
    step = min(512, part)
    ids, slot = route(ids_ref[...])
    at = ids[:, :1] * (slices * CAP) + slot
    lane = iota((rows, count), 1).astype(f32)
    for s in range(slices):
        pick = mask(at + s * CAP == lane)
        for k, rows_ref in enumerate(chunk_refs):
            for c in range(0, part, step):
                start = s * depth + k * part + c
                out_ref[:, start : start + step] = jnp.dot(
                    pick, rows_ref[:, c : c + step], preferred_element_type=f32
                ).astype(bf16)


def collect(ids_row, chunks, slices):
    width = sum(c.shape[1] for c in chunks) * slices
    return pl.pallas_call(
        functools.partial(collect_kernel, slices),
        out_shape=jax.ShapeDtypeStruct((ids_row.shape[1], width), bf16),
        compiler_params=params(),
        name="collect",
    )(ids_row, *chunks)


def turn(a, n, slices, r):
    return lax.ppermute(
        a, "expert", [(d, d // slices * slices + (d + r) % slices) for d in range(n)]
    )


def swap(a, groups=None):
    return lax.all_to_all(
        a, "expert", split_axis=0, concat_axis=0, axis_index_groups=groups, tiled=True
    )


def across(a, q, n, slices):
    pairs = [(d, (d // slices ^ q) * slices + d % slices) for d in range(n)]
    return lax.ppermute(a, "expert", pairs)


def exchange(arrays, n, slices):
    out = list(arrays)
    for q in reversed(range(1, EXPERTS)):
        out[q] = across(arrays[q], q, n, slices)
    return out


def shards(
    tokens, w_in, w_out, w_bcd, dt_bias, decay_rate, skip_gain, norm_gain, expert_ids, decode_heads
):
    n = lax.axis_size("expert")
    slices = n // EXPERTS
    in_dev = w_in.shape[2]
    units = in_dev // EXPERTS
    width = min(HEADDIM, units)
    heads = units // width
    me = lax.axis_index("expert")
    chip = (me // slices).astype(jnp.int32)
    place = jnp.stack([(me % slices).astype(jnp.int32), chip])
    start = place[0] * in_dev + chip * units
    same_slice = [[j * slices + k for j in range(EXPERTS)] for k in range(slices)]
    ids_row = expert_ids.reshape(1, -1)
    w_in, w_out = w_in[0], w_out[0]

    pack, outgoing = dispatch(decode_heads, ids_row, tokens, w_bcd.T, slices)
    landed = swap(outgoing)
    pack = lax.all_gather(pack, "expert", axis=0, tiled=True)
    own_heads = start // HEADDIM + jnp.arange(heads, dtype=jnp.int32)

    pieces = [landed] + [turn(landed, n, slices, r) for r in range(1, slices)]
    inner = [None] * EXPERTS
    for order in ((7, 6, 5, 4), (3, 2, 1), (0,)):
        if order == (0,):
            weights = prepare(place, own_heads, dt_bias, decay_rate, skip_gain, pack)
            pieces, weights = lax.optimization_barrier((pieces, weights))
        for q, a in zip(order, in_projection(place, pieces, w_in, units, order)):
            inner[q] = a
    x = exchange(inner, n, slices)

    gain = lax.dynamic_slice(norm_gain, (start,), (units,)).reshape(1, units)
    z = swap(scan(place, x, weights, gain, heads), same_slice)

    inverse = 1.0 / lax.dynamic_slice(norm_gain, (place[0] * in_dev,), (in_dev,))
    inverse = inverse.reshape(1, in_dev)
    project = functools.partial(out_projection, place=place, z=z, w_out=w_out)
    sent = []
    for k in range(CHUNKS):
        got = project("send", k, inverse=inverse if k == 0 else None)
        if k == 0:
            squares = [got[1]] + [turn(got[1], n, slices, r) for r in range(1, slices)]
        sent.append([turn(got[0][r - 1], n, slices, r) for r in range(1, slices)])
    done = None
    for k in range(CHUNKS):
        [done] = project("finish", k, squares=squares, parts=sent[k], before=done)
    mixed = collect(ids_row, [swap(done)], slices)

    def picked(head):
        first = head * HEADDIM % in_dev
        parts = [
            lax.dynamic_slice(
                z, ((first + i) // units, z.shape[1] - NS, (first + i) % units), (1, NS, width)
            )
            for i in range(0, HEADDIM, width)
        ]
        return jnp.concatenate(parts, axis=0) if len(parts) > 1 else parts[0]

    want = decode_heads[0]
    chosen = picked(want)
    for r in range(1, slices):
        other = chip * slices + (place[0] + r) % slices
        asked = lax.dynamic_slice(
            pack, (other * tokens.shape[0], 2 * NS + 2 * HEADS + 2), (1, 1)
        )[0, 0].astype(jnp.int32)
        got = turn(picked(asked), n, slices, r)
        lies = want * HEADDIM // in_dev
        chosen = jnp.where((place[0] - lies + slices) % slices == r, got, chosen)
    chosen = chosen.transpose(0, 2, 1).astype(f32)
    return (mixed, chosen.reshape(1, HEADDIM * NS))


def solution(mesh):
    in_specs = (
        P(("groups", "expert"), None),
        P("expert", None, None),
        P("expert", None, None),
        P(),
        P(),
        P(),
        P(),
        P(),
        P(("groups", "expert"), None),
        P("expert"),
    )
    out_specs = (P(("groups", "expert"), None), P(("groups", "expert"), None))
    return jax.shard_map(shards, mesh=mesh, in_specs=in_specs, out_specs=out_specs, check_vma=False)
```

```python
import functools

import jax
import jax.numpy as jnp
from jax import lax
from jax.experimental import pallas as pl
from jax.experimental.pallas import tpu as pltpu
from jax.sharding import PartitionSpec as P

INNER = 4096
HEADDIM = 128
HEADS = 32
NS = 64
EXPERTS = 8
CAP = 24
PAIR = 256
PACK = 256
CHUNKS = 1
VMEM_BYTES = 48 * 1024 * 1024

f32 = jnp.float32
bf16 = jnp.bfloat16


def params(limit=VMEM_BYTES):
    return pltpu.CompilerParams(vmem_limit_bytes=limit)


def mask(condition):
    return condition.astype(f32).astype(bf16)


def iota(shape, dim):
    return lax.broadcasted_iota(jnp.int32, shape, dim)


def route(ids_row):
    rows = ids_row.shape[1]
    ids = jnp.broadcast_to(ids_row.astype(f32), (rows, rows)).T
    onehot = (ids == iota((rows, rows), 1).astype(f32)).astype(f32)
    lower = mask(iota((rows, rows), 1) < iota((rows, rows), 0))
    before = jnp.dot(lower, onehot.astype(bf16), preferred_element_type=f32)
    return ids, jnp.sum(before * onehot, axis=1, keepdims=True)


def fetched(refs, buffers, sems):
    copies = [
        pltpu.make_async_copy(ref, buffer, sems.at[i])
        for i, (ref, buffer) in enumerate(zip(refs, buffers))
    ]
    for copy in copies:
        copy.start()
    for copy in copies:
        copy.wait()


def dispatch_kernel(slices, *refs):
    pack_ref, out_ref = refs[4:6]
    want_ref = refs[0]
    ids_ref, tok_ref, bcd_ref, sems = refs[6:]
    fetched(refs[1:4], refs[6:9], sems)
    rows, width = tok_ref.shape
    depth = width // slices
    ids, slot = route(ids_ref[...])
    pick = mask(ids[:, :1] * CAP + slot == iota((rows, EXPERTS * CAP), 1).astype(f32))
    step = min(512, depth)
    for c in range(0, depth, step):
        got = [
            lax.dot_general(
                pick,
                tok_ref[:, s * depth + c : s * depth + c + step],
                (((0,), (0,)), ((), ())),
                preferred_element_type=f32,
            )
            for s in range(slices)
        ]
        for e in range(EXPERTS):
            piece = jnp.concatenate([g[e * CAP : (e + 1) * CAP] for g in got], axis=0)
            out_ref[e * slices * CAP : (e + 1) * slices * CAP, c : c + step] = piece.astype(bf16)

    across = (((1,), (1,)), ((), ()))
    tok = tok_ref[...]
    pack_ref[:, : 2 * NS] = lax.dot_general(
        tok, bcd_ref[: 2 * NS, :], across, preferred_element_type=f32
    ).astype(bf16)
    steps = bcd_ref[2 * NS : 2 * NS + HEADS, :]
    raw = lax.dot_general(
        tok, jnp.concatenate([steps] * 4, axis=0), across, preferred_element_type=f32
    )
    coarse = raw.astype(bf16).astype(f32)
    lane = iota((rows, 128), 1)
    side = jnp.where(lane < HEADS, coarse, raw - coarse)
    side = jnp.where(lane == 2 * HEADS, ids, jnp.where(lane == 2 * HEADS + 1, slot, side))
    side = jnp.where(lane == 2 * HEADS + 2, want_ref[0].astype(f32), side)
    pack_ref[:, 2 * NS :] = jnp.where(lane < 2 * HEADS + 3, side, 0.0).astype(bf16)


def dispatch(want, ids_row, tokens, bcd, slices):
    rows, width = tokens.shape
    operands = (ids_row, tokens, bcd)
    return pl.pallas_call(
        functools.partial(dispatch_kernel, slices),
        out_shape=(
            jax.ShapeDtypeStruct((rows, PACK), bf16),
            jax.ShapeDtypeStruct((EXPERTS * slices * CAP, width // slices), bf16),
        ),
        in_specs=[pl.BlockSpec(memory_space=pltpu.SMEM)]
        + [pl.BlockSpec(memory_space=pltpu.HBM)] * len(operands),
        scratch_shapes=[pltpu.VMEM(a.shape, a.dtype) for a in operands]
        + [pltpu.SemaphoreType.DMA((len(operands),))],
        compiler_params=params(60 * 1024 * 1024),
        name="dispatch",
    )(want, *operands)


def in_kernel(count, shares, turns, place_ref, *refs):
    rows_refs, w_refs, out_refs = refs[:count], refs[count : 2 * count], refs[2 * count :]
    total = None
    for r in range(count):
        part = jnp.dot(rows_refs[r][...], w_refs[r][...], preferred_element_type=f32)
        total = part if total is None else total + part
    for i, q in enumerate(turns):

        @pl.when(pl.program_id(0) == i)
        def _(i=i, q=q):
            units = out_refs[i].shape[1]
            own = total[:, :units]
            for k in range(1, shares):
                at = (place_ref[1] ^ q) % shares
                own = jnp.where(at == k, total[:, k * units : (k + 1) * units], own)
            out_refs[i][...] = own.astype(bf16)


def in_projection(place, pieces, w_in, units, turns):
    slices = len(pieces)
    rows, depth = pieces[0].shape
    tile = max(128, units)
    shares = tile // units

    def w_spec(r):
        def index(i, place_ref):
            q = sum(jnp.where(i == k, t, 0) for k, t in enumerate(turns))
            return (place_ref[0] - r + slices) % slices, (place_ref[1] ^ q) // shares

        return pl.BlockSpec((depth, tile), index)

    return pl.pallas_call(
        functools.partial(in_kernel, slices, shares, turns),
        out_shape=[jax.ShapeDtypeStruct((rows, units), bf16)] * len(turns),
        grid_spec=pltpu.PrefetchScalarGridSpec(
            num_scalar_prefetch=1,
            grid=(len(turns),),
            in_specs=[pl.BlockSpec((rows, depth), lambda i, place_ref: (0, 0))] * slices
            + [w_spec(r) for r in range(slices)],
            out_specs=[pl.BlockSpec((rows, units), lambda i, place_ref: (0, 0))] * len(turns),
        ),
        compiler_params=params(),
        cost_estimate=pl.CostEstimate(flops=rows, bytes_accessed=rows, transcendentals=0),
        name="in_projection",
    )(place, *pieces, *([w_in] * slices))


def prep_kernel(heads, place_ref, head_ref, bias_ref, rate_ref, skip_ref, pack_ref, w_ref, c_ref, b_ref, a_ref):
    pack = pack_ref[...]
    few = 8
    row = iota((few, PACK), 0)
    lane = iota((few, PACK), 1)
    side = lane - 2 * NS - 2 * HEADS
    choose = ((row == heads) & (side == 0)) | ((row == heads + 1) & (side == 1))
    choose = choose.astype(f32)
    row = iota((few, PAIR), 0)
    rate = bias = jnp.zeros((few, PAIR), f32)
    for h in range(heads):
        at = lane - 2 * NS - head_ref[h]
        choose = jnp.where((iota((few, PACK), 0) == h) & ((at == 0) | (at == HEADS)), 1.0, choose)
        rate = jnp.where(row == h, rate_ref[head_ref[h]], rate)
        bias = jnp.where(row == h, bias_ref[head_ref[h]], bias)
    across = lax.dot_general(
        choose.astype(bf16), pack, (((1,), (1,)), ((), ())), preferred_element_type=f32
    )
    raw = across + bias
    steps_dt = jnp.maximum(raw, 0.0) + jnp.log1p(jnp.exp(-jnp.abs(raw)))
    upto = iota((PAIR, PAIR), 0)
    now = iota((PAIR, PAIR), 1)
    rest = -steps_dt * rate
    split = []
    for _ in range(3):
        split.append(rest.astype(bf16).astype(f32))
        rest = rest - split[-1]
    sums = jnp.dot(
        jnp.concatenate(split + [jnp.zeros_like(rest)], axis=0).astype(bf16),
        mask(upto <= now),
        preferred_element_type=f32,
    )
    running = sums[:few] + sums[few : 2 * few] + sums[2 * few : 3 * few]
    second = iota((1, PAIR), 1) >= PAIR // 2
    turn_of = across[heads : heads + 1].astype(jnp.int32) ^ place_ref[1]
    column = turn_of * (2 * CAP) + across[heads + 1 : heads + 2].astype(jnp.int32)
    column = column + jnp.where(second, CAP, 0)
    slots = 2 * CAP * EXPERTS
    place_t = mask(iota((slots, PAIR), 0) == column)
    down = jnp.concatenate([running] * (128 // few), axis=0).T
    b_rows = pack[:, :NS]
    c_rows = pack[:, NS : 2 * NS]
    scores = lax.dot_general(
        c_rows, b_rows, (((1,), (1,)), ((), ())), preferred_element_type=f32
    )
    causal = upto >= now
    diagonal = upto == now
    b_cols = b_rows.astype(f32).T
    c_wide = c_rows.astype(f32)
    to_place, b_now = [], []
    for h in range(heads):
        run_row = running[h : h + 1]
        run_col = down[:, h : h + 1]
        dt_row = steps_dt[h : h + 1]
        last = run_row[:, PAIR - 1 : PAIR]
        gap = jnp.where(causal, run_col - run_row, 0.0)
        weights = jnp.where(causal, jnp.exp(gap) * scores * dt_row, 0.0)
        weights = weights + jnp.where(diagonal, skip_ref[head_ref[h]], 0.0)
        to_place.append(weights.astype(bf16))
        b_now.append((b_cols * (jnp.exp(last - run_row) * dt_row)).astype(bf16))
        c_now = (c_wide * jnp.exp(run_col)).astype(bf16)
        c_ref[h, 0] = jnp.dot(place_t, c_now, preferred_element_type=f32).astype(bf16)
        a_ref[h, 0] = jnp.broadcast_to(jnp.exp(last), (8, 128))
    together = jnp.concatenate(to_place, axis=1) if heads > 1 else to_place[0]
    half = jnp.dot(place_t, together, preferred_element_type=f32).astype(bf16)
    rows = [half[:, h * PAIR : (h + 1) * PAIR] for h in range(heads)] + b_now
    placed = lax.dot_general(
        jnp.concatenate(rows, axis=0),
        place_t,
        (((1,), (1,)), ((), ())),
        preferred_element_type=f32,
    ).astype(bf16)
    for h in range(heads):
        w_ref[h, 0] = placed[h * slots : (h + 1) * slots]
        below = heads * slots + h * NS
        b_ref[h, 0] = placed[below : below + NS]


def prepare(place, own_heads, bias, rate, skip, pack):
    heads = own_heads.shape[0]
    pairs = pack.shape[0] // PAIR
    slots = 2 * CAP * EXPERTS
    smem = pl.BlockSpec(memory_space=pltpu.SMEM)

    def block(*dims):
        return pl.BlockSpec((heads, 1, *dims), lambda p: (0, p, 0, 0))

    return pl.pallas_call(
        functools.partial(prep_kernel, heads),
        out_shape=(
            jax.ShapeDtypeStruct((heads, pairs, slots, slots), bf16),
            jax.ShapeDtypeStruct((heads, pairs, slots, NS), bf16),
            jax.ShapeDtypeStruct((heads, pairs, NS, slots), bf16),
            jax.ShapeDtypeStruct((heads, pairs, 8, 128), f32),
        ),
        grid=(pairs,),
        in_specs=[smem] * 5 + [pl.BlockSpec((PAIR, PACK), lambda p: (p, 0))],
        out_specs=(block(slots, slots), block(slots, NS), block(NS, slots), block(8, 128)),
        compiler_params=params(),
        cost_estimate=pl.CostEstimate(
            flops=4 * heads * pairs * slots * slots * PAIR,
            bytes_accessed=2 * heads * pairs * slots * slots,
            transcendentals=heads * pairs * PAIR * PAIR,
        ),
        name="scan_weights",
    )(place, own_heads, bias, rate, skip, pack)


def scan_kernel(heads, place_ref, *refs):
    x_refs, refs = refs[:EXPERTS], refs[EXPERTS:]
    w_ref, c_ref, b_ref, a_ref, gain_ref, out_ref, state = refs

    @pl.when(pl.program_id(0) == 0)
    def _():
        state[...] = jnp.zeros_like(state)

    rows = 2 * CAP
    width = state.shape[2]
    steps = w_ref.shape[1]
    for i in range(steps):
        at = slice(i * rows, (i + 1) * rows)
        to = pl.ds(pl.multiple_of((pl.program_id(0) * steps + i) * rows, rows), rows)
        x = jnp.concatenate([x_ref[at, :] for x_ref in x_refs], axis=0)
        y = []
        for h in range(heads):
            x_head = x[:, h * width : (h + 1) * width]
            now = state[h]
            y.append(
                jnp.dot(w_ref[h, i], x_head, preferred_element_type=f32)
                + jnp.dot(c_ref[h, i], now.astype(bf16), preferred_element_type=f32)
            )
            state[h] = now * a_ref[h, i, 0:1, 0:1] + jnp.dot(
                b_ref[h, i], x_head, preferred_element_type=f32
            )
        y = jnp.concatenate(y, axis=1) if heads > 1 else y[0]
        z = (y * gain_ref[...]).astype(bf16)
        for q in range(EXPERTS):
            out_ref[place_ref[1] ^ q, to, :] = z[q * rows : (q + 1) * rows]

    @pl.when(pl.program_id(0) == pl.num_programs(0) - 1)
    def _():
        last = [state[h].astype(bf16) for h in range(heads)]
        last = jnp.concatenate(last, axis=1) if heads > 1 else last[0]
        for j in range(EXPERTS):
            out_ref[j, out_ref.shape[1] - NS :, :] = last


def scan(place, x, weights, gain, heads):
    rows, units = x[0].shape
    width = units // heads
    pairs = rows // (2 * CAP)
    step = 2
    slots = 2 * CAP * EXPERTS

    def block(*dims):
        return pl.BlockSpec((heads, step, *dims), lambda p, place_ref: (0, p, 0, 0))

    return pl.pallas_call(
        functools.partial(scan_kernel, heads),
        out_shape=pltpu.HBM((EXPERTS, rows + NS, units), bf16),
        grid_spec=pltpu.PrefetchScalarGridSpec(
            num_scalar_prefetch=1,
            grid=(pairs // step,),
            in_specs=[pl.BlockSpec((2 * CAP * step, units), lambda p, place_ref: (p, 0))] * EXPERTS
            + [
                block(slots, slots),
                block(slots, NS),
                block(NS, slots),
                block(8, 128),
                pl.BlockSpec((1, units), lambda p, place_ref: (0, 0)),
            ],
            out_specs=pl.BlockSpec(
                (EXPERTS, rows + NS, units), lambda p, place_ref: (0, 0, 0)
            ),
            scratch_shapes=[pltpu.VMEM((heads, NS, width), f32)],
        ),
        compiler_params=pltpu.CompilerParams(vmem_limit_bytes=VMEM_BYTES // 2),
        cost_estimate=pl.CostEstimate(
            flops=2 * heads * pairs * slots * (slots + 2 * NS) * width,
            bytes_accessed=2 * heads * pairs * slots * slots,
            transcendentals=0,
        ),
        name="scan",
    )(place, *x, *weights, gain)


def out_kernel(kind, counted, others, resumed, place_ref, *refs):
    refs = list(refs)

    def take(count):
        got = refs[:count]
        del refs[:count]
        return got

    z_ref, w_ref = take(2)
    inverse_ref = take(1)[0] if counted else None
    squares_refs = take(1 + others) if kind == "finish" else None
    part_refs = take(others) if kind == "finish" else None
    if resumed:
        take(1)
    out_ref = take(1)[0]
    _, rows, units = z_ref.shape
    if counted:

        @pl.when(pl.program_id(0) == 0)
        def _():
            squares = jnp.zeros((rows, units), f32)
            for j in range(EXPERTS):
                z = z_ref[j].astype(f32) * inverse_ref[:, j * units : (j + 1) * units]
                squares = squares + z * z
            refs[0][...] = jnp.sum(squares, axis=1, keepdims=True)

    total = None
    for j in range(EXPERTS):
        part = jnp.dot(
            z_ref[j], w_ref[j * units : (j + 1) * units, :], preferred_element_type=f32
        )
        total = part if total is None else total + part
    if kind == "finish":
        squares = sum(r[...] for r in squares_refs)
        for part in part_refs:
            total = total + part[...].astype(f32)
        out_ref[...] = (total * lax.rsqrt(squares / INNER + 1e-05)).astype(bf16)
    else:
        out_ref[0] = total.astype(bf16)


def out_projection(
    kind, chunk, *, place, z, w_out, inverse=None, squares=(), parts=(), before=None
):
    _, rows, units = z.shape
    rows = rows - NS
    slices = INNER // w_out.shape[0]
    slice_width = w_out.shape[1] // slices
    part = slice_width // CHUNKS
    count, first = (slices - 1, 1) if kind == "send" else (1, 0)
    tile = min(512, part)
    tiles = part // tile
    whole = slice_width // tile
    offset = chunk * tiles

    def column(n, place_ref):
        return (place_ref[0] + first + n // tiles) % slices * whole + offset + n % tiles

    def fixed(*dims):
        return pl.BlockSpec(dims, lambda n, place_ref: (0,) * len(dims))

    operands = [z, w_out]
    specs = [fixed(EXPERTS, rows, units)]
    specs.append(
        pl.BlockSpec((w_out.shape[0], tile), lambda n, place_ref: (0, column(n, place_ref)))
    )
    if inverse is not None:
        operands.append(inverse)
        specs.append(fixed(*inverse.shape))
    operands += [*squares, *parts]
    specs += [fixed(rows, 1)] * len(squares)
    specs += [pl.BlockSpec((rows, tile), lambda n, place_ref: (0, n))] * len(parts)
    aliases = {}
    if before is not None:
        aliases = {1 + len(operands): 0}
        operands.append(before)
        specs.append(pl.BlockSpec(memory_space=pl.ANY))
    if kind == "finish":
        out_shape = [pltpu.HBM((rows, slice_width), bf16)]
        out_specs = [pl.BlockSpec((rows, tile), lambda n, place_ref: (0, offset + n))]
    else:
        out_shape = [jax.ShapeDtypeStruct((count, rows, part), bf16)]
        out_specs = [
            pl.BlockSpec((1, rows, tile), lambda n, place_ref: (n // tiles, 0, n % tiles))
        ]
    if inverse is not None:
        out_shape.append(jax.ShapeDtypeStruct((rows, 1), f32))
        out_specs.append(fixed(rows, 1))
    return pl.pallas_call(
        functools.partial(out_kernel, kind, inverse is not None, len(parts), before is not None),
        out_shape=out_shape,
        grid_spec=pltpu.PrefetchScalarGridSpec(
            num_scalar_prefetch=1, grid=(count * tiles,), in_specs=specs, out_specs=out_specs
        ),
        input_output_aliases=aliases,
        compiler_params=params(),
        cost_estimate=pl.CostEstimate(
            flops=2 * rows * w_out.shape[0] * count * part,
            bytes_accessed=2 * w_out.shape[0] * count * part + 2 * rows * count * part,
            transcendentals=0,
        ),
        name="out_" + kind,
    )(place, *operands)


def collect_kernel(slices, ids_ref, *refs):
    chunk_refs, out_ref = refs[:-1], refs[-1]
    count, part = chunk_refs[0].shape
    rows = ids_ref.shape[1]
    depth = part * len(chunk_refs)
    step = min(512, part)
    ids, slot = route(ids_ref[...])
    at = ids[:, :1] * (slices * CAP) + slot
    lane = iota((rows, count), 1).astype(f32)
    for s in range(slices):
        pick = mask(at + s * CAP == lane)
        for k, rows_ref in enumerate(chunk_refs):
            for c in range(0, part, step):
                start = s * depth + k * part + c
                out_ref[:, start : start + step] = jnp.dot(
                    pick, rows_ref[:, c : c + step], preferred_element_type=f32
                ).astype(bf16)


def collect(ids_row, chunks, slices):
    width = sum(c.shape[1] for c in chunks) * slices
    return pl.pallas_call(
        functools.partial(collect_kernel, slices),
        out_shape=jax.ShapeDtypeStruct((ids_row.shape[1], width), bf16),
        compiler_params=params(),
        name="collect",
    )(ids_row, *chunks)


def turn(a, n, slices, r):
    return lax.ppermute(
        a, "expert", [(d, d // slices * slices + (d + r) % slices) for d in range(n)]
    )


def swap(a, groups=None):
    return lax.all_to_all(
        a, "expert", split_axis=0, concat_axis=0, axis_index_groups=groups, tiled=True
    )


def across(a, q, n, slices):
    pairs = [(d, (d // slices ^ q) * slices + d % slices) for d in range(n)]
    return lax.ppermute(a, "expert", pairs)


def exchange(arrays, n, slices):
    out = list(arrays)
    for q in reversed(range(1, EXPERTS)):
        out[q] = across(arrays[q], q, n, slices)
    return out


def shards(
    tokens, w_in, w_out, w_bcd, dt_bias, decay_rate, skip_gain, norm_gain, expert_ids, decode_heads
):
    n = lax.axis_size("expert")
    slices = n // EXPERTS
    in_dev = w_in.shape[2]
    units = in_dev // EXPERTS
    width = min(HEADDIM, units)
    heads = units // width
    me = lax.axis_index("expert")
    chip = (me // slices).astype(jnp.int32)
    place = jnp.stack([(me % slices).astype(jnp.int32), chip])
    start = place[0] * in_dev + chip * units
    same_slice = [[j * slices + k for j in range(EXPERTS)] for k in range(slices)]
    ids_row = expert_ids.reshape(1, -1)
    w_in, w_out = w_in[0], w_out[0]

    pack, outgoing = dispatch(decode_heads, ids_row, tokens, w_bcd.T, slices)
    landed = swap(outgoing)
    pack = lax.all_gather(pack, "expert", axis=0, tiled=True)
    own_heads = start // HEADDIM + jnp.arange(heads, dtype=jnp.int32)

    pieces = [landed] + [turn(landed, n, slices, r) for r in range(1, slices)]
    inner = [None] * EXPERTS
    for order in ((7, 6), (5, 4, 3), (2, 1), (0,)):
        if order == (0,):
            weights = prepare(place, own_heads, dt_bias, decay_rate, skip_gain, pack)
            pieces, weights = lax.optimization_barrier((pieces, weights))
        for q, a in zip(order, in_projection(place, pieces, w_in, units, order)):
            inner[q] = a
    x = exchange(inner, n, slices)

    gain = lax.dynamic_slice(norm_gain, (start,), (units,)).reshape(1, units)
    z = swap(scan(place, x, weights, gain, heads), same_slice)

    inverse = 1.0 / lax.dynamic_slice(norm_gain, (place[0] * in_dev,), (in_dev,))
    inverse = inverse.reshape(1, in_dev)
    project = functools.partial(out_projection, place=place, z=z, w_out=w_out)
    sent = []
    for k in range(CHUNKS):
        got = project("send", k, inverse=inverse if k == 0 else None)
        if k == 0:
            squares = [got[1]] + [turn(got[1], n, slices, r) for r in range(1, slices)]
        sent.append([turn(got[0][r - 1], n, slices, r) for r in range(1, slices)])
    done = None
    for k in range(CHUNKS):
        [done] = project("finish", k, squares=squares, parts=sent[k], before=done)
    mixed = collect(ids_row, [swap(done)], slices)

    def picked(head):
        first = head * HEADDIM % in_dev
        parts = [
            lax.dynamic_slice(
                z, ((first + i) // units, z.shape[1] - NS, (first + i) % units), (1, NS, width)
            )
            for i in range(0, HEADDIM, width)
        ]
        return jnp.concatenate(parts, axis=0) if len(parts) > 1 else parts[0]

    want = decode_heads[0]
    chosen = picked(want)
    for r in range(1, slices):
        other = chip * slices + (place[0] + r) % slices
        asked = lax.dynamic_slice(
            pack, (other * tokens.shape[0], 2 * NS + 2 * HEADS + 2), (1, 1)
        )[0, 0].astype(jnp.int32)
        got = turn(picked(asked), n, slices, r)
        lies = want * HEADDIM // in_dev
        chosen = jnp.where((place[0] - lies + slices) % slices == r, got, chosen)
    chosen = chosen.transpose(0, 2, 1).astype(f32)
    return (mixed, chosen.reshape(1, HEADDIM * NS))


def solution(mesh):
    in_specs = (
        P(("groups", "expert"), None),
        P("expert", None, None),
        P("expert", None, None),
        P(),
        P(),
        P(),
        P(),
        P(),
        P(("groups", "expert"), None),
        P("expert"),
    )
    out_specs = (P(("groups", "expert"), None), P(("groups", "expert"), None))
    return jax.shard_map(shards, mesh=mesh, in_specs=in_specs, out_specs=out_specs, check_vma=False)
```

```python
import functools

import jax
import jax.numpy as jnp
from jax import lax
from jax.experimental import pallas as pl
from jax.experimental.pallas import tpu as pltpu
from jax.sharding import PartitionSpec as P

INNER = 4096
HEADDIM = 128
HEADS = 32
NS = 64
EXPERTS = 8
CAP = 24
PAIR = 256
PACK = 256
CHUNKS = 1
VMEM_BYTES = 48 * 1024 * 1024

f32 = jnp.float32
bf16 = jnp.bfloat16


def params(limit=VMEM_BYTES):
    return pltpu.CompilerParams(vmem_limit_bytes=limit)


def mask(condition):
    return condition.astype(f32).astype(bf16)


def iota(shape, dim):
    return lax.broadcasted_iota(jnp.int32, shape, dim)


def route(ids_row):
    rows = ids_row.shape[1]
    ids = jnp.broadcast_to(ids_row.astype(f32), (rows, rows)).T
    onehot = (ids == iota((rows, rows), 1).astype(f32)).astype(f32)
    lower = mask(iota((rows, rows), 1) < iota((rows, rows), 0))
    before = jnp.dot(lower, onehot.astype(bf16), preferred_element_type=f32)
    return ids, jnp.sum(before * onehot, axis=1, keepdims=True)


def fetched(refs, buffers, sems):
    copies = [
        pltpu.make_async_copy(ref, buffer, sems.at[i])
        for i, (ref, buffer) in enumerate(zip(refs, buffers))
    ]
    for copy in copies:
        copy.start()
    for copy in copies:
        copy.wait()


def dispatch_kernel(slices, *refs):
    pack_ref, out_ref = refs[4:6]
    want_ref = refs[0]
    ids_ref, tok_ref, bcd_ref, sems = refs[6:]
    fetched(refs[1:4], refs[6:9], sems)
    rows, width = tok_ref.shape
    depth = width // slices
    ids, slot = route(ids_ref[...])
    pick = mask(ids[:, :1] * CAP + slot == iota((rows, EXPERTS * CAP), 1).astype(f32))
    step = min(512, depth)
    for c in range(0, depth, step):
        got = [
            lax.dot_general(
                pick,
                tok_ref[:, s * depth + c : s * depth + c + step],
                (((0,), (0,)), ((), ())),
                preferred_element_type=f32,
            )
            for s in range(slices)
        ]
        for e in range(EXPERTS):
            piece = jnp.concatenate([g[e * CAP : (e + 1) * CAP] for g in got], axis=0)
            out_ref[e * slices * CAP : (e + 1) * slices * CAP, c : c + step] = piece.astype(bf16)

    across = (((1,), (1,)), ((), ()))
    tok = tok_ref[...]
    pack_ref[:, : 2 * NS] = lax.dot_general(
        tok, bcd_ref[: 2 * NS, :], across, preferred_element_type=f32
    ).astype(bf16)
    steps = bcd_ref[2 * NS : 2 * NS + HEADS, :]
    raw = lax.dot_general(
        tok, jnp.concatenate([steps] * 4, axis=0), across, preferred_element_type=f32
    )
    coarse = raw.astype(bf16).astype(f32)
    lane = iota((rows, 128), 1)
    side = jnp.where(lane < HEADS, coarse, raw - coarse)
    side = jnp.where(lane == 2 * HEADS, ids, jnp.where(lane == 2 * HEADS + 1, slot, side))
    side = jnp.where(lane == 2 * HEADS + 2, want_ref[0].astype(f32), side)
    pack_ref[:, 2 * NS :] = jnp.where(lane < 2 * HEADS + 3, side, 0.0).astype(bf16)


def dispatch(want, ids_row, tokens, bcd, slices):
    rows, width = tokens.shape
    operands = (ids_row, tokens, bcd)
    return pl.pallas_call(
        functools.partial(dispatch_kernel, slices),
        out_shape=(
            jax.ShapeDtypeStruct((rows, PACK), bf16),
            jax.ShapeDtypeStruct((EXPERTS * slices * CAP, width // slices), bf16),
        ),
        in_specs=[pl.BlockSpec(memory_space=pltpu.SMEM)]
        + [pl.BlockSpec(memory_space=pltpu.HBM)] * len(operands),
        scratch_shapes=[pltpu.VMEM(a.shape, a.dtype) for a in operands]
        + [pltpu.SemaphoreType.DMA((len(operands),))],
        compiler_params=params(60 * 1024 * 1024),
        name="dispatch",
    )(want, *operands)


def in_kernel(count, shares, turns, place_ref, *refs):
    rows_refs, w_refs, out_refs = refs[:count], refs[count : 2 * count], refs[2 * count :]
    total = None
    for r in range(count):
        part = jnp.dot(rows_refs[r][...], w_refs[r][...], preferred_element_type=f32)
        total = part if total is None else total + part
    for i, q in enumerate(turns):

        @pl.when(pl.program_id(0) == i)
        def _(i=i, q=q):
            units = out_refs[i].shape[1]
            own = total[:, :units]
            for k in range(1, shares):
                at = (place_ref[1] ^ q) % shares
                own = jnp.where(at == k, total[:, k * units : (k + 1) * units], own)
            out_refs[i][...] = own.astype(bf16)


def in_projection(place, pieces, w_in, units, turns):
    slices = len(pieces)
    rows, depth = pieces[0].shape
    tile = max(128, units)
    shares = tile // units

    def w_spec(r):
        def index(i, place_ref):
            q = sum(jnp.where(i == k, t, 0) for k, t in enumerate(turns))
            return (place_ref[0] - r + slices) % slices, (place_ref[1] ^ q) // shares

        return pl.BlockSpec((depth, tile), index)

    return pl.pallas_call(
        functools.partial(in_kernel, slices, shares, turns),
        out_shape=[jax.ShapeDtypeStruct((rows, units), bf16)] * len(turns),
        grid_spec=pltpu.PrefetchScalarGridSpec(
            num_scalar_prefetch=1,
            grid=(len(turns),),
            in_specs=[pl.BlockSpec((rows, depth), lambda i, place_ref: (0, 0))] * slices
            + [w_spec(r) for r in range(slices)],
            out_specs=[pl.BlockSpec((rows, units), lambda i, place_ref: (0, 0))] * len(turns),
        ),
        compiler_params=params(),
        cost_estimate=pl.CostEstimate(flops=rows, bytes_accessed=rows, transcendentals=0),
        name="in_projection",
    )(place, *pieces, *([w_in] * slices))


def prep_kernel(heads, place_ref, head_ref, bias_ref, rate_ref, skip_ref, pack_ref, w_ref, c_ref, b_ref, a_ref):
    pack = pack_ref[...]
    few = 8
    row = iota((few, PACK), 0)
    lane = iota((few, PACK), 1)
    side = lane - 2 * NS - 2 * HEADS
    choose = ((row == heads) & (side == 0)) | ((row == heads + 1) & (side == 1))
    choose = choose.astype(f32)
    row = iota((few, PAIR), 0)
    rate = bias = jnp.zeros((few, PAIR), f32)
    for h in range(heads):
        at = lane - 2 * NS - head_ref[h]
        choose = jnp.where((iota((few, PACK), 0) == h) & ((at == 0) | (at == HEADS)), 1.0, choose)
        rate = jnp.where(row == h, rate_ref[head_ref[h]], rate)
        bias = jnp.where(row == h, bias_ref[head_ref[h]], bias)
    across = lax.dot_general(
        choose.astype(bf16), pack, (((1,), (1,)), ((), ())), preferred_element_type=f32
    )
    raw = across + bias
    steps_dt = jnp.maximum(raw, 0.0) + jnp.log1p(jnp.exp(-jnp.abs(raw)))
    upto = iota((PAIR, PAIR), 0)
    now = iota((PAIR, PAIR), 1)
    rest = -steps_dt * rate
    split = []
    for _ in range(3):
        split.append(rest.astype(bf16).astype(f32))
        rest = rest - split[-1]
    sums = jnp.dot(
        jnp.concatenate(split + [jnp.zeros_like(rest)], axis=0).astype(bf16),
        mask(upto <= now),
        preferred_element_type=f32,
    )
    running = sums[:few] + sums[few : 2 * few] + sums[2 * few : 3 * few]
    second = iota((1, PAIR), 1) >= PAIR // 2
    turn_of = across[heads : heads + 1].astype(jnp.int32) ^ place_ref[1]
    column = turn_of * (2 * CAP) + across[heads + 1 : heads + 2].astype(jnp.int32)
    column = column + jnp.where(second, CAP, 0)
    slots = 2 * CAP * EXPERTS
    place_t = mask(iota((slots, PAIR), 0) == column)
    down = jnp.concatenate([running] * (128 // few), axis=0).T
    b_rows = pack[:, :NS]
    c_rows = pack[:, NS : 2 * NS]
    scores = lax.dot_general(
        c_rows, b_rows, (((1,), (1,)), ((), ())), preferred_element_type=f32
    )
    causal = upto >= now
    diagonal = upto == now
    b_cols = b_rows.astype(f32).T
    c_wide = c_rows.astype(f32)
    to_place, b_now = [], []
    for h in range(heads):
        run_row = running[h : h + 1]
        run_col = down[:, h : h + 1]
        dt_row = steps_dt[h : h + 1]
        last = run_row[:, PAIR - 1 : PAIR]
        gap = jnp.where(causal, run_col - run_row, 0.0)
        weights = jnp.where(causal, jnp.exp(gap) * scores * dt_row, 0.0)
        weights = weights + jnp.where(diagonal, skip_ref[head_ref[h]], 0.0)
        to_place.append(weights.astype(bf16))
        b_now.append((b_cols * (jnp.exp(last - run_row) * dt_row)).astype(bf16))
        c_now = (c_wide * jnp.exp(run_col)).astype(bf16)
        c_ref[h, 0] = jnp.dot(place_t, c_now, preferred_element_type=f32).astype(bf16)
        a_ref[h, 0] = jnp.broadcast_to(jnp.exp(last), (8, 128))
    together = jnp.concatenate(to_place, axis=1) if heads > 1 else to_place[0]
    half = jnp.dot(place_t, together, preferred_element_type=f32).astype(bf16)
    rows = [half[:, h * PAIR : (h + 1) * PAIR] for h in range(heads)] + b_now
    placed = lax.dot_general(
        jnp.concatenate(rows, axis=0),
        place_t,
        (((1,), (1,)), ((), ())),
        preferred_element_type=f32,
    ).astype(bf16)
    for h in range(heads):
        w_ref[h, 0] = placed[h * slots : (h + 1) * slots]
        below = heads * slots + h * NS
        b_ref[h, 0] = placed[below : below + NS]


def prepare(place, own_heads, bias, rate, skip, pack):
    heads = own_heads.shape[0]
    pairs = pack.shape[0] // PAIR
    slots = 2 * CAP * EXPERTS
    smem = pl.BlockSpec(memory_space=pltpu.SMEM)

    def block(*dims):
        return pl.BlockSpec((heads, 1, *dims), lambda p: (0, p, 0, 0))

    return pl.pallas_call(
        functools.partial(prep_kernel, heads),
        out_shape=(
            jax.ShapeDtypeStruct((heads, pairs, slots, slots), bf16),
            jax.ShapeDtypeStruct((heads, pairs, slots, NS), bf16),
            jax.ShapeDtypeStruct((heads, pairs, NS, slots), bf16),
            jax.ShapeDtypeStruct((heads, pairs, 8, 128), f32),
        ),
        grid=(pairs,),
        in_specs=[smem] * 5 + [pl.BlockSpec((PAIR, PACK), lambda p: (p, 0))],
        out_specs=(block(slots, slots), block(slots, NS), block(NS, slots), block(8, 128)),
        compiler_params=params(56 * 1024 * 1024),
        cost_estimate=pl.CostEstimate(
            flops=4 * heads * pairs * slots * slots * PAIR,
            bytes_accessed=2 * heads * pairs * slots * slots,
            transcendentals=heads * pairs * PAIR * PAIR,
        ),
        name="scan_weights",
    )(place, own_heads, bias, rate, skip, pack)


def scan_kernel(heads, place_ref, *refs):
    x_refs, refs = refs[:EXPERTS], refs[EXPERTS:]
    w_ref, c_ref, b_ref, a_ref, gain_ref, out_ref, state = refs

    @pl.when(pl.program_id(0) == 0)
    def _():
        state[...] = jnp.zeros_like(state)

    rows = 2 * CAP
    width = state.shape[2]
    steps = w_ref.shape[1]
    for i in range(steps):
        at = slice(i * rows, (i + 1) * rows)
        to = pl.ds(pl.multiple_of((pl.program_id(0) * steps + i) * rows, rows), rows)
        x = jnp.concatenate([x_ref[at, :] for x_ref in x_refs], axis=0)
        y = []
        for h in range(heads):
            x_head = x[:, h * width : (h + 1) * width]
            now = state[h]
            y.append(
                jnp.dot(w_ref[h, i], x_head, preferred_element_type=f32)
                + jnp.dot(c_ref[h, i], now.astype(bf16), preferred_element_type=f32)
            )
            state[h] = now * a_ref[h, i, 0:1, 0:1] + jnp.dot(
                b_ref[h, i], x_head, preferred_element_type=f32
            )
        y = jnp.concatenate(y, axis=1) if heads > 1 else y[0]
        z = (y * gain_ref[...]).astype(bf16)
        for q in range(EXPERTS):
            out_ref[place_ref[1] ^ q, to, :] = z[q * rows : (q + 1) * rows]

    @pl.when(pl.program_id(0) == pl.num_programs(0) - 1)
    def _():
        last = [state[h].astype(bf16) for h in range(heads)]
        last = jnp.concatenate(last, axis=1) if heads > 1 else last[0]
        for j in range(EXPERTS):
            out_ref[j, out_ref.shape[1] - NS :, :] = last


def scan(place, x, weights, gain, heads):
    rows, units = x[0].shape
    width = units // heads
    pairs = rows // (2 * CAP)
    step = 2
    slots = 2 * CAP * EXPERTS

    def block(*dims):
        return pl.BlockSpec((heads, step, *dims), lambda p, place_ref: (0, p, 0, 0))

    return pl.pallas_call(
        functools.partial(scan_kernel, heads),
        out_shape=pltpu.HBM((EXPERTS, rows + NS, units), bf16),
        grid_spec=pltpu.PrefetchScalarGridSpec(
            num_scalar_prefetch=1,
            grid=(pairs // step,),
            in_specs=[pl.BlockSpec((2 * CAP * step, units), lambda p, place_ref: (p, 0))] * EXPERTS
            + [
                block(slots, slots),
                block(slots, NS),
                block(NS, slots),
                block(8, 128),
                pl.BlockSpec((1, units), lambda p, place_ref: (0, 0)),
            ],
            out_specs=pl.BlockSpec(
                (EXPERTS, rows + NS, units), lambda p, place_ref: (0, 0, 0)
            ),
            scratch_shapes=[pltpu.VMEM((heads, NS, width), f32)],
        ),
        compiler_params=pltpu.CompilerParams(vmem_limit_bytes=VMEM_BYTES // 2),
        cost_estimate=pl.CostEstimate(
            flops=2 * heads * pairs * slots * (slots + 2 * NS) * width,
            bytes_accessed=2 * heads * pairs * slots * slots,
            transcendentals=0,
        ),
        name="scan",
    )(place, *x, *weights, gain)


def out_kernel(kind, counted, others, resumed, place_ref, *refs):
    refs = list(refs)

    def take(count):
        got = refs[:count]
        del refs[:count]
        return got

    z_ref, w_ref = take(2)
    inverse_ref = take(1)[0] if counted else None
    squares_refs = take(1 + others) if kind == "finish" else None
    part_refs = take(others) if kind == "finish" else None
    if resumed:
        take(1)
    out_ref = take(1)[0]
    _, rows, units = z_ref.shape
    if counted:

        @pl.when(pl.program_id(0) == 0)
        def _():
            squares = jnp.zeros((rows, units), f32)
            for j in range(EXPERTS):
                z = z_ref[j].astype(f32) * inverse_ref[:, j * units : (j + 1) * units]
                squares = squares + z * z
            refs[0][...] = jnp.sum(squares, axis=1, keepdims=True)

    total = None
    for j in range(EXPERTS):
        part = jnp.dot(
            z_ref[j], w_ref[j * units : (j + 1) * units, :], preferred_element_type=f32
        )
        total = part if total is None else total + part
    if kind == "finish":
        squares = sum(r[...] for r in squares_refs)
        for part in part_refs:
            total = total + part[...].astype(f32)
        out_ref[...] = (total * lax.rsqrt(squares / INNER + 1e-05)).astype(bf16)
    else:
        out_ref[0] = total.astype(bf16)


def out_projection(
    kind, chunk, *, place, z, w_out, inverse=None, squares=(), parts=(), before=None
):
    _, rows, units = z.shape
    rows = rows - NS
    slices = INNER // w_out.shape[0]
    slice_width = w_out.shape[1] // slices
    part = slice_width // CHUNKS
    count, first = (slices - 1, 1) if kind == "send" else (1, 0)
    tile = min(512, part)
    tiles = part // tile
    whole = slice_width // tile
    offset = chunk * tiles

    def column(n, place_ref):
        return (place_ref[0] + first + n // tiles) % slices * whole + offset + n % tiles

    def fixed(*dims):
        return pl.BlockSpec(dims, lambda n, place_ref: (0,) * len(dims))

    operands = [z, w_out]
    specs = [fixed(EXPERTS, rows, units)]
    specs.append(
        pl.BlockSpec((w_out.shape[0], tile), lambda n, place_ref: (0, column(n, place_ref)))
    )
    if inverse is not None:
        operands.append(inverse)
        specs.append(fixed(*inverse.shape))
    operands += [*squares, *parts]
    specs += [fixed(rows, 1)] * len(squares)
    specs += [pl.BlockSpec((rows, tile), lambda n, place_ref: (0, n))] * len(parts)
    aliases = {}
    if before is not None:
        aliases = {1 + len(operands): 0}
        operands.append(before)
        specs.append(pl.BlockSpec(memory_space=pl.ANY))
    if kind == "finish":
        out_shape = [pltpu.HBM((rows, slice_width), bf16)]
        out_specs = [pl.BlockSpec((rows, tile), lambda n, place_ref: (0, offset + n))]
    else:
        out_shape = [jax.ShapeDtypeStruct((count, rows, part), bf16)]
        out_specs = [
            pl.BlockSpec((1, rows, tile), lambda n, place_ref: (n // tiles, 0, n % tiles))
        ]
    if inverse is not None:
        out_shape.append(jax.ShapeDtypeStruct((rows, 1), f32))
        out_specs.append(fixed(rows, 1))
    return pl.pallas_call(
        functools.partial(out_kernel, kind, inverse is not None, len(parts), before is not None),
        out_shape=out_shape,
        grid_spec=pltpu.PrefetchScalarGridSpec(
            num_scalar_prefetch=1, grid=(count * tiles,), in_specs=specs, out_specs=out_specs
        ),
        input_output_aliases=aliases,
        compiler_params=params(),
        cost_estimate=pl.CostEstimate(
            flops=2 * rows * w_out.shape[0] * count * part,
            bytes_accessed=2 * w_out.shape[0] * count * part + 2 * rows * count * part,
            transcendentals=0,
        ),
        name="out_" + kind,
    )(place, *operands)


def collect_kernel(slices, ids_ref, *refs):
    chunk_refs, out_ref = refs[:-1], refs[-1]
    count, part = chunk_refs[0].shape
    rows = ids_ref.shape[1]
    depth = part * len(chunk_refs)
    step = min(512, part)
    ids, slot = route(ids_ref[...])
    at = ids[:, :1] * (slices * CAP) + slot
    lane = iota((rows, count), 1).astype(f32)
    for s in range(slices):
        pick = mask(at + s * CAP == lane)
        for k, rows_ref in enumerate(chunk_refs):
            for c in range(0, part, step):
                start = s * depth + k * part + c
                out_ref[:, start : start + step] = jnp.dot(
                    pick, rows_ref[:, c : c + step], preferred_element_type=f32
                ).astype(bf16)


def collect(ids_row, chunks, slices):
    width = sum(c.shape[1] for c in chunks) * slices
    return pl.pallas_call(
        functools.partial(collect_kernel, slices),
        out_shape=jax.ShapeDtypeStruct((ids_row.shape[1], width), bf16),
        compiler_params=params(),
        name="collect",
    )(ids_row, *chunks)


def turn(a, n, slices, r):
    return lax.ppermute(
        a, "expert", [(d, d // slices * slices + (d + r) % slices) for d in range(n)]
    )


def swap(a, groups=None):
    return lax.all_to_all(
        a, "expert", split_axis=0, concat_axis=0, axis_index_groups=groups, tiled=True
    )


def across(a, q, n, slices):
    pairs = [(d, (d // slices ^ q) * slices + d % slices) for d in range(n)]
    return lax.ppermute(a, "expert", pairs)


def exchange(arrays, n, slices):
    out = list(arrays)
    for q in reversed(range(1, EXPERTS)):
        out[q] = across(arrays[q], q, n, slices)
    return out


def shards(
    tokens, w_in, w_out, w_bcd, dt_bias, decay_rate, skip_gain, norm_gain, expert_ids, decode_heads
):
    n = lax.axis_size("expert")
    slices = n // EXPERTS
    in_dev = w_in.shape[2]
    units = in_dev // EXPERTS
    width = min(HEADDIM, units)
    heads = units // width
    me = lax.axis_index("expert")
    chip = (me // slices).astype(jnp.int32)
    place = jnp.stack([(me % slices).astype(jnp.int32), chip])
    start = place[0] * in_dev + chip * units
    same_slice = [[j * slices + k for j in range(EXPERTS)] for k in range(slices)]
    ids_row = expert_ids.reshape(1, -1)
    w_in, w_out = w_in[0], w_out[0]

    pack, outgoing = dispatch(decode_heads, ids_row, tokens, w_bcd.T, slices)
    landed = swap(outgoing)
    pack = lax.all_gather(pack, "expert", axis=0, tiled=True)
    own_heads = start // HEADDIM + jnp.arange(heads, dtype=jnp.int32)

    pieces = [landed] + [turn(landed, n, slices, r) for r in range(1, slices)]
    inner = [None] * EXPERTS
    for order in ((7, 6), (5, 4, 3), (2, 1), (0,)):
        if order == (0,):
            weights = prepare(place, own_heads, dt_bias, decay_rate, skip_gain, pack)
            pieces, weights = lax.optimization_barrier((pieces, weights))
        for q, a in zip(order, in_projection(place, pieces, w_in, units, order)):
            inner[q] = a
    x = exchange(inner, n, slices)

    gain = lax.dynamic_slice(norm_gain, (start,), (units,)).reshape(1, units)
    z = swap(scan(place, x, weights, gain, heads), same_slice)

    inverse = 1.0 / lax.dynamic_slice(norm_gain, (place[0] * in_dev,), (in_dev,))
    inverse = inverse.reshape(1, in_dev)
    project = functools.partial(out_projection, place=place, z=z, w_out=w_out)
    sent = []
    for k in range(CHUNKS):
        got = project("send", k, inverse=inverse if k == 0 else None)
        if k == 0:
            squares = [got[1]] + [turn(got[1], n, slices, r) for r in range(1, slices)]
        sent.append([turn(got[0][r - 1], n, slices, r) for r in range(1, slices)])
    done = None
    for k in range(CHUNKS):
        [done] = project("finish", k, squares=squares, parts=sent[k], before=done)
    mixed = collect(ids_row, [swap(done)], slices)

    def picked(head):
        first = head * HEADDIM % in_dev
        parts = [
            lax.dynamic_slice(
                z, ((first + i) // units, z.shape[1] - NS, (first + i) % units), (1, NS, width)
            )
            for i in range(0, HEADDIM, width)
        ]
        return jnp.concatenate(parts, axis=0) if len(parts) > 1 else parts[0]

    want = decode_heads[0]
    chosen = picked(want)
    for r in range(1, slices):
        other = chip * slices + (place[0] + r) % slices
        asked = lax.dynamic_slice(
            pack, (other * tokens.shape[0], 2 * NS + 2 * HEADS + 2), (1, 1)
        )[0, 0].astype(jnp.int32)
        got = turn(picked(asked), n, slices, r)
        lies = want * HEADDIM // in_dev
        chosen = jnp.where((place[0] - lies + slices) % slices == r, got, chosen)
    chosen = chosen.transpose(0, 2, 1).astype(f32)
    return (mixed, chosen.reshape(1, HEADDIM * NS))


def solution(mesh):
    in_specs = (
        P(("groups", "expert"), None),
        P("expert", None, None),
        P("expert", None, None),
        P(),
        P(),
        P(),
        P(),
        P(),
        P(("groups", "expert"), None),
        P("expert"),
    )
    out_specs = (P(("groups", "expert"), None), P(("groups", "expert"), None))
    return jax.shard_map(shards, mesh=mesh, in_specs=in_specs, out_specs=out_specs, check_vma=False)
```

```python
import functools

import jax
import jax.numpy as jnp
from jax import lax
from jax.experimental import pallas as pl
from jax.experimental.pallas import tpu as pltpu
from jax.sharding import PartitionSpec as P

INNER = 4096
HEADDIM = 128
HEADS = 32
NS = 64
EXPERTS = 8
CAP = 24
PAIR = 256
PACK = 256
CHUNKS = 1
VMEM_BYTES = 48 * 1024 * 1024

f32 = jnp.float32
bf16 = jnp.bfloat16


def params(limit=VMEM_BYTES):
    return pltpu.CompilerParams(vmem_limit_bytes=limit)


def mask(condition):
    return condition.astype(f32).astype(bf16)


def iota(shape, dim):
    return lax.broadcasted_iota(jnp.int32, shape, dim)


def route(ids_row):
    rows = ids_row.shape[1]
    ids = jnp.broadcast_to(ids_row.astype(f32), (rows, rows)).T
    onehot = (ids == iota((rows, rows), 1).astype(f32)).astype(f32)
    lower = mask(iota((rows, rows), 1) < iota((rows, rows), 0))
    before = jnp.dot(lower, onehot.astype(bf16), preferred_element_type=f32)
    return ids, jnp.sum(before * onehot, axis=1, keepdims=True)


def fetched(refs, buffers, sems):
    copies = [
        pltpu.make_async_copy(ref, buffer, sems.at[i])
        for i, (ref, buffer) in enumerate(zip(refs, buffers))
    ]
    for copy in copies:
        copy.start()
    for copy in copies:
        copy.wait()


def dispatch_kernel(slices, *refs):
    pack_ref, out_ref = refs[4:6]
    want_ref = refs[0]
    ids_ref, tok_ref, bcd_ref, sems = refs[6:]
    fetched(refs[1:4], refs[6:9], sems)
    rows, width = tok_ref.shape
    depth = width // slices
    ids, slot = route(ids_ref[...])
    pick = mask(ids[:, :1] * CAP + slot == iota((rows, EXPERTS * CAP), 1).astype(f32))
    step = min(512, depth)
    for c in range(0, depth, step):
        got = [
            lax.dot_general(
                pick,
                tok_ref[:, s * depth + c : s * depth + c + step],
                (((0,), (0,)), ((), ())),
                preferred_element_type=f32,
            )
            for s in range(slices)
        ]
        for e in range(EXPERTS):
            piece = jnp.concatenate([g[e * CAP : (e + 1) * CAP] for g in got], axis=0)
            out_ref[e * slices * CAP : (e + 1) * slices * CAP, c : c + step] = piece.astype(bf16)

    across = (((1,), (1,)), ((), ()))
    tok = tok_ref[...]
    pack_ref[:, : 2 * NS] = lax.dot_general(
        tok, bcd_ref[: 2 * NS, :], across, preferred_element_type=f32
    ).astype(bf16)
    steps = bcd_ref[2 * NS : 2 * NS + HEADS, :]
    raw = lax.dot_general(
        tok, jnp.concatenate([steps] * 4, axis=0), across, preferred_element_type=f32
    )
    coarse = raw.astype(bf16).astype(f32)
    lane = iota((rows, 128), 1)
    side = jnp.where(lane < HEADS, coarse, raw - coarse)
    side = jnp.where(lane == 2 * HEADS, ids, jnp.where(lane == 2 * HEADS + 1, slot, side))
    side = jnp.where(lane == 2 * HEADS + 2, want_ref[0].astype(f32), side)
    pack_ref[:, 2 * NS :] = jnp.where(lane < 2 * HEADS + 3, side, 0.0).astype(bf16)


def dispatch(want, ids_row, tokens, bcd, slices):
    rows, width = tokens.shape
    operands = (ids_row, tokens, bcd)
    return pl.pallas_call(
        functools.partial(dispatch_kernel, slices),
        out_shape=(
            jax.ShapeDtypeStruct((rows, PACK), bf16),
            jax.ShapeDtypeStruct((EXPERTS * slices * CAP, width // slices), bf16),
        ),
        in_specs=[pl.BlockSpec(memory_space=pltpu.SMEM)]
        + [pl.BlockSpec(memory_space=pltpu.HBM)] * len(operands),
        scratch_shapes=[pltpu.VMEM(a.shape, a.dtype) for a in operands]
        + [pltpu.SemaphoreType.DMA((len(operands),))],
        compiler_params=params(60 * 1024 * 1024),
        name="dispatch",
    )(want, *operands)


def in_kernel(count, shares, turns, place_ref, *refs):
    rows_refs, w_refs, out_refs = refs[:count], refs[count : 2 * count], refs[2 * count :]
    total = None
    for r in range(count):
        part = jnp.dot(rows_refs[r][...], w_refs[r][...], preferred_element_type=f32)
        total = part if total is None else total + part
    for i, q in enumerate(turns):

        @pl.when(pl.program_id(0) == i)
        def _(i=i, q=q):
            units = out_refs[i].shape[1]
            own = total[:, :units]
            for k in range(1, shares):
                at = (place_ref[1] ^ q) % shares
                own = jnp.where(at == k, total[:, k * units : (k + 1) * units], own)
            out_refs[i][...] = own.astype(bf16)


def in_projection(place, pieces, w_in, units, turns):
    slices = len(pieces)
    rows, depth = pieces[0].shape
    tile = max(128, units)
    shares = tile // units

    def w_spec(r):
        def index(i, place_ref):
            q = sum(jnp.where(i == k, t, 0) for k, t in enumerate(turns))
            return (place_ref[0] - r + slices) % slices, (place_ref[1] ^ q) // shares

        return pl.BlockSpec((depth, tile), index)

    return pl.pallas_call(
        functools.partial(in_kernel, slices, shares, turns),
        out_shape=[jax.ShapeDtypeStruct((rows, units), bf16)] * len(turns),
        grid_spec=pltpu.PrefetchScalarGridSpec(
            num_scalar_prefetch=1,
            grid=(len(turns),),
            in_specs=[pl.BlockSpec((rows, depth), lambda i, place_ref: (0, 0))] * slices
            + [w_spec(r) for r in range(slices)],
            out_specs=[pl.BlockSpec((rows, units), lambda i, place_ref: (0, 0))] * len(turns),
        ),
        compiler_params=params(),
        cost_estimate=pl.CostEstimate(flops=rows, bytes_accessed=rows, transcendentals=0),
        name="in_projection",
    )(place, *pieces, *([w_in] * slices))


def prep_kernel(heads, place_ref, head_ref, bias_ref, rate_ref, skip_ref, pack_ref, w_ref, c_ref, b_ref, a_ref):
    pack = pack_ref[...]
    few = 8
    row = iota((few, PACK), 0)
    lane = iota((few, PACK), 1)
    side = lane - 2 * NS - 2 * HEADS
    choose = ((row == heads) & (side == 0)) | ((row == heads + 1) & (side == 1))
    choose = choose.astype(f32)
    row = iota((few, PAIR), 0)
    rate = bias = jnp.zeros((few, PAIR), f32)
    for h in range(heads):
        at = lane - 2 * NS - head_ref[h]
        choose = jnp.where((iota((few, PACK), 0) == h) & ((at == 0) | (at == HEADS)), 1.0, choose)
        rate = jnp.where(row == h, rate_ref[head_ref[h]], rate)
        bias = jnp.where(row == h, bias_ref[head_ref[h]], bias)
    across = lax.dot_general(
        choose.astype(bf16), pack, (((1,), (1,)), ((), ())), preferred_element_type=f32
    )
    raw = across + bias
    steps_dt = jnp.maximum(raw, 0.0) + jnp.log1p(jnp.exp(-jnp.abs(raw)))
    upto = iota((PAIR, PAIR), 0)
    now = iota((PAIR, PAIR), 1)
    rest = -steps_dt * rate
    split = []
    for _ in range(3):
        split.append(rest.astype(bf16).astype(f32))
        rest = rest - split[-1]
    sums = jnp.dot(
        jnp.concatenate(split + [jnp.zeros_like(rest)], axis=0).astype(bf16),
        mask(upto <= now),
        preferred_element_type=f32,
    )
    running = sums[:few] + sums[few : 2 * few] + sums[2 * few : 3 * few]
    second = iota((1, PAIR), 1) >= PAIR // 2
    turn_of = across[heads : heads + 1].astype(jnp.int32) ^ place_ref[1]
    column = turn_of * (2 * CAP) + across[heads + 1 : heads + 2].astype(jnp.int32)
    column = column + jnp.where(second, CAP, 0)
    slots = 2 * CAP * EXPERTS
    place_t = mask(iota((slots, PAIR), 0) == column)
    down = jnp.concatenate([running] * (128 // few), axis=0).T
    b_rows = pack[:, :NS]
    c_rows = pack[:, NS : 2 * NS]
    scores = lax.dot_general(
        c_rows, b_rows, (((1,), (1,)), ((), ())), preferred_element_type=f32
    )
    causal = upto >= now
    diagonal = upto == now
    b_cols = b_rows.astype(f32).T
    c_wide = c_rows.astype(f32)
    to_place, b_now = [], []
    for h in range(heads):
        run_row = running[h : h + 1]
        run_col = down[:, h : h + 1]
        dt_row = steps_dt[h : h + 1]
        last = run_row[:, PAIR - 1 : PAIR]
        gap = jnp.where(causal, run_col - run_row, 0.0)
        weights = jnp.where(causal, jnp.exp(gap) * scores * dt_row, 0.0)
        weights = weights + jnp.where(diagonal, skip_ref[head_ref[h]], 0.0)
        to_place.append(weights.astype(bf16))
        b_now.append((b_cols * (jnp.exp(last - run_row) * dt_row)).astype(bf16))
        c_now = (c_wide * jnp.exp(run_col)).astype(bf16)
        c_ref[h, 0] = jnp.dot(place_t, c_now, preferred_element_type=f32).astype(bf16)
        a_ref[h, 0] = jnp.broadcast_to(jnp.exp(last), (8, 128))
    together = jnp.concatenate(to_place, axis=1) if heads > 1 else to_place[0]
    half = jnp.dot(place_t, together, preferred_element_type=f32).astype(bf16)
    rows = [half[:, h * PAIR : (h + 1) * PAIR] for h in range(heads)] + b_now
    placed = lax.dot_general(
        jnp.concatenate(rows, axis=0),
        place_t,
        (((1,), (1,)), ((), ())),
        preferred_element_type=f32,
    ).astype(bf16)
    for h in range(heads):
        w_ref[h, 0] = placed[h * slots : (h + 1) * slots]
        below = heads * slots + h * NS
        b_ref[h, 0] = placed[below : below + NS]


def prepare(place, own_heads, bias, rate, skip, pack):
    heads = own_heads.shape[0]
    pairs = pack.shape[0] // PAIR
    slots = 2 * CAP * EXPERTS
    smem = pl.BlockSpec(memory_space=pltpu.SMEM)

    def block(*dims):
        return pl.BlockSpec((heads, 1, *dims), lambda p: (0, p, 0, 0))

    return pl.pallas_call(
        functools.partial(prep_kernel, heads),
        out_shape=(
            jax.ShapeDtypeStruct((heads, pairs, slots, slots), bf16),
            jax.ShapeDtypeStruct((heads, pairs, slots, NS), bf16),
            jax.ShapeDtypeStruct((heads, pairs, NS, slots), bf16),
            jax.ShapeDtypeStruct((heads, pairs, 8, 128), f32),
        ),
        grid=(pairs,),
        in_specs=[smem] * 5 + [pl.BlockSpec((PAIR, PACK), lambda p: (p, 0))],
        out_specs=(block(slots, slots), block(slots, NS), block(NS, slots), block(8, 128)),
        compiler_params=params(56 * 1024 * 1024),
        cost_estimate=pl.CostEstimate(
            flops=4 * heads * pairs * slots * slots * PAIR,
            bytes_accessed=2 * heads * pairs * slots * slots,
            transcendentals=heads * pairs * PAIR * PAIR,
        ),
        name="scan_weights",
    )(place, own_heads, bias, rate, skip, pack)


def scan_kernel(heads, place_ref, *refs):
    x_refs, refs = refs[:EXPERTS], refs[EXPERTS:]
    w_ref, c_ref, b_ref, a_ref, gain_ref, out_ref, state = refs

    @pl.when(pl.program_id(0) == 0)
    def _():
        state[...] = jnp.zeros_like(state)

    rows = 2 * CAP
    width = state.shape[2]
    steps = w_ref.shape[1]
    for i in range(steps):
        at = slice(i * rows, (i + 1) * rows)
        to = pl.ds(pl.multiple_of((pl.program_id(0) * steps + i) * rows, rows), rows)
        x = jnp.concatenate([x_ref[at, :] for x_ref in x_refs], axis=0)
        y = []
        for h in range(heads):
            x_head = x[:, h * width : (h + 1) * width]
            now = state[h]
            y.append(
                jnp.dot(w_ref[h, i], x_head, preferred_element_type=f32)
                + jnp.dot(c_ref[h, i], now.astype(bf16), preferred_element_type=f32)
            )
            state[h] = now * a_ref[h, i, 0:1, 0:1] + jnp.dot(
                b_ref[h, i], x_head, preferred_element_type=f32
            )
        y = jnp.concatenate(y, axis=1) if heads > 1 else y[0]
        z = (y * gain_ref[...]).astype(bf16)
        for q in range(EXPERTS):
            out_ref[place_ref[1] ^ q, to, :] = z[q * rows : (q + 1) * rows]

    @pl.when(pl.program_id(0) == pl.num_programs(0) - 1)
    def _():
        last = [state[h].astype(bf16) for h in range(heads)]
        last = jnp.concatenate(last, axis=1) if heads > 1 else last[0]
        for j in range(EXPERTS):
            out_ref[j, out_ref.shape[1] - NS :, :] = last


def scan(place, x, weights, gain, heads):
    rows, units = x[0].shape
    width = units // heads
    pairs = rows // (2 * CAP)
    step = 4
    slots = 2 * CAP * EXPERTS

    def block(*dims):
        return pl.BlockSpec((heads, step, *dims), lambda p, place_ref: (0, p, 0, 0))

    return pl.pallas_call(
        functools.partial(scan_kernel, heads),
        out_shape=pltpu.HBM((EXPERTS, rows + NS, units), bf16),
        grid_spec=pltpu.PrefetchScalarGridSpec(
            num_scalar_prefetch=1,
            grid=(pairs // step,),
            in_specs=[pl.BlockSpec((2 * CAP * step, units), lambda p, place_ref: (p, 0))] * EXPERTS
            + [
                block(slots, slots),
                block(slots, NS),
                block(NS, slots),
                block(8, 128),
                pl.BlockSpec((1, units), lambda p, place_ref: (0, 0)),
            ],
            out_specs=pl.BlockSpec(
                (EXPERTS, rows + NS, units), lambda p, place_ref: (0, 0, 0)
            ),
            scratch_shapes=[pltpu.VMEM((heads, NS, width), f32)],
        ),
        compiler_params=pltpu.CompilerParams(vmem_limit_bytes=VMEM_BYTES // 2),
        cost_estimate=pl.CostEstimate(
            flops=2 * heads * pairs * slots * (slots + 2 * NS) * width,
            bytes_accessed=2 * heads * pairs * slots * slots,
            transcendentals=0,
        ),
        name="scan",
    )(place, *x, *weights, gain)


def out_kernel(kind, counted, others, resumed, place_ref, *refs):
    refs = list(refs)

    def take(count):
        got = refs[:count]
        del refs[:count]
        return got

    z_ref, w_ref = take(2)
    inverse_ref = take(1)[0] if counted else None
    squares_refs = take(1 + others) if kind == "finish" else None
    part_refs = take(others) if kind == "finish" else None
    if resumed:
        take(1)
    out_ref = take(1)[0]
    _, rows, units = z_ref.shape
    if counted:

        @pl.when(pl.program_id(0) == 0)
        def _():
            squares = jnp.zeros((rows, units), f32)
            for j in range(EXPERTS):
                z = z_ref[j].astype(f32) * inverse_ref[:, j * units : (j + 1) * units]
                squares = squares + z * z
            refs[0][...] = jnp.sum(squares, axis=1, keepdims=True)

    total = None
    for j in range(EXPERTS):
        part = jnp.dot(
            z_ref[j], w_ref[j * units : (j + 1) * units, :], preferred_element_type=f32
        )
        total = part if total is None else total + part
    if kind == "finish":
        squares = sum(r[...] for r in squares_refs)
        for part in part_refs:
            total = total + part[...].astype(f32)
        out_ref[...] = (total * lax.rsqrt(squares / INNER + 1e-05)).astype(bf16)
    else:
        out_ref[0] = total.astype(bf16)


def out_projection(
    kind, chunk, *, place, z, w_out, inverse=None, squares=(), parts=(), before=None
):
    _, rows, units = z.shape
    rows = rows - NS
    slices = INNER // w_out.shape[0]
    slice_width = w_out.shape[1] // slices
    part = slice_width // CHUNKS
    count, first = (slices - 1, 1) if kind == "send" else (1, 0)
    tile = min(512, part)
    tiles = part // tile
    whole = slice_width // tile
    offset = chunk * tiles

    def column(n, place_ref):
        return (place_ref[0] + first + n // tiles) % slices * whole + offset + n % tiles

    def fixed(*dims):
        return pl.BlockSpec(dims, lambda n, place_ref: (0,) * len(dims))

    operands = [z, w_out]
    specs = [fixed(EXPERTS, rows, units)]
    specs.append(
        pl.BlockSpec((w_out.shape[0], tile), lambda n, place_ref: (0, column(n, place_ref)))
    )
    if inverse is not None:
        operands.append(inverse)
        specs.append(fixed(*inverse.shape))
    operands += [*squares, *parts]
    specs += [fixed(rows, 1)] * len(squares)
    specs += [pl.BlockSpec((rows, tile), lambda n, place_ref: (0, n))] * len(parts)
    aliases = {}
    if before is not None:
        aliases = {1 + len(operands): 0}
        operands.append(before)
        specs.append(pl.BlockSpec(memory_space=pl.ANY))
    if kind == "finish":
        out_shape = [pltpu.HBM((rows, slice_width), bf16)]
        out_specs = [pl.BlockSpec((rows, tile), lambda n, place_ref: (0, offset + n))]
    else:
        out_shape = [jax.ShapeDtypeStruct((count, rows, part), bf16)]
        out_specs = [
            pl.BlockSpec((1, rows, tile), lambda n, place_ref: (n // tiles, 0, n % tiles))
        ]
    if inverse is not None:
        out_shape.append(jax.ShapeDtypeStruct((rows, 1), f32))
        out_specs.append(fixed(rows, 1))
    return pl.pallas_call(
        functools.partial(out_kernel, kind, inverse is not None, len(parts), before is not None),
        out_shape=out_shape,
        grid_spec=pltpu.PrefetchScalarGridSpec(
            num_scalar_prefetch=1, grid=(count * tiles,), in_specs=specs, out_specs=out_specs
        ),
        input_output_aliases=aliases,
        compiler_params=params(),
        cost_estimate=pl.CostEstimate(
            flops=2 * rows * w_out.shape[0] * count * part,
            bytes_accessed=2 * w_out.shape[0] * count * part + 2 * rows * count * part,
            transcendentals=0,
        ),
        name="out_" + kind,
    )(place, *operands)


def collect_kernel(slices, ids_ref, *refs):
    chunk_refs, out_ref = refs[:-1], refs[-1]
    count, part = chunk_refs[0].shape
    rows = ids_ref.shape[1]
    depth = part * len(chunk_refs)
    step = min(512, part)
    ids, slot = route(ids_ref[...])
    at = ids[:, :1] * (slices * CAP) + slot
    lane = iota((rows, count), 1).astype(f32)
    for s in range(slices):
        pick = mask(at + s * CAP == lane)
        for k, rows_ref in enumerate(chunk_refs):
            for c in range(0, part, step):
                start = s * depth + k * part + c
                out_ref[:, start : start + step] = jnp.dot(
                    pick, rows_ref[:, c : c + step], preferred_element_type=f32
                ).astype(bf16)


def collect(ids_row, chunks, slices):
    width = sum(c.shape[1] for c in chunks) * slices
    return pl.pallas_call(
        functools.partial(collect_kernel, slices),
        out_shape=jax.ShapeDtypeStruct((ids_row.shape[1], width), bf16),
        compiler_params=params(),
        name="collect",
    )(ids_row, *chunks)


def turn(a, n, slices, r):
    return lax.ppermute(
        a, "expert", [(d, d // slices * slices + (d + r) % slices) for d in range(n)]
    )


def swap(a, groups=None):
    return lax.all_to_all(
        a, "expert", split_axis=0, concat_axis=0, axis_index_groups=groups, tiled=True
    )


def across(a, q, n, slices):
    pairs = [(d, (d // slices ^ q) * slices + d % slices) for d in range(n)]
    return lax.ppermute(a, "expert", pairs)


def exchange(arrays, n, slices):
    out = list(arrays)
    for q in reversed(range(1, EXPERTS)):
        out[q] = across(arrays[q], q, n, slices)
    return out


def shards(
    tokens, w_in, w_out, w_bcd, dt_bias, decay_rate, skip_gain, norm_gain, expert_ids, decode_heads
):
    n = lax.axis_size("expert")
    slices = n // EXPERTS
    in_dev = w_in.shape[2]
    units = in_dev // EXPERTS
    width = min(HEADDIM, units)
    heads = units // width
    me = lax.axis_index("expert")
    chip = (me // slices).astype(jnp.int32)
    place = jnp.stack([(me % slices).astype(jnp.int32), chip])
    start = place[0] * in_dev + chip * units
    same_slice = [[j * slices + k for j in range(EXPERTS)] for k in range(slices)]
    ids_row = expert_ids.reshape(1, -1)
    w_in, w_out = w_in[0], w_out[0]

    pack, outgoing = dispatch(decode_heads, ids_row, tokens, w_bcd.T, slices)
    landed = swap(outgoing)
    pack = lax.all_gather(pack, "expert", axis=0, tiled=True)
    own_heads = start // HEADDIM + jnp.arange(heads, dtype=jnp.int32)

    pieces = [landed] + [turn(landed, n, slices, r) for r in range(1, slices)]
    inner = [None] * EXPERTS
    for order in ((7, 6), (5, 4, 3), (2, 1), (0,)):
        if order == (0,):
            weights = prepare(place, own_heads, dt_bias, decay_rate, skip_gain, pack)
            pieces, weights = lax.optimization_barrier((pieces, weights))
        for q, a in zip(order, in_projection(place, pieces, w_in, units, order)):
            inner[q] = a
    x = exchange(inner, n, slices)

    gain = lax.dynamic_slice(norm_gain, (start,), (units,)).reshape(1, units)
    z = swap(scan(place, x, weights, gain, heads), same_slice)

    inverse = 1.0 / lax.dynamic_slice(norm_gain, (place[0] * in_dev,), (in_dev,))
    inverse = inverse.reshape(1, in_dev)
    project = functools.partial(out_projection, place=place, z=z, w_out=w_out)
    sent = []
    for k in range(CHUNKS):
        got = project("send", k, inverse=inverse if k == 0 else None)
        if k == 0:
            squares = [got[1]] + [turn(got[1], n, slices, r) for r in range(1, slices)]
        sent.append([turn(got[0][r - 1], n, slices, r) for r in range(1, slices)])
    done = None
    for k in range(CHUNKS):
        [done] = project("finish", k, squares=squares, parts=sent[k], before=done)
    mixed = collect(ids_row, [swap(done)], slices)

    def picked(head):
        first = head * HEADDIM % in_dev
        parts = [
            lax.dynamic_slice(
                z, ((first + i) // units, z.shape[1] - NS, (first + i) % units), (1, NS, width)
            )
            for i in range(0, HEADDIM, width)
        ]
        return jnp.concatenate(parts, axis=0) if len(parts) > 1 else parts[0]

    want = decode_heads[0]
    chosen = picked(want)
    for r in range(1, slices):
        other = chip * slices + (place[0] + r) % slices
        asked = lax.dynamic_slice(
            pack, (other * tokens.shape[0], 2 * NS + 2 * HEADS + 2), (1, 1)
        )[0, 0].astype(jnp.int32)
        got = turn(picked(asked), n, slices, r)
        lies = want * HEADDIM // in_dev
        chosen = jnp.where((place[0] - lies + slices) % slices == r, got, chosen)
    chosen = chosen.transpose(0, 2, 1).astype(f32)
    return (mixed, chosen.reshape(1, HEADDIM * NS))


def solution(mesh):
    in_specs = (
        P(("groups", "expert"), None),
        P("expert", None, None),
        P("expert", None, None),
        P(),
        P(),
        P(),
        P(),
        P(),
        P(("groups", "expert"), None),
        P("expert"),
    )
    out_specs = (P(("groups", "expert"), None), P(("groups", "expert"), None))
    return jax.shard_map(shards, mesh=mesh, in_specs=in_specs, out_specs=out_specs, check_vma=False)
```
